32 devices in a mesh: dom: 8 (over y, x, core), plane: 4 (over z).
Axes of the slice: x: 2, y: 2, z: 4, core: 2. Of those that a mesh axis runs over, the one named last changes fastest.
Arguments:
- adjoint: float32 [3, 64, 9, 9, 256], P(None, 'plane', None, None, 'dom'), may hold values from -6 to 6
- metric: float32 [4, 256], P(None, 'dom'), may hold values from 0.5 to 2
- base_flow: float32 [2, 12, 1327104], P(None, None, ('dom', 'plane')), may hold values from -6 to 6
- edge_list: int32 [8, 5, 24], P('dom'), may hold values from -1 to 127, as said below
- flips: int32 [8, 5, 24], P('dom'), may hold values from 0 to 1, as said below
Outputs:
- adjoint_next: float32 [3, 64, 9, 9, 256], P(None, 'plane', None, None, 'dom')
The draws below stay inside these ranges and needn't reach their ends.
Inputs may be any that keep to these rules, and one draw needn't show every extreme that they name: `edge_list`: entries are -1 or a local edge id j * 32 + l; no edge appears twice in one partition; filled slots come first in each block; a slot is filled exactly where its pair (as the steps define it) is filled, so block 2 has an even count; some block of some partition has all 24 slots filled, and every partition has an empty slot. `flips`: paired slots carry the same flag.
All inputs are finite; a program needn't handle non-finite values.
Results may differ from the reference program's by a relative error of at most 0.0003.
Values sent between devices are 32-bit elements; how exact they have to be, the bound alone decides.
No kernel may reach another device: no remote copies, remote signals or barrier semaphores. Data moves between devices by JAX's collectives and lax.ppermute only.
A program may use at most 128 MiB of HBM per device.

```python
import jax
import jax.numpy as jnp
from jax import lax

NP = 9
MODES = 64
E_DEV = 32
CAP = 24
REACH = 2
STEPS = 2
PARTITIONS = 8
ELEMS = 256
PTS_ALL = 20736
N_PLANE = 4


def pair_tables(key):
    blocks = 2 * REACH + 1
    raw_count = jax.random.randint(jax.random.fold_in(key, 1), (PARTITIONS, blocks), 1, CAP + 1)
    busy_rank = jax.random.randint(jax.random.fold_in(key, 3), (), 0, PARTITIONS)
    raw_count = raw_count.at[busy_rank, REACH + 1].set(CAP)
    self_count = 2 * jax.random.randint(jax.random.fold_in(key, 2), (PARTITIONS,), 0, CAP // 2)
    part_ids = jnp.arange(PARTITIONS, dtype=jnp.int32)[:, None]
    block_ids = jnp.arange(blocks, dtype=jnp.int32)[None, :]
    offset = block_ids - REACH
    canon_part = jnp.broadcast_to(jnp.where(offset > 0, part_ids, (part_ids + offset) % PARTITIONS), (PARTITIONS, blocks))
    canon_block = jnp.broadcast_to(jnp.where(offset > 0, block_ids, 2 * REACH - block_ids), (PARTITIONS, blocks))
    slot_count = raw_count[canon_part, canon_block]
    slot_count = jnp.where(offset == 0, self_count[:, None], slot_count)
    part_keys = jax.random.split(jax.random.fold_in(key, 4), PARTITIONS)
    orders = jax.vmap(lambda one_key: jax.random.permutation(one_key, 4 * E_DEV))(part_keys).astype(jnp.int32)
    chosen = jax.random.randint(jax.random.fold_in(key, 5), (PARTITIONS,), 0, blocks - 1)
    chosen = chosen + (chosen >= REACH).astype(jnp.int32)
    target = chosen * CAP
    found_at = jnp.argmax(orders == 4 * E_DEV - 1, axis=1)
    rows = jnp.arange(PARTITIONS, dtype=jnp.int32)
    moved = orders[rows, target]
    orders = orders.at[rows, found_at].set(moved)
    orders = orders.at[rows, target].set(4 * E_DEV - 1)
    edge_ids = orders[:, :blocks * CAP].reshape(PARTITIONS, blocks, CAP)
    slot_ids = jnp.arange(CAP, dtype=jnp.int32)[None, None, :]
    edge_table = jnp.where(slot_ids < slot_count[:, :, None], edge_ids, -1).astype(jnp.int32)
    raw_flip = jax.random.randint(jax.random.fold_in(key, 6), (PARTITIONS, blocks, CAP), 0, 2)
    canon_slot = jnp.broadcast_to(jnp.where(offset[:, :, None] == 0, slot_ids - slot_ids % 2, slot_ids), (PARTITIONS, blocks, CAP))
    flip_table = raw_flip[jnp.broadcast_to(canon_part[:, :, None], (PARTITIONS, blocks, CAP)), jnp.broadcast_to(canon_block[:, :, None], (PARTITIONS, blocks, CAP)), canon_slot]
    return (edge_table, flip_table.astype(jnp.int32))


def draw_edge_list(key, part):
    return pair_tables(key)[0]


def draw_flips(key, part):
    return pair_tables(key)[1]


def steps_of(stream_key, dims, cuts, low, high):
    loudness, own = 1.0, jax.random.fold_in(stream_key, 6)
    for axis_at, blocks in cuts:
        heights = jnp.exp(jax.random.uniform(jax.random.fold_in(own, axis_at), (blocks,), jnp.float32, low / len(cuts), high / len(cuts)))
        loudness = loudness * jnp.repeat(heights, dims[axis_at] // blocks).reshape([-1 if axis == axis_at else 1 for axis in range(len(dims))])
    return loudness


def centred(stream_key, dims, spread, reach, pieces=(), kind=jnp.bfloat16):
    entries = jax.random.normal(stream_key, dims, jnp.float32) * spread
    if len(pieces) > 0:
        entries = steps_of(stream_key, dims, pieces, -0.22, 0.18) * entries
    return jnp.clip(entries, min=-reach, max=reach).astype(kind)


def setup_inputs(seed: int = 0) -> dict:
    key_list = jax.random.split(jax.random.key(seed), 6)
    return {
        "adjoint": centred(key_list[0], (3, MODES, NP, NP, ELEMS), 1.0, 6.0, ((1, 4), (4, 8)), jnp.float32),
        "metric": jnp.clip(0.5 + 1.5 * jax.random.uniform(key_list[1], (4, ELEMS), jnp.float32) ** steps_of(key_list[1], (4, ELEMS), ((1, 8),), -0.2, 0.2), 0.5, 2.0),
        "base_flow": centred(key_list[2], (STEPS, 12, PTS_ALL * MODES), 1.0, 6.0, ((2, 32),), jnp.float32),
        "edge_list": draw_edge_list(jax.random.fold_in(key_list[5], 71), 0),
        "flips": draw_flips(jax.random.fold_in(key_list[5], 71), 0),
    }


step_size = 0.01
viscosity = 0.02


def cheb_table(node_count):
    order = node_count - 1
    node_ids = jnp.arange(node_count, dtype=jnp.int32)
    node_coords = -jnp.cos(jnp.pi * node_ids.astype(jnp.float32) / order)
    weight = jnp.where((node_ids == 0) | (node_ids == order), 2.0, 1.0).astype(jnp.float32)
    parity = jnp.where((node_ids[:, None] + node_ids[None, :]) % 2 == 0, 1.0, -1.0).astype(jnp.float32)
    on_diag = node_ids[:, None] == node_ids[None, :]
    differ = jnp.where(on_diag, 1.0, node_coords[:, None] - node_coords[None, :])
    off_diag = jnp.where(on_diag, 0.0, weight[:, None] / weight[None, :] * parity / differ)
    return off_diag - jnp.diag(jnp.sum(off_diag, axis=1))


def span_tables(modes):
    mode_ids = jnp.arange(modes, dtype=jnp.int32)
    wavenumber = (mode_ids + 1) // 2
    is_cosine = (mode_ids % 2 == 1) | (mode_ids == 0)
    span_ids = jnp.arange(modes, dtype=jnp.int32)
    phase_num = (span_ids[:, None] * wavenumber[None, :]) % modes
    angles = 2.0 * jnp.pi * phase_num.astype(jnp.float32) / modes
    cosines = jnp.cos(angles)
    sines = jnp.sin(angles)
    wave_f = wavenumber.astype(jnp.float32)
    span_basis = jnp.where(is_cosine[None, :], cosines, sines)
    span_slope = jnp.where(is_cosine[None, :], -wave_f[None, :] * sines, wave_f[None, :] * cosines)
    scaling = jnp.where((mode_ids == 0) | (mode_ids == modes - 1), 1.0 / modes, 2.0 / modes).astype(jnp.float32)
    forward = span_basis.T * scaling[:, None]
    return span_basis, span_slope, forward, wave_f * wave_f


def directional(field_data, metric, deriv_table, xi_row, eta_row):
    along_xi = jnp.einsum('ai,cmije->cmaje', deriv_table, field_data, precision=lax.Precision.HIGHEST)
    along_eta = jnp.einsum('bj,cmije->cmibe', deriv_table, field_data, precision=lax.Precision.HIGHEST)
    return metric[xi_row] * along_xi + metric[eta_row] * along_eta


def advect(coeffs, base_now, span_basis, span_slope, forward):
    values = jnp.einsum('nm,fmq->fnq', span_basis, coeffs, precision=lax.Precision.HIGHEST)
    along_z = jnp.einsum('nm,cmq->cnq', span_slope, coeffs[0:3], precision=lax.Precision.HIGHEST)
    products = []
    for comp in range(3):
        term = base_now[0] * values[3 + comp] + base_now[1] * values[6 + comp] + base_now[2] * along_z[comp]
        term = term - (values[0] * base_now[3 + comp] + values[1] * base_now[6 + comp] + values[2] * base_now[9 + comp])
        products.append(term)
    return jnp.einsum('mn,cnq->cmq', forward, jnp.stack(products), precision=lax.Precision.HIGHEST)


def accumulate(field_data, edge_sums, counts):
    node_count = field_data.shape[2]
    last = node_count - 1
    total = field_data
    total = total.at[:, :, :, 0, :].add(edge_sums[:, :, :, 0, :])
    total = total.at[:, :, last, :, :].add(edge_sums[:, :, :, 1, :])
    total = total.at[:, :, :, last, :].add(edge_sums[:, :, :, 2, :])
    total = total.at[:, :, 0, :, :].add(edge_sums[:, :, :, 3, :])
    weight = jnp.ones((node_count, node_count, field_data.shape[4]), jnp.float32)
    weight = weight.at[:, 0, :].add(counts[0][None, :])
    weight = weight.at[last, :, :].add(counts[1][None, :])
    weight = weight.at[:, last, :].add(counts[2][None, :])
    weight = weight.at[0, :, :].add(counts[3][None, :])
    return total / weight


def edge_traces(field_data):
    last = field_data.shape[2] - 1
    return jnp.stack([field_data[:, :, :, 0, :], field_data[:, :, last, :, :],
                      field_data[:, :, :, last, :], field_data[:, :, 0, :, :]], axis=3)


def assemble_all(field_data, edge_list, flips):
    components, modes, node_count, _, total_elems = field_data.shape
    partitions, blocks, capacity = edge_list.shape
    half_span = (blocks - 1) // 2
    elements = total_elems // partitions
    row_count = components * modes * node_count
    traces = edge_traces(field_data).reshape(components, modes, node_count, 4, partitions, elements)
    edge_table = jnp.transpose(traces, (4, 0, 1, 2, 3, 5)).reshape(partitions, row_count, 4 * elements)
    part_ids = jnp.arange(partitions, dtype=jnp.int32)[:, None, None]
    block_ids = jnp.arange(blocks, dtype=jnp.int32)[None, :, None]
    slot_ids = jnp.arange(capacity, dtype=jnp.int32)[None, None, :]
    shape3 = (partitions, blocks, capacity)
    partner = jnp.broadcast_to((part_ids + block_ids - half_span) % partitions, shape3)
    partner_block = jnp.broadcast_to(2 * half_span - block_ids, shape3)
    partner_slot = jnp.broadcast_to(jnp.where(block_ids == half_span, slot_ids + 1 - 2 * (slot_ids % 2), slot_ids), shape3)
    partner_edge = edge_list[partner, partner_block, partner_slot]
    gathered = edge_table[partner, :, jnp.maximum(partner_edge, 0)]
    gathered = gathered.reshape(partitions, blocks, capacity, components * modes, node_count)
    occupied = (edge_list >= 0).astype(jnp.float32)
    gathered = jnp.where((flips == 1)[..., None, None], gathered[..., ::-1], gathered) * occupied[..., None, None]
    gathered = gathered.reshape(partitions, blocks * capacity, row_count)
    slot_edges = edge_list.reshape(partitions, blocks * capacity)
    onehot = (slot_edges[:, :, None] == jnp.arange(4 * elements, dtype=jnp.int32)[None, None, :]).astype(jnp.float32)
    edge_sums = jnp.einsum('psr,pse->pre', gathered, onehot, precision=lax.Precision.HIGHEST)
    edge_sums = edge_sums.reshape(partitions, components, modes, node_count, 4, elements)
    edge_sums = jnp.transpose(edge_sums, (1, 2, 3, 4, 0, 5)).reshape(components, modes, node_count, 4, total_elems)
    counts = jnp.sum(onehot, axis=1).reshape(partitions, 4, elements)
    counts = jnp.transpose(counts, (1, 0, 2)).reshape(4, total_elems)
    return accumulate(field_data, edge_sums, counts)


def reference(adjoint, metric, base_flow, edge_list, flips):
    components, modes, node_count, _, total_elems = adjoint.shape
    partitions = edge_list.shape[0]
    elements = total_elems // partitions
    points = node_count * node_count * elements
    local_points = points // N_PLANE
    deriv_table = cheb_table(node_count)
    span_basis, span_slope, forward, wave_sq = span_tables(modes)
    adjoint_state = adjoint
    zero_index = jnp.zeros((), jnp.int32)
    for step_index in range(STEPS):
        grad_x = directional(adjoint_state, metric, deriv_table, 0, 2)
        grad_y = directional(adjoint_state, metric, deriv_table, 1, 3)
        stacked = jnp.concatenate([adjoint_state, grad_x, grad_y], axis=0)

        def physical(part_index, stacked=stacked, step_index=step_index):
            part_index = part_index.astype(jnp.int32)
            elem_start = (part_index * elements).astype(jnp.int32)
            coeffs = lax.dynamic_slice_in_dim(stacked, elem_start, elements, 4).reshape(9, modes, points)
            starts = (jnp.full((), step_index, jnp.int32), zero_index, (part_index * (modes * points)).astype(jnp.int32))
            base_flat = lax.dynamic_slice(base_flow, starts, (1, 12, modes * points))[0]
            base_now = jnp.transpose(base_flat.reshape(12, N_PLANE, modes, local_points), (0, 2, 1, 3)).reshape(12, modes, points)
            return advect(coeffs, base_now, span_basis, span_slope, forward).reshape(3, modes, node_count, node_count, elements)

        rates = lax.map(physical, jnp.arange(partitions, dtype=jnp.int32))
        returned = jnp.transpose(rates, (1, 2, 3, 4, 0, 5)).reshape(adjoint_state.shape)
        laplacian = directional(grad_x, metric, deriv_table, 0, 2) + directional(grad_y, metric, deriv_table, 1, 3)
        updated = adjoint_state + step_size * (returned + viscosity * (laplacian - wave_sq[None, :, None, None, None] * adjoint_state))
        adjoint_state = assemble_all(updated, edge_list, flips)
    return adjoint_state
```

```python
import functools

import jax
import jax.numpy as jnp
import numpy as np
from jax import lax
from jax.experimental import pallas as pl
from jax.experimental.pallas import tpu as pltpu
from jax.sharding import PartitionSpec as P

MODES = 64
STEPS = 2


step_size = 0.01
viscosity = 0.02


def passed_along(shard, axis, by):
    size = lax.axis_size(axis)
    return lax.ppermute(shard, axis, [(i, (i + by) % size) for i in range(size)])


def cheb_table(node_count):
    order = node_count - 1
    node_ids = jnp.arange(node_count, dtype=jnp.int32)
    node_coords = -jnp.cos(jnp.pi * node_ids.astype(jnp.float32) / order)
    weight = jnp.where((node_ids == 0) | (node_ids == order), 2.0, 1.0).astype(jnp.float32)
    parity = jnp.where((node_ids[:, None] + node_ids[None, :]) % 2 == 0, 1.0, -1.0).astype(
        jnp.float32
    )
    on_diag = node_ids[:, None] == node_ids[None, :]
    differ = jnp.where(on_diag, 1.0, node_coords[:, None] - node_coords[None, :])
    off_diag = jnp.where(on_diag, 0.0, weight[:, None] / weight[None, :] * parity / differ)
    return off_diag - jnp.diag(jnp.sum(off_diag, axis=1))


def span_tables(modes):
    mode_ids = jnp.arange(modes, dtype=jnp.int32)
    wavenumber = (mode_ids + 1) // 2
    is_cosine = (mode_ids % 2 == 1) | (mode_ids == 0)
    span_ids = jnp.arange(modes, dtype=jnp.int32)
    phase_num = span_ids[:, None] * wavenumber[None, :] % modes
    angles = 2.0 * jnp.pi * phase_num.astype(jnp.float32) / modes
    cosines = jnp.cos(angles)
    sines = jnp.sin(angles)
    wave_f = wavenumber.astype(jnp.float32)
    span_basis = jnp.where(is_cosine[None, :], cosines, sines)
    span_slope = jnp.where(is_cosine[None, :], -wave_f[None, :] * sines, wave_f[None, :] * cosines)
    scaling = jnp.where((mode_ids == 0) | (mode_ids == modes - 1), 1.0 / modes, 2.0 / modes).astype(
        jnp.float32
    )
    forward = span_basis.T * scaling[:, None]
    return (span_basis, span_slope, forward, wave_f * wave_f)


def directional(field_data, metric, deriv_table, xi_row, eta_row):
    along_xi = jnp.einsum(
        "ai,cmije->cmaje", deriv_table, field_data, precision=lax.Precision.HIGHEST
    )
    along_eta = jnp.einsum(
        "bj,cmije->cmibe", deriv_table, field_data, precision=lax.Precision.HIGHEST
    )
    return metric[xi_row] * along_xi + metric[eta_row] * along_eta


def advect(coeffs, base_now, span_basis, span_slope, forward):
    values = jnp.einsum("nm,fmq->fnq", span_basis, coeffs, precision=lax.Precision.HIGHEST)
    along_z = jnp.einsum("nm,cmq->cnq", span_slope, coeffs[0:3], precision=lax.Precision.HIGHEST)
    products = []
    for comp in range(3):
        term = (
            base_now[0] * values[3 + comp]
            + base_now[1] * values[6 + comp]
            + base_now[2] * along_z[comp]
        )
        term = term - (
            values[0] * base_now[3 + comp]
            + values[1] * base_now[6 + comp]
            + values[2] * base_now[9 + comp]
        )
        products.append(term)
    return jnp.einsum("mn,cnq->cmq", forward, jnp.stack(products), precision=lax.Precision.HIGHEST)


def accumulate(field_data, edge_sums, counts):
    node_count = field_data.shape[2]
    last = node_count - 1
    total = field_data
    total = total.at[:, :, :, 0, :].add(edge_sums[:, :, :, 0, :])
    total = total.at[:, :, last, :, :].add(edge_sums[:, :, :, 1, :])
    total = total.at[:, :, :, last, :].add(edge_sums[:, :, :, 2, :])
    total = total.at[:, :, 0, :, :].add(edge_sums[:, :, :, 3, :])
    weight = jnp.ones((node_count, node_count, field_data.shape[4]), jnp.float32)
    weight = weight.at[:, 0, :].add(counts[0][None, :])
    weight = weight.at[last, :, :].add(counts[1][None, :])
    weight = weight.at[:, last, :].add(counts[2][None, :])
    weight = weight.at[0, :, :].add(counts[3][None, :])
    return total / weight


def assemble(field_data, edge_slots, flip_flags):
    components, local_modes, node_count, _, elements = field_data.shape
    last = node_count - 1
    row_count = components * local_modes * node_count
    traces = jnp.stack(
        [
            field_data[:, :, :, 0, :],
            field_data[:, :, last, :, :],
            field_data[:, :, :, last, :],
            field_data[:, :, 0, :, :],
        ],
        axis=3,
    )
    edge_table = traces.reshape(row_count, 4 * elements)
    blocks, capacity = edge_slots.shape
    half_span = (blocks - 1) // 2
    slot_edges = edge_slots.reshape(-1)
    occupied = (slot_edges >= 0).astype(jnp.float32)
    outgoing = jnp.take(edge_table, jnp.maximum(slot_edges, 0), axis=1) * occupied[None, :]

    def block_of(block_id):
        return outgoing[:, block_id * capacity : (block_id + 1) * capacity]

    own_pairs = (
        block_of(half_span)
        .reshape(row_count, capacity // 2, 2)[:, :, ::-1]
        .reshape(row_count, capacity)
    )
    received = {half_span: own_pairs}
    for block_id in range(blocks):
        if block_id != half_span:
            received[block_id] = passed_along(
                block_of(blocks - 1 - block_id), "dom", half_span - block_id
            )
    partners = jnp.concatenate([received[block_id] for block_id in range(blocks)], axis=1)
    shaped = partners.reshape(components * local_modes, node_count, blocks * capacity)
    shaped = (
        jnp.where(flip_flags.reshape(-1)[None, None, :] == 1, shaped[:, ::-1, :], shaped)
        * occupied[None, None, :]
    )
    onehot = (slot_edges[:, None] == jnp.arange(4 * elements, dtype=jnp.int32)[None, :]).astype(
        jnp.float32
    )
    edge_sums = jnp.dot(
        shaped.reshape(row_count, blocks * capacity), onehot, precision=lax.Precision.HIGHEST
    )
    edge_sums = edge_sums.reshape(components, local_modes, node_count, 4, elements)
    counts = jnp.sum(onehot, axis=0).reshape(4, elements)
    return accumulate(field_data, edge_sums, counts)


def advance(
    adjoint_state,
    metric,
    base_now,
    edge_slots,
    flip_flags,
    deriv_table,
    span_basis,
    span_slope,
    forward,
    wave_local,
):
    components, local_modes, node_count, _, elements = adjoint_state.shape
    points = node_count * node_count * elements
    grad_x = directional(adjoint_state, metric, deriv_table, 0, 2)
    grad_y = directional(adjoint_state, metric, deriv_table, 1, 3)
    stacked = jnp.concatenate([adjoint_state, grad_x, grad_y], axis=0).reshape(
        9, local_modes, points
    )
    gathered = lax.all_to_all(stacked, "plane", split_axis=2, concat_axis=1, tiled=True)
    advective = advect(gathered, base_now, span_basis, span_slope, forward)
    returned = lax.all_to_all(advective, "plane", split_axis=1, concat_axis=2, tiled=True).reshape(
        adjoint_state.shape
    )
    laplacian = directional(grad_x, metric, deriv_table, 0, 2) + directional(
        grad_y, metric, deriv_table, 1, 3
    )
    updated = adjoint_state + step_size * (
        returned + viscosity * (laplacian - wave_local[None, :, None, None, None] * adjoint_state)
    )
    return assemble(updated, edge_slots, flip_flags)


NODES = 9
LANES = 128
SLAB_TILES = 3
STATE_TILES = 7
SEND_TILES = 12
CHUNK_TILES = 6
BODY_TILES = 5
BACK_TILES = 31
GROUP = 8
PARTNERS = (0, 2, 3, 1)
STEP_VISC = step_size * viscosity


def cheb_numbers():
    order = NODES - 1
    coords = -np.cos(np.pi * np.arange(NODES) / order)
    weight = np.ones(NODES)
    weight[0] = weight[-1] = 2.0
    table = np.zeros((NODES, NODES))
    for a in range(NODES):
        for i in range(NODES):
            if a != i:
                table[a, i] = weight[a] / weight[i] * (-1.0) ** (a + i) / (coords[a] - coords[i])
    return table - np.diag(table.sum(axis=1))


DERIV = cheb_numbers()


def span_numbers():
    modes = np.arange(MODES)
    wave = (modes + 1) // 2
    is_cosine = (modes % 2 == 1) | (modes == 0)
    angles = 2.0 * np.pi * (np.arange(MODES)[:, None] * wave[None, :] % MODES) / MODES
    cosines, sines = np.cos(angles), np.sin(angles)
    basis = np.where(is_cosine, cosines, sines)
    slope = np.where(is_cosine, -wave * sines, wave * cosines)
    scaling = np.where((modes == 0) | (modes == MODES - 1), 1.0 / MODES, 2.0 / MODES)
    return basis, slope, basis.T * scaling[:, None]


def in_two(table):
    table = table.astype(np.float32)
    high = table.astype(jnp.bfloat16)
    low = (table - high.astype(np.float32)).astype(jnp.bfloat16)
    return high, low


def span_weights(planes):
    basis, slope, forward = span_numbers()
    local = MODES // planes
    to_span, to_modes = [], []
    for me in range(planes):
        came = np.concatenate([(me ^ step) * local + np.arange(local) for step in PARTNERS])
        high, low = in_two(np.concatenate([basis, slope])[:, came])
        to_span.append(np.concatenate([high, high, low], axis=1))
        high, low = in_two(forward[came])
        to_modes.append(np.concatenate([high, high, low], axis=1))
    return np.stack(to_span), np.stack(to_modes)


def eta_bands(first_lane, lanes, count):
    bands = np.zeros((24, lanes), np.float32)
    for lane in range(count):
        j = (first_lane + lane) % 288 // 32
        for d in range(-8, 9):
            if 0 <= j + d < NODES:
                bands[d + 8, lane] = DERIV[j, j + d]
    return bands


def tile_plan(segments, tiles):
    plan = [[] for _ in range(tiles)]
    for source, src, dst, length in segments:
        done = 0
        while done < length:
            s, d = src + done, dst + done
            size = min(length - done, LANES - s % LANES, LANES - d % LANES)
            plan[d // LANES].append((source, s // LANES, (d - s) % LANES, d % LANES, size))
            done += size
    return plan


def send_segments(chunk, points):
    ring, slab = STATE_TILES * LANES, NODES * 32
    turned = (points - 2 * slab) * chunk
    segments = []
    for r in range(3):
        start = (r * slab - turned) % ring
        first = min(slab, ring - start)
        segments.append((("state", 2 * chunk + r), 0, start, first))
        if first < slab:
            segments.append((("state", 2 * chunk + r), first, 0, slab - first))
    gap = (3 * slab - turned) % ring
    body = (points // LANES) * LANES
    lane = points * chunk
    for lane in range(points * chunk, points * (chunk + 1), 8):
        at = lane - points * chunk
        target = ring + at if at < body else gap + at - body
        source = ("xi", lane // slab)
        if segments[-1][0] == source and segments[-1][1] + segments[-1][3] == lane % slab and (
            segments[-1][2] + segments[-1][3] == target
        ):
            segments[-1] = (source, segments[-1][1], segments[-1][2], segments[-1][3] + 8)
        else:
            segments.append((source, lane % slab, target, 8))
    return segments, gap


def return_segments(points):
    slab = NODES * 32
    body = points // LANES * LANES
    plans = []
    for i in range(NODES):
        segments = []
        for chunk in range(4):
            for name, start, stop in (("body", 0, body), ("tail", body, points)):
                low = max(i * slab, chunk * points + start)
                high = min((i + 1) * slab, chunk * points + stop)
                if low < high:
                    segments.append(((name, chunk), low - chunk * points - start, low - i * slab, high - low))
        plans.append(tile_plan(segments, SLAB_TILES))
    return plans


def lane_ids(rows):
    return lax.broadcasted_iota(jnp.int32, (rows, LANES), 1)


def turn(value, shift):
    return value if shift % LANES == 0 else pltpu.roll(value, shift % LANES, 1)


def pieced(pieces, load, lanes):
    total = None
    for source, tile, shift, low, size in pieces:
        value = turn(load(source, tile), shift)
        if total is None:
            total = value
        else:
            total = jnp.where((lanes >= low) & (lanes < low + size), value, total)
    return total


def tile_at(ref, lead, rows, tile):
    return ref[(*lead, rows, pl.ds(tile * LANES, LANES))]


def along_i(tiles):
    return [
        sum(tiles[i] * float(DERIV[a, i]) for i in range(1, NODES)) + tiles[0] * float(DERIV[a, 0])
        for a in range(NODES)
    ]


def turned_tiles(tiles, lanes):
    out = [tiles]
    for s in range(1, 4):
        spun = [pltpu.roll(t, LANES - 32 * s, 1) for t in tiles]
        out.append(
            [
                jnp.where(lanes < LANES - 32 * s, spun[t], spun[(t + 1) % len(tiles)])
                for t in range(len(tiles))
            ]
        )
    return out


def along_j(turned, ring, tile, band, used):
    total = None
    for d in used:
        term = turned[d % 4][(tile + d // 4) % ring] * band(d)
        total = term if total is None else total + term
    return total


def make_sends(me, plans, rows_total, state, xi, staged, outs):
    rows_step = 8
    lanes = lane_ids(rows_step)

    def some_rows(g, _):
        rows = pl.ds(pl.multiple_of(g * rows_step, rows_step), rows_step)
        for t in range(SLAB_TILES):
            for a, value in enumerate(along_i([tile_at(state, (i,), rows, t) for i in range(NODES)])):
                xi[a, rows, pl.ds(t * LANES, LANES)] = value

        def load(source, tile):
            return tile_at(state if source[0] == "state" else xi, (source[1],), rows, tile)

        for chunk, plan in enumerate(plans):
            for t, pieces in enumerate(plan):
                staged[chunk, rows, pl.ds(t * LANES, LANES)] = pieced(pieces, load, lanes)
        return 0

    lax.fori_loop(0, rows_total // rows_step, some_rows, 0)
    for k, out in enumerate(outs):
        out[...] = staged[me ^ PARTNERS[k]]


def first_kernel(plans, adjoint, state, out0, out1, out2, out3, xi, staged, taken, sems):
    me = lax.axis_index("plane")
    comps, local = taken.shape[0], taken.shape[3]
    copies = [pltpu.make_async_copy(adjoint.at[:, i], taken.at[:, i], sems.at[i]) for i in range(NODES)]
    for copy in copies:
        copy.start()
    for i in range(NODES):
        copies[i].wait()
        for c in range(comps):
            rows = pl.ds(c * local, local)
            for t in range(SLAB_TILES):
                parts = [taken[c, i, j] for j in range(4 * t, min(4 * t + 4, NODES))]
                parts += [jnp.zeros_like(parts[0])] * (4 - len(parts))
                state[i, rows, pl.ds(t * LANES, LANES)] = jnp.concatenate(parts, axis=1)
    make_sends(me, plans, comps * local, state, xi, staged, (out0, out1, out2, out3))


def flow_kernel(points, flow, metric, out0, out1):
    me = lax.axis_index("plane")
    per_field = MODES * points // LANES
    lanes, subs = lane_ids(8), lax.broadcasted_iota(jnp.int32, (8, LANES), 0)
    shift = lax.rem(LANES - lax.rem(me * points, LANES), LANES)
    turned = pltpu.roll(metric[...], shift, 1)
    xi_x, xi_y, eta_x, eta_y = (turned[r : r + 1, :] for r in range(4))
    last = CHUNK_TILES - 1

    for s, out in enumerate((out0, out1)):
        for half in range(2):

            moved = (lanes + 64 * half + 8 * subs) & (LANES - 1)
            kept = lanes < LANES - 64 * half - 8 * subs

            def some_rows(h, _, s=s, half=half, out=out, moved=moved, kept=kept):
                rows = pl.ds(pl.multiple_of(16 * h + 8 * half, 8), 8)

                def field(f):
                    spun = []
                    for k in range(CHUNK_TILES):
                        start = 2 * (f * per_field + 40 * half + k) + s + h * (16 * points // LANES * 2)
                        block = flow[pl.ds(start, 8, stride=10), :]
                        spun.append(pick(block, moved))
                    tiles = [jnp.where(kept, spun[k], spun[k + 1]) for k in range(last)]
                    return tiles + [spun[last]]

                def put(f, t, value):
                    out[f, rows, pl.ds(t * LANES, LANES)] = value

                first, second = field(0), field(1)
                for t in range(CHUNK_TILES):
                    put(0, t, first[t] * xi_x + second[t] * xi_y)
                    put(1, t, first[t] * eta_x + second[t] * eta_y)
                for f in range(2, 12):
                    for t, value in enumerate(field(f)):
                        put(f, t, value)
                return 0

            lax.fori_loop(0, MODES // 16, some_rows, 0)


def tables_kernel(edges, flags, table):
    capacity, blocks = edges.shape
    lanes = lane_ids(capacity)
    slots = lax.broadcasted_iota(jnp.int32, (capacity, LANES), 0)
    here = slots == lax.rem(lanes, capacity)
    flag = jnp.zeros((1, LANES), jnp.int32)
    count = jnp.zeros((1, LANES), jnp.int32)
    table[...] = jnp.zeros(table.shape, jnp.int32)
    for o in range(blocks):
        column = jnp.broadcast_to(edges[:, o : o + 1], (capacity, LANES))
        held = column == lanes

        def summed(mask, value):
            return jnp.sum(jnp.where(mask, value, 0), axis=0, keepdims=True)

        table[o : o + 1, :] = summed(here, jnp.maximum(column, 0))
        table[5 + o : 6 + o, :] = summed(held, slots)
        present = summed(held, jnp.ones_like(slots))
        table[10 + o : 11 + o, :] = present
        flag += summed(held, jnp.broadcast_to(flags[:, o : o + 1], (capacity, LANES)))
        count += present
        if o == blocks // 2:
            partner = slots + 1 - 2 * lax.rem(slots, 2)
            slot_of = jnp.broadcast_to(summed(held, partner), (capacity, LANES))
            partner_edge = summed(slots == slot_of, jnp.maximum(column, 0))
            table[16:17, :] = jnp.where(present > 0, partner_edge, 0)
    table[15:16, :] = flag
    table[17:18, :] = count


def diffuse_kernel(state, metric, bands, local_sum, first, second):
    me = lax.axis_index("plane")
    rows_total = state.shape[1]
    lanes = lane_ids(8)
    local = rows_total // 3
    xi_x, xi_y, eta_x, eta_y = (metric[r : r + 1, :] for r in range(4))
    g_ii = xi_x * xi_x + xi_y * xi_y
    g_ij = xi_x * eta_x + xi_y * eta_y
    g_jj = eta_x * eta_x + eta_y * eta_y
    used = [[d for d in range(-8, 9) if any(0 <= j + d < NODES for j in range(4 * t, min(4 * t + 4, NODES)))]
            for t in range(SLAB_TILES)]

    def eta_of(tiles):
        turned = turned_tiles(tiles, lanes)
        return [
            along_j(turned, SLAB_TILES, t, lambda d, t=t: tile_at(bands, (), pl.ds(d + 8, 1), t), used[t])
            for t in range(SLAB_TILES)
        ]

    def some_rows(g, _):
        rows = pl.ds(pl.multiple_of(g * 8, 8), 8)
        first_mode = me * local + lax.rem(g * 8, local)
        wave = ((first_mode + lax.broadcasted_iota(jnp.int32, (8, LANES), 0) + 1) // 2).astype(jnp.float32)
        wave_sq = wave * wave
        for t in range(SLAB_TILES):
            for a, value in enumerate(along_i([tile_at(state, (i,), rows, t) for i in range(NODES)])):
                first[a, :, pl.ds(t * LANES, LANES)] = value
        for i in range(NODES):
            eta = eta_of([tile_at(state, (i,), rows, t) for t in range(SLAB_TILES)])
            mixed = []
            for t in range(SLAB_TILES):
                xi = first[i, :, pl.ds(t * LANES, LANES)]
                first[i, :, pl.ds(t * LANES, LANES)] = g_ii * xi + g_ij * eta[t]
                mixed.append(g_ij * xi + g_jj * eta[t])
            for t, value in enumerate(eta_of(mixed)):
                second[i, :, pl.ds(t * LANES, LANES)] = value
        for t in range(SLAB_TILES):
            tiles = [first[i, :, pl.ds(t * LANES, LANES)] for i in range(NODES)]
            for a, value in enumerate(along_i(tiles)):
                now = tile_at(state, (a,), rows, t)
                laplacian = value + second[a, :, pl.ds(t * LANES, LANES)]
                local_sum[a, rows, pl.ds(t * LANES, LANES)] = now + STEP_VISC * (laplacian - wave_sq * now)
        return 0

    lax.fori_loop(0, rows_total // 8, some_rows, 0)


def halves(value):
    high = value.astype(jnp.bfloat16)
    return high, (value - high.astype(jnp.float32)).astype(jnp.bfloat16)


def fields_kernel(gaps, source, bands, fields):
    me = lax.axis_index("plane")
    rows_total = source.shape[0]
    local = fields.shape[2]
    lanes = lane_ids(GROUP)
    gap = sum(jnp.where(me == b, g, 0) for b, g in enumerate(gaps))
    gap_tile, gap_lane = gap // LANES, lax.rem(gap, LANES)

    def some_rows(g, _):
        rows = pl.ds(pl.multiple_of(g * GROUP, GROUP), GROUP)
        c = g * GROUP // local
        target = pl.ds(pl.multiple_of(lax.rem(g * GROUP, local), GROUP), GROUP)

        def put(kind, t, value):
            fields[kind, c, target, pl.ds(t * LANES, LANES)] = value

        tiles = [tile_at(source, (), rows, t) for t in range(STATE_TILES)]
        turned = turned_tiles(tiles, lanes)
        for t in range(CHUNK_TILES):
            put(0, t, tiles[t])
            put(2, t, along_j(turned, STATE_TILES, t,
                              lambda d, t=t: bands[me, pl.ds(d + 8, 1), pl.ds(t * LANES, LANES)],
                              range(-8, 9)))
        for t in range(BODY_TILES):
            put(1, t, tile_at(source, (), rows, STATE_TILES + t))
        tail = source[rows, pl.ds(pl.multiple_of(gap_tile * LANES, LANES), LANES)]
        put(1, BODY_TILES, pltpu.roll(tail, lax.rem(LANES - gap_lane, LANES), 1))
        return 0

    lax.fori_loop(0, rows_total // GROUP, some_rows, 0)


def advect_kernel(fields0, fields1, fields2, fields3, flow, to_span, to_modes, *outs):
    me = lax.axis_index("plane")
    comps = fields0.shape[1]
    both = to_span[me]
    basis = both[:MODES]
    back = to_modes[me]
    width = 2 * LANES
    chunks = CHUNK_TILES * LANES // width
    lanes = lane_ids(GROUP)

    def dot(a, value):
        high, low = halves(value)
        stacked = jnp.concatenate([high, low, high], axis=0)
        return jnp.dot(a, stacked, preferred_element_type=jnp.float32)

    def results(part):
        def field(kind, c):
            return jnp.concatenate(
                [fields[kind, c, :, part] for fields in (fields0, fields1, fields2, fields3)], axis=0
            )

        values, sums = [], []
        for c in range(comps):
            out = dot(both, field(0, c))
            values.append(out[:MODES])
            along_x = flow[0, :, part] * dot(basis, field(1, c))
            along_y = flow[1, :, part] * dot(basis, field(2, c))
            sums.append(along_x + along_y + flow[2, :, part] * out[MODES:])
        for c in range(comps):
            taken = values[0] * flow[3 + c, :, part]
            taken += values[1] * flow[6 + c, :, part]
            taken += values[2] * flow[9 + c, :, part]
            yield c, dot(back, sums[c] - taken)

    def split(c, result):
        for k, out in enumerate(outs):
            for half in range(MODES // len(outs) // GROUP):
                first = k * (MODES // len(outs)) + half * GROUP
                yield k, out, c * (MODES // len(outs) // GROUP) + half, result[first : first + GROUP]

    def some_lanes(p, _):
        first = pl.multiple_of(p * width, width)
        for c, result in results(pl.ds(first, width)):
            for _, out, g, piece in split(c, result):
                out[:, pl.ds(pl.multiple_of(BODY_TILES * g * LANES + first, LANES), width)] = piece
        return 0

    lax.fori_loop(0, chunks - 1, some_lanes, 0)
    tails = [None] * len(outs)
    for c, result in results(pl.ds((chunks - 1) * width, width)):
        for k, out, g, piece in split(c, result):
            out[:, pl.ds((BODY_TILES * (g + 1) - 1) * LANES, LANES)] = piece[:, :LANES]
            tail = turn(piece[:, LANES:], 8 * g)
            tails[k] = tail if g == 0 else jnp.where(lanes >= 8 * g, tail, tails[k])
    for out, tail in zip(outs, tails):
        out[:, pl.ds((BACK_TILES - 1) * LANES, LANES)] = tail


def trace_blocks(me):
    odd, late = lax.rem(me, 2), lax.rem(me, 4) // 2
    return 3 - 2 * odd, 1 + 2 * odd, 4 - 4 * late, 4 * late


def trace_partner(me, matching, size):
    step, start = ((1, 0), (1, 1), (2, 0), (2, 2))[matching]
    return (((me + start) ^ step) - start) % size


def update_kernel(plans, in0, in1, in2, in3, local_sum, table, updated, own, out0, out1, out2, out3, chunks):
    me = lax.axis_index("plane")
    rows_total = local_sum.shape[1]
    last = NODES - 1
    lanes = lane_ids(8)
    for k, source in enumerate((in0, in1, in2, in3)):
        chunks[me ^ PARTNERS[k]] = source[...]

    trace_plans = [
        tile_plan([(k, 0, 0, 32), (last, 32 * k, 32, 32), (k, 256, 64, 32), (0, 32 * k, 96, 32)], 1)[0]
        for k in range(NODES)
    ]

    blocks = trace_blocks(lax.axis_index("dom"))

    def wide(row):
        return jnp.broadcast_to(table[pl.ds(row, 1), :], (8, LANES))

    def some_rows(g, _):
        rows = pl.ds(pl.multiple_of(g * 8, 8), 8)
        tails = [
            pltpu.roll(tile_at(chunks, (b,), slice(None), BACK_TILES - 1), lax.rem(LANES - 8 * g, LANES), 1)
            for b in range(4)
        ]

        def load(source, tile):
            if source[0] == "tail":
                return tails[source[1]]
            at = pl.multiple_of((BODY_TILES * g + tile) * LANES, LANES)
            return chunks[source[1], :, pl.ds(at, LANES)]

        for i in range(NODES):
            for t in range(SLAB_TILES):
                value = pieced(plans[i][t], load, lanes)
                updated[i, rows, pl.ds(t * LANES, LANES)] = (
                    tile_at(local_sum, (i,), rows, t) + step_size * value
                )
        raw = [
            pieced(plan, lambda i, tile: tile_at(updated, (i,), rows, tile), lanes) for plan in trace_plans
        ]
        turned_round = wide(15) == 1
        seen = [jnp.where(turned_round, raw[last - k], raw[k]) for k in range(NODES)]
        partner = wide(16)
        for k in range(NODES):
            own[k, rows, :] = pick(seen[k], partner)
        for o, out in zip(blocks, (out0, out1, out2, out3)):
            slot_edge = wide(o)
            for t in range(2):
                total = None
                for k in range(5 * t, min(5 * t + 5, NODES)):
                    value = pick(seen[k], slot_edge)
                    total = value if total is None else jnp.where(lanes >= 24 * (k - 5 * t), value, total)
                out[rows, pl.ds(t * LANES, LANES)] = total
        return 0

    lax.fori_loop(0, rows_total // 8, some_rows, 0)


def pick(value, index):
    return jnp.take_along_axis(value, index, axis=1, mode="promise_in_bounds")


def join_edges(table, updated, own, came, state):
    rows_total = updated.shape[1]
    last = NODES - 1
    lanes = lane_ids(8)
    blocks = trace_blocks(lax.axis_index("dom"))

    def wide(row):
        return jnp.broadcast_to(table[pl.ds(row, 1), :], (8, LANES))

    share = wide(17).astype(jnp.float32)
    quarter = lanes // 32

    def group(value, at):
        return turn(value, -32 * at)

    def some_rows(g, _):
        rows = pl.ds(pl.multiple_of(g * 8, 8), 8)
        sums = []
        for k in range(NODES):
            total = jnp.where(wide(12) > 0, own[k, rows, :], 0.0)
            for o, source in zip(blocks, came):
                value = pick(tile_at(source, (), rows, k // 5), wide(5 + o) + 24 * (k % 5))
                total = jnp.where(wide(10 + o) > 0, value, total)
            sums.append(total)

        def spread(at, t):
            nodes = range(4 * t, min(4 * t + 4, NODES))
            value, number = None, None
            for k in nodes:
                q = k - 4 * t
                moved = turn(sums[k], 32 * (q - at))
                many = turn(share, 32 * (q - at))
                value = jnp.where(quarter == q, moved, 0.0 if value is None else value)
                number = jnp.where(quarter == q, many, 0.0 if number is None else number)
            return value, number

        for i in range(NODES):
            for t in range(SLAB_TILES):
                total = tile_at(updated, (i,), rows, t)
                weight = None
                if t == 0:
                    total += jnp.where(quarter == 0, sums[i], 0.0)
                    weight = 1.0 + jnp.where(quarter == 0, share, 0.0)
                if i == last:
                    value, number = spread(1, t)
                    total += value
                    weight = (1.0 if weight is None else weight) + number
                if t == 2:
                    total += jnp.where(quarter == 0, group(sums[i], 2), 0.0)
                    weight = (1.0 if weight is None else weight) + jnp.where(quarter == 0, group(share, 2), 0.0)
                if i == 0:
                    value, number = spread(3, t)
                    total += value
                    weight = (1.0 if weight is None else weight) + number
                if weight is not None:
                    total = total / weight
                state[i, rows, pl.ds(t * LANES, LANES)] = total
        return 0

    lax.fori_loop(0, rows_total // 8, some_rows, 0)


def next_kernel(plans, table, updated, own, r0, r1, r2, r3, state, out0, out1, out2, out3, xi, staged):
    me = lax.axis_index("plane")
    join_edges(table, updated, own, (r0, r1, r2, r3), state)
    make_sends(me, plans, updated.shape[1], state, xi, staged, (out0, out1, out2, out3))


def last_kernel(table, updated, own, r0, r1, r2, r3, out, state, given, sems):
    join_edges(table, updated, own, (r0, r1, r2, r3), state)
    comps, local, elements = given.shape[0], given.shape[3], given.shape[4]
    copies = []
    for i in range(NODES):
        for c in range(comps):
            rows = pl.ds(c * local, local)
            for t in range(SLAB_TILES):
                tile = tile_at(state, (i,), rows, t)
                for q in range(min(4, NODES - 4 * t)):
                    given[c, i, 4 * t + q] = turn(tile, -32 * q)[:, :elements]
        copies.append(pltpu.make_async_copy(given.at[:, i], out.at[:, i], sems.at[i]))
        copies[-1].start()
    for copy in copies:
        copy.wait()


def f32(*shape):
    return jax.ShapeDtypeStruct(shape, jnp.float32)


def kernel_call(body, outs, scratch, flops, moved, **more):
    return pl.pallas_call(
        body,
        out_shape=outs,
        scratch_shapes=scratch,
        compiler_params=pltpu.CompilerParams(vmem_limit_bytes=16 * 1024 * 1024),
        cost_estimate=pl.CostEstimate(flops=flops, bytes_accessed=moved, transcendentals=0),
        **more,
    )


def swapped(buffers):
    planes = range(len(buffers))
    return [buffers[0]] + [
        lax.ppermute(buffer, "plane", [(i, i ^ step) for i in planes])
        for buffer, step in zip(buffers[1:], PARTNERS[1:])
    ]


def packed_shards(adjoint, metric, base_flow, edge_list, flips):
    comps, local, nodes, _, elements = adjoint.shape
    planes = MODES // local
    points = nodes * nodes * elements // planes
    rows_total = comps * local
    partitions = lax.axis_size("dom")
    state_shape = (nodes, rows_total, SLAB_TILES * LANES)

    layouts = [send_segments(chunk, points) for chunk in range(planes)]
    plans = [tile_plan(segments, SEND_TILES) for segments, _ in layouts]
    gaps = [gap for _, gap in layouts]
    back_plans = return_segments(points)
    to_span, to_modes = span_weights(planes)
    slab_bands = eta_bands(0, SLAB_TILES * LANES, nodes * elements)
    chunk_bands = np.stack(
        [eta_bands((points - 2 * nodes * elements) * b, CHUNK_TILES * LANES, points) for b in range(planes)]
    )

    metric_tile = jnp.pad(jnp.tile(metric, (1, LANES // elements)), ((0, 4), (0, 0)))
    flow_rows = (
        base_flow.reshape(STEPS, 12, -1, LANES).transpose(1, 2, 0, 3).reshape(-1, LANES)
    )

    in_hbm = pl.BlockSpec(memory_space=pltpu.HBM)
    sends = [f32(rows_total, SEND_TILES * LANES)] * planes
    send_scratch = [
        pltpu.VMEM(state_shape, jnp.float32),
        pltpu.VMEM((planes, rows_total, SEND_TILES * LANES), jnp.float32),
    ]
    row_copies = [
        pltpu.VMEM((comps, nodes, nodes, local, elements), jnp.float32),
        pltpu.SemaphoreType.DMA((nodes,)),
    ]
    in_rows = pltpu.with_memory_space_constraint(adjoint.transpose(0, 2, 3, 1, 4), pltpu.HBM)
    state, *outgoing = kernel_call(
        functools.partial(first_kernel, plans),
        [f32(*state_shape), *sends],
        send_scratch + row_copies,
        4 * 10**6,
        4 * 10**6,
        in_specs=[in_hbm],
    )(in_rows)
    flows = kernel_call(
        functools.partial(flow_kernel, points),
        [f32(12, MODES, CHUNK_TILES * LANES)] * STEPS,
        [],
        4 * 10**6,
        9 * 10**6,
    )(flow_rows, metric_tile)
    table = kernel_call(
        tables_kernel, jax.ShapeDtypeStruct((24, LANES), jnp.int32), [], 10**5, 10**5
    )(edge_list[0].T, flips[0].T)

    for step_index in range(STEPS):
        fields = [
            kernel_call(
                functools.partial(fields_kernel, gaps),
                f32(3, comps, local, CHUNK_TILES * LANES),
                [],
                2 * 10**6,
                10**6,
            )(came, chunk_bands)
            for came in swapped(outgoing)
        ]
        returning = kernel_call(
            advect_kernel,
            [f32(GROUP, BACK_TILES * LANES)] * planes,
            [],
            80 * 10**6,
            5 * 10**6,
        )(*fields, flows[step_index], to_span, to_modes)
        local_sum = kernel_call(
            diffuse_kernel,
            f32(*state_shape),
            [pltpu.VMEM((nodes, GROUP, SLAB_TILES * LANES), jnp.float32)] * 2,
            12 * 10**6,
            2 * 10**6,
        )(state, metric_tile, slab_bands)
        updated, own, *leaving = kernel_call(
            functools.partial(update_kernel, back_plans),
            [f32(*state_shape), f32(nodes, rows_total, LANES)] + [f32(rows_total, 2 * LANES)] * 4,
            [pltpu.VMEM((planes, GROUP, BACK_TILES * LANES), jnp.float32)],
            2 * 10**6,
            3 * 10**6,
        )(*swapped(returning), local_sum, table)
        traces = [
            lax.ppermute(
                buffer, "dom", [(i, trace_partner(i, matching, partitions)) for i in range(partitions)]
            )
            for matching, buffer in enumerate(leaving)
        ]
        if step_index + 1 < STEPS:
            state, *outgoing = kernel_call(
                functools.partial(next_kernel, plans),
                [f32(*state_shape), *sends],
                send_scratch,
                6 * 10**6,
                4 * 10**6,
            )(table, updated, own, *traces)
        else:
            result = kernel_call(
                last_kernel,
                f32(comps, nodes, nodes, local, elements),
                [pltpu.VMEM(state_shape, jnp.float32), *row_copies],
                2 * 10**6,
                3 * 10**6,
                out_specs=in_hbm,
            )(table, updated, own, *traces)
    return result.transpose(0, 3, 1, 2, 4)


def plain_shards(adjoint, metric, base_flow, edge_list, flips):
    local_modes = adjoint.shape[1]
    deriv_table = cheb_table(adjoint.shape[2])
    span_basis, span_slope, forward, wave_sq = span_tables(MODES)
    wave_local = lax.dynamic_slice_in_dim(
        wave_sq, lax.axis_index("plane") * local_modes, local_modes, 0
    )
    adjoint_state = adjoint
    for step_index in range(STEPS):
        base_now = base_flow[step_index].reshape(12, MODES, -1)
        adjoint_state = advance(
            adjoint_state,
            metric,
            base_now,
            edge_list[0],
            flips[0],
            deriv_table,
            span_basis,
            span_slope,
            forward,
            wave_local,
        )
    return adjoint_state


def shards(adjoint, metric, base_flow, edge_list, flips):
    if adjoint.shape[1:] == (MODES // 4, NODES, NODES, 32) and (
        edge_list.shape[1:] == (5, 24) and lax.axis_size("dom") % 4 == 0
    ):
        return packed_shards(adjoint, metric, base_flow, edge_list, flips)
    return plain_shards(adjoint, metric, base_flow, edge_list, flips)


def solution(mesh):
    placed = (
        P(None, "plane", None, None, "dom"),
        P(None, "dom"),
        P(None, None, ("dom", "plane")),
        P("dom", None, None),
        P("dom", None, None),
    )
    return jax.shard_map(
        shards,
        mesh=mesh,
        in_specs=placed,
        out_specs=P(None, "plane", None, None, "dom"),
        check_vma=False,
    )
```

```python
import functools

import jax
import jax.numpy as jnp
import numpy as np
from jax import lax
from jax.experimental import pallas as pl
from jax.experimental.pallas import tpu as pltpu
from jax.sharding import PartitionSpec as P

MODES = 64
STEPS = 2


step_size = 0.01
viscosity = 0.02


def passed_along(shard, axis, by):
    size = lax.axis_size(axis)
    return lax.ppermute(shard, axis, [(i, (i + by) % size) for i in range(size)])


def cheb_table(node_count):
    order = node_count - 1
    node_ids = jnp.arange(node_count, dtype=jnp.int32)
    node_coords = -jnp.cos(jnp.pi * node_ids.astype(jnp.float32) / order)
    weight = jnp.where((node_ids == 0) | (node_ids == order), 2.0, 1.0).astype(jnp.float32)
    parity = jnp.where((node_ids[:, None] + node_ids[None, :]) % 2 == 0, 1.0, -1.0).astype(
        jnp.float32
    )
    on_diag = node_ids[:, None] == node_ids[None, :]
    differ = jnp.where(on_diag, 1.0, node_coords[:, None] - node_coords[None, :])
    off_diag = jnp.where(on_diag, 0.0, weight[:, None] / weight[None, :] * parity / differ)
    return off_diag - jnp.diag(jnp.sum(off_diag, axis=1))


def span_tables(modes):
    mode_ids = jnp.arange(modes, dtype=jnp.int32)
    wavenumber = (mode_ids + 1) // 2
    is_cosine = (mode_ids % 2 == 1) | (mode_ids == 0)
    span_ids = jnp.arange(modes, dtype=jnp.int32)
    phase_num = span_ids[:, None] * wavenumber[None, :] % modes
    angles = 2.0 * jnp.pi * phase_num.astype(jnp.float32) / modes
    cosines = jnp.cos(angles)
    sines = jnp.sin(angles)
    wave_f = wavenumber.astype(jnp.float32)
    span_basis = jnp.where(is_cosine[None, :], cosines, sines)
    span_slope = jnp.where(is_cosine[None, :], -wave_f[None, :] * sines, wave_f[None, :] * cosines)
    scaling = jnp.where((mode_ids == 0) | (mode_ids == modes - 1), 1.0 / modes, 2.0 / modes).astype(
        jnp.float32
    )
    forward = span_basis.T * scaling[:, None]
    return (span_basis, span_slope, forward, wave_f * wave_f)


def directional(field_data, metric, deriv_table, xi_row, eta_row):
    along_xi = jnp.einsum(
        "ai,cmije->cmaje", deriv_table, field_data, precision=lax.Precision.HIGHEST
    )
    along_eta = jnp.einsum(
        "bj,cmije->cmibe", deriv_table, field_data, precision=lax.Precision.HIGHEST
    )
    return metric[xi_row] * along_xi + metric[eta_row] * along_eta


def advect(coeffs, base_now, span_basis, span_slope, forward):
    values = jnp.einsum("nm,fmq->fnq", span_basis, coeffs, precision=lax.Precision.HIGHEST)
    along_z = jnp.einsum("nm,cmq->cnq", span_slope, coeffs[0:3], precision=lax.Precision.HIGHEST)
    products = []
    for comp in range(3):
        term = (
            base_now[0] * values[3 + comp]
            + base_now[1] * values[6 + comp]
            + base_now[2] * along_z[comp]
        )
        term = term - (
            values[0] * base_now[3 + comp]
            + values[1] * base_now[6 + comp]
            + values[2] * base_now[9 + comp]
        )
        products.append(term)
    return jnp.einsum("mn,cnq->cmq", forward, jnp.stack(products), precision=lax.Precision.HIGHEST)


def accumulate(field_data, edge_sums, counts):
    node_count = field_data.shape[2]
    last = node_count - 1
    total = field_data
    total = total.at[:, :, :, 0, :].add(edge_sums[:, :, :, 0, :])
    total = total.at[:, :, last, :, :].add(edge_sums[:, :, :, 1, :])
    total = total.at[:, :, :, last, :].add(edge_sums[:, :, :, 2, :])
    total = total.at[:, :, 0, :, :].add(edge_sums[:, :, :, 3, :])
    weight = jnp.ones((node_count, node_count, field_data.shape[4]), jnp.float32)
    weight = weight.at[:, 0, :].add(counts[0][None, :])
    weight = weight.at[last, :, :].add(counts[1][None, :])
    weight = weight.at[:, last, :].add(counts[2][None, :])
    weight = weight.at[0, :, :].add(counts[3][None, :])
    return total / weight


def assemble(field_data, edge_slots, flip_flags):
    components, local_modes, node_count, _, elements = field_data.shape
    last = node_count - 1
    row_count = components * local_modes * node_count
    traces = jnp.stack(
        [
            field_data[:, :, :, 0, :],
            field_data[:, :, last, :, :],
            field_data[:, :, :, last, :],
            field_data[:, :, 0, :, :],
        ],
        axis=3,
    )
    edge_table = traces.reshape(row_count, 4 * elements)
    blocks, capacity = edge_slots.shape
    half_span = (blocks - 1) // 2
    slot_edges = edge_slots.reshape(-1)
    occupied = (slot_edges >= 0).astype(jnp.float32)
    outgoing = jnp.take(edge_table, jnp.maximum(slot_edges, 0), axis=1) * occupied[None, :]

    def block_of(block_id):
        return outgoing[:, block_id * capacity : (block_id + 1) * capacity]

    own_pairs = (
        block_of(half_span)
        .reshape(row_count, capacity // 2, 2)[:, :, ::-1]
        .reshape(row_count, capacity)
    )
    received = {half_span: own_pairs}
    for block_id in range(blocks):
        if block_id != half_span:
            received[block_id] = passed_along(
                block_of(blocks - 1 - block_id), "dom", half_span - block_id
            )
    partners = jnp.concatenate([received[block_id] for block_id in range(blocks)], axis=1)
    shaped = partners.reshape(components * local_modes, node_count, blocks * capacity)
    shaped = (
        jnp.where(flip_flags.reshape(-1)[None, None, :] == 1, shaped[:, ::-1, :], shaped)
        * occupied[None, None, :]
    )
    onehot = (slot_edges[:, None] == jnp.arange(4 * elements, dtype=jnp.int32)[None, :]).astype(
        jnp.float32
    )
    edge_sums = jnp.dot(
        shaped.reshape(row_count, blocks * capacity), onehot, precision=lax.Precision.HIGHEST
    )
    edge_sums = edge_sums.reshape(components, local_modes, node_count, 4, elements)
    counts = jnp.sum(onehot, axis=0).reshape(4, elements)
    return accumulate(field_data, edge_sums, counts)


def advance(
    adjoint_state,
    metric,
    base_now,
    edge_slots,
    flip_flags,
    deriv_table,
    span_basis,
    span_slope,
    forward,
    wave_local,
):
    components, local_modes, node_count, _, elements = adjoint_state.shape
    points = node_count * node_count * elements
    grad_x = directional(adjoint_state, metric, deriv_table, 0, 2)
    grad_y = directional(adjoint_state, metric, deriv_table, 1, 3)
    stacked = jnp.concatenate([adjoint_state, grad_x, grad_y], axis=0).reshape(
        9, local_modes, points
    )
    gathered = lax.all_to_all(stacked, "plane", split_axis=2, concat_axis=1, tiled=True)
    advective = advect(gathered, base_now, span_basis, span_slope, forward)
    returned = lax.all_to_all(advective, "plane", split_axis=1, concat_axis=2, tiled=True).reshape(
        adjoint_state.shape
    )
    laplacian = directional(grad_x, metric, deriv_table, 0, 2) + directional(
        grad_y, metric, deriv_table, 1, 3
    )
    updated = adjoint_state + step_size * (
        returned + viscosity * (laplacian - wave_local[None, :, None, None, None] * adjoint_state)
    )
    return assemble(updated, edge_slots, flip_flags)


NODES = 9
LANES = 128
SLAB_TILES = 3
STATE_TILES = 7
SEND_TILES = 12
CHUNK_TILES = 6
BODY_TILES = 5
BACK_TILES = 31
GROUP = 8
PARTNERS = (0, 2, 1, 3)
STEP_VISC = step_size * viscosity


def cheb_numbers():
    order = NODES - 1
    coords = -np.cos(np.pi * np.arange(NODES) / order)
    weight = np.ones(NODES)
    weight[0] = weight[-1] = 2.0
    table = np.zeros((NODES, NODES))
    for a in range(NODES):
        for i in range(NODES):
            if a != i:
                table[a, i] = weight[a] / weight[i] * (-1.0) ** (a + i) / (coords[a] - coords[i])
    return table - np.diag(table.sum(axis=1))


DERIV = cheb_numbers()


def span_numbers():
    modes = np.arange(MODES)
    wave = (modes + 1) // 2
    is_cosine = (modes % 2 == 1) | (modes == 0)
    angles = 2.0 * np.pi * (np.arange(MODES)[:, None] * wave[None, :] % MODES) / MODES
    cosines, sines = np.cos(angles), np.sin(angles)
    basis = np.where(is_cosine, cosines, sines)
    slope = np.where(is_cosine, -wave * sines, wave * cosines)
    scaling = np.where((modes == 0) | (modes == MODES - 1), 1.0 / MODES, 2.0 / MODES)
    return basis, slope, basis.T * scaling[:, None]


def in_two(table):
    table = table.astype(np.float32)
    high = table.astype(jnp.bfloat16)
    low = (table - high.astype(np.float32)).astype(jnp.bfloat16)
    return high, low


def span_weights(planes):
    basis, slope, forward = span_numbers()
    local = MODES // planes
    to_span, to_modes = [], []
    for me in range(planes):
        came = np.concatenate([(me ^ step) * local + np.arange(local) for step in PARTNERS])
        high, low = in_two(np.concatenate([basis, slope])[:, came])
        to_span.append(np.concatenate([high, high, low], axis=1))
        high, low = in_two(forward[came])
        to_modes.append(np.concatenate([high, high, low], axis=1))
    return np.stack(to_span), np.stack(to_modes)


def eta_bands(first_lane, lanes, count):
    bands = np.zeros((24, lanes), np.float32)
    for lane in range(count):
        j = (first_lane + lane) % 288 // 32
        for d in range(-8, 9):
            if 0 <= j + d < NODES:
                bands[d + 8, lane] = DERIV[j, j + d]
    return bands


def tile_plan(segments, tiles):
    plan = [[] for _ in range(tiles)]
    for source, src, dst, length in segments:
        done = 0
        while done < length:
            s, d = src + done, dst + done
            size = min(length - done, LANES - s % LANES, LANES - d % LANES)
            plan[d // LANES].append((source, s // LANES, (d - s) % LANES, d % LANES, size))
            done += size
    return plan


def send_segments(chunk, points):
    ring, slab = STATE_TILES * LANES, NODES * 32
    turned = (points - 2 * slab) * chunk
    segments = []
    for r in range(3):
        start = (r * slab - turned) % ring
        first = min(slab, ring - start)
        segments.append((("state", 2 * chunk + r), 0, start, first))
        if first < slab:
            segments.append((("state", 2 * chunk + r), first, 0, slab - first))
    gap = (3 * slab - turned) % ring
    body = (points // LANES) * LANES
    lane = points * chunk
    for lane in range(points * chunk, points * (chunk + 1), 8):
        at = lane - points * chunk
        target = ring + at if at < body else gap + at - body
        source = ("xi", lane // slab)
        if segments[-1][0] == source and segments[-1][1] + segments[-1][3] == lane % slab and (
            segments[-1][2] + segments[-1][3] == target
        ):
            segments[-1] = (source, segments[-1][1], segments[-1][2], segments[-1][3] + 8)
        else:
            segments.append((source, lane % slab, target, 8))
    return segments, gap


def return_segments(points):
    slab = NODES * 32
    body = points // LANES * LANES
    plans = []
    for i in range(NODES):
        segments = []
        for chunk in range(4):
            for name, start, stop in (("body", 0, body), ("tail", body, points)):
                low = max(i * slab, chunk * points + start)
                high = min((i + 1) * slab, chunk * points + stop)
                if low < high:
                    segments.append(((name, chunk), low - chunk * points - start, low - i * slab, high - low))
        plans.append(tile_plan(segments, SLAB_TILES))
    return plans


def lane_ids(rows):
    return lax.broadcasted_iota(jnp.int32, (rows, LANES), 1)


def turn(value, shift):
    return value if shift % LANES == 0 else pltpu.roll(value, shift % LANES, 1)


def turner(load):
    made = {}

    def turned(source, tile, shift):
        key = source, tile, shift
        if key not in made:
            made[key] = turn(load(source, tile), shift)
        return made[key]

    return turned


def pieced(pieces, turned, lanes):
    total = None
    for source, tile, shift, low, size in pieces:
        value = turned(source, tile, shift)
        if total is None:
            total = value
        elif low + size == LANES:
            total = jnp.where(lanes >= low, value, total)
        else:
            total = jnp.where((lanes >= low) & (lanes < low + size), value, total)
    return total


def aligned(index, unit):
    return index if isinstance(index, int) else pl.multiple_of(index, unit)


def group_rows(g):
    return pl.ds(aligned(g * GROUP, GROUP), GROUP)


def tile_at(ref, lead, rows, tile):
    return ref[(*lead, rows, pl.ds(tile * LANES, LANES))]


def along_i(tiles):
    return [
        sum(tiles[i] * float(DERIV[a, i]) for i in range(1, NODES)) + tiles[0] * float(DERIV[a, 0])
        for a in range(NODES)
    ]


def turned_tiles(tiles, lanes):
    out = [tiles]
    for s in range(1, 4):
        spun = [pltpu.roll(t, LANES - 32 * s, 1) for t in tiles]
        out.append(
            [
                jnp.where(lanes < LANES - 32 * s, spun[t], spun[(t + 1) % len(tiles)])
                for t in range(len(tiles))
            ]
        )
    return out


def along_j(turned, ring, tile, band, used):
    total = None
    for d in used:
        term = turned[d % 4][(tile + d // 4) % ring] * band(d)
        total = term if total is None else total + term
    return total


def make_sends(plans, groups, state, xi, staged):
    lanes = lane_ids(GROUP)
    for g in groups:
        rows = group_rows(g)
        for t in range(SLAB_TILES):
            for a, value in enumerate(along_i([tile_at(state, (i,), rows, t) for i in range(NODES)])):
                xi[a, rows, pl.ds(t * LANES, LANES)] = value
    for g in groups:
        rows = group_rows(g)

        def load(source, tile, rows=rows):
            return tile_at(state if source[0] == "state" else xi, (source[1],), rows, tile)

        turned = turner(load)
        for chunk, plan in enumerate(plans):
            for t, pieces in enumerate(plan):
                staged[chunk, rows, pl.ds(t * LANES, LANES)] = pieced(pieces, turned, lanes)


def hand_out(me, staged, outs):
    for step, out in zip(PARTNERS, outs):
        out[...] = staged[me ^ step]


def first_kernel(plans, adjoint, state, out0, out1, out2, out3, xi, staged, taken, sems):
    me = lax.axis_index("plane")
    comps, local = taken.shape[0], taken.shape[3]

    def copy(c):
        return pltpu.make_async_copy(adjoint.at[c], taken.at[c], sems.at[c])

    for c in range(comps):
        copy(c).start()

    for c in range(comps):
        copy(c).wait()
        rows = pl.ds(c * local, local)
        for i in range(NODES):
            for t in range(SLAB_TILES):
                parts = [taken[c, i, j] for j in range(4 * t, min(4 * t + 4, NODES))]
                parts += [jnp.zeros_like(parts[0])] * (4 - len(parts))
                state[i, rows, pl.ds(t * LANES, LANES)] = jnp.concatenate(parts, axis=1)
        make_sends(plans, range(c * local // GROUP, (c + 1) * local // GROUP), state, xi, staged)
    hand_out(me, staged, (out0, out1, out2, out3))


def metric_rows(metric):
    wide = jnp.concatenate([metric[...]] * (LANES // metric.shape[1]), axis=1)
    return jnp.concatenate([wide, wide], axis=0)


def flow_kernel(points, flow, metric, out0, out1, flat):
    me = lax.axis_index("plane")
    lanes, subs = lane_ids(8), lax.broadcasted_iota(jnp.int32, (8, LANES), 0)
    shift = lax.rem(LANES - lax.rem(me * points, LANES), LANES)
    turned = pltpu.roll(metric_rows(metric), shift, 1)
    ahead = pl.program_id(0) == 0
    first_first = jnp.where(ahead, turned[0:1], 1.0)
    first_second = jnp.where(ahead, turned[1:2], 0.0)
    second_first = jnp.where(ahead, turned[2:3], 0.0)
    second_second = jnp.where(ahead, turned[3:4], 1.0)
    per_sixteen = 16 * points // LANES
    last = CHUNK_TILES - 1

    for f in range(2):
        for s in range(STEPS):
            flat[f, s] = flow[f, s].reshape(flat.shape[2:])

    for s, out in enumerate((out0, out1)):
        for half in range(2):
            moved = (lanes + 64 * half + 8 * subs) & (LANES - 1)
            kept = lanes < LANES - 64 * half - 8 * subs

            def some_rows(h, _, s=s, half=half, out=out, moved=moved, kept=kept):
                rows = pl.ds(pl.multiple_of(16 * h + 8 * half, 8), 8)

                def field(f):
                    spun = []
                    for k in range(CHUNK_TILES):
                        start = per_sixteen * h + 40 * half + k
                        spun.append(pick(flat[f, s, pl.ds(start, 8, stride=5), :], moved))
                    return [jnp.where(kept, spun[k], spun[k + 1]) for k in range(last)] + [spun[last]]

                for t, (one, two) in enumerate(zip(field(0), field(1))):
                    out[0, rows, pl.ds(t * LANES, LANES)] = one * first_first + two * first_second
                    out[1, rows, pl.ds(t * LANES, LANES)] = one * second_first + two * second_second
                return 0

            lax.fori_loop(0, MODES // 16, some_rows, 0)


def tables_kernel(edges, flags, table, square):
    blocks, _, capacity = edges.shape
    lanes = lane_ids(capacity)
    slots = lax.broadcasted_iota(jnp.int32, (capacity, LANES), 0)
    here = slots == lax.rem(lanes, capacity)
    flag = jnp.zeros((1, LANES), jnp.int32)
    count = jnp.zeros((1, LANES), jnp.int32)
    table[...] = jnp.zeros(table.shape, jnp.int32)
    square[...] = jnp.zeros(square.shape, jnp.float32)
    for o in range(blocks):
        square[o : o + 1, 0:capacity] = edges[o].astype(jnp.float32)
        square[blocks + o : blocks + o + 1, 0:capacity] = flags[o].astype(jnp.float32)
    columns = square[...].T[0:capacity].astype(jnp.int32)
    for o in range(blocks):
        column = jnp.broadcast_to(columns[:, o : o + 1], (capacity, LANES))
        held = column == lanes

        def summed(mask, value):
            return jnp.sum(jnp.where(mask, value, 0), axis=0, keepdims=True)

        table[o : o + 1, :] = summed(here, jnp.maximum(column, 0))
        table[5 + o : 6 + o, :] = summed(held, slots)
        present = summed(held, jnp.ones_like(slots))
        table[10 + o : 11 + o, :] = present
        flag += summed(held, jnp.broadcast_to(columns[:, blocks + o : blocks + o + 1], (capacity, LANES)))
        count += present
        if o == blocks // 2:
            partner = slots + 1 - 2 * lax.rem(slots, 2)
            slot_of = jnp.broadcast_to(summed(held, partner), (capacity, LANES))
            partner_edge = summed(slots == slot_of, jnp.maximum(column, 0))
            table[16:17, :] = jnp.where(present > 0, partner_edge, 0)
    table[15:16, :] = flag
    table[17:18, :] = count


def diffuse_kernel(state, metric, bands, local_sum, first, second):
    me = lax.axis_index("plane")
    rows_total = state.shape[1]
    lanes = lane_ids(8)
    local = rows_total // 3
    wide = metric_rows(metric)
    xi_x, xi_y, eta_x, eta_y = (wide[r : r + 1] for r in range(4))
    g_ii = xi_x * xi_x + xi_y * xi_y
    g_ij = xi_x * eta_x + xi_y * eta_y
    g_jj = eta_x * eta_x + eta_y * eta_y
    used = [[d for d in range(-8, 9) if any(0 <= j + d < NODES for j in range(4 * t, min(4 * t + 4, NODES)))]
            for t in range(SLAB_TILES)]

    def eta_of(tiles):
        turned = turned_tiles(tiles, lanes)
        return [
            along_j(turned, SLAB_TILES, t, lambda d, t=t: tile_at(bands, (), pl.ds(d + 8, 1), t), used[t])
            for t in range(SLAB_TILES)
        ]

    def some_rows(g, _):
        rows = pl.ds(pl.multiple_of(g * 8, 8), 8)
        first_mode = me * local + lax.rem(g * 8, local)
        wave = ((first_mode + lax.broadcasted_iota(jnp.int32, (8, LANES), 0) + 1) // 2).astype(jnp.float32)
        wave_sq = wave * wave
        for t in range(SLAB_TILES):
            for a, value in enumerate(along_i([tile_at(state, (i,), rows, t) for i in range(NODES)])):
                first[a, :, pl.ds(t * LANES, LANES)] = value
        for i in range(NODES):
            eta = eta_of([tile_at(state, (i,), rows, t) for t in range(SLAB_TILES)])
            mixed = []
            for t in range(SLAB_TILES):
                xi = first[i, :, pl.ds(t * LANES, LANES)]
                first[i, :, pl.ds(t * LANES, LANES)] = g_ii * xi + g_ij * eta[t]
                mixed.append(g_ij * xi + g_jj * eta[t])
            for t, value in enumerate(eta_of(mixed)):
                second[i, :, pl.ds(t * LANES, LANES)] = value
        for t in range(SLAB_TILES):
            tiles = [first[i, :, pl.ds(t * LANES, LANES)] for i in range(NODES)]
            for a, value in enumerate(along_i(tiles)):
                now = tile_at(state, (a,), rows, t)
                laplacian = value + second[a, :, pl.ds(t * LANES, LANES)]
                local_sum[a, rows, pl.ds(t * LANES, LANES)] = now + STEP_VISC * (laplacian - wave_sq * now)
        return 0

    lax.fori_loop(0, rows_total // 8, some_rows, 0)


def halves(value):
    high = value.astype(jnp.bfloat16)
    return high, (value - high.astype(jnp.float32)).astype(jnp.bfloat16)


def fields_kernel(gaps, source, bands, fields):
    me = lax.axis_index("plane")
    rows_total = source.shape[0]
    local = fields.shape[2]
    lanes = lane_ids(GROUP)
    gap = sum(jnp.where(me == b, g, 0) for b, g in enumerate(gaps))
    gap_tile, gap_lane = gap // LANES, lax.rem(gap, LANES)

    for g in range(rows_total // GROUP):
        rows = group_rows(g)
        c = g * GROUP // local
        target = pl.ds(g * GROUP % local, GROUP)
        tiles = [tile_at(source, (), rows, t) for t in range(STATE_TILES)]
        turned = turned_tiles(tiles, lanes)
        for t in range(CHUNK_TILES):
            at = pl.ds(t * LANES, LANES)
            fields[0, c, target, at] = tiles[t]
            fields[2, c, target, at] = along_j(
                turned, STATE_TILES, t, lambda d, at=at: bands[me, pl.ds(d + 8, 1), at], range(-8, 9)
            )
        for t in range(BODY_TILES):
            fields[1, c, target, pl.ds(t * LANES, LANES)] = tile_at(source, (), rows, STATE_TILES + t)
        tail = source[rows, pl.ds(pl.multiple_of(gap_tile * LANES, LANES), LANES)]
        fields[1, c, target, pl.ds(BODY_TILES * LANES, LANES)] = pltpu.roll(
            tail, lax.rem(LANES - gap_lane, LANES), 1
        )


def advect_kernel(fields0, fields1, fields2, fields3, flow, to_span, to_modes, *outs):
    me = lax.axis_index("plane")
    comps = fields0.shape[1]
    both = to_span[me]
    basis = both[:MODES]
    back = to_modes[me]
    width = 2 * LANES
    chunks = CHUNK_TILES * LANES // width
    lanes = lane_ids(GROUP)

    def dot(a, value):
        high, low = halves(value)
        stacked = jnp.concatenate([high, low, high], axis=0)
        return jnp.dot(a, stacked, preferred_element_type=jnp.float32)

    def results(part):
        def field(kind, c):
            return jnp.concatenate(
                [fields[kind, c, :, part] for fields in (fields0, fields1, fields2, fields3)], axis=0
            )

        values, sums = [], []
        for c in range(comps):
            out = dot(both, field(0, c))
            values.append(out[:MODES])
            along_x = flow[0, :, part] * dot(basis, field(1, c))
            along_y = flow[1, :, part] * dot(basis, field(2, c))
            sums.append(along_x + along_y + flow[2, :, part] * out[MODES:])
        for c in range(comps):
            taken = values[0] * flow[3 + c, :, part]
            taken += values[1] * flow[6 + c, :, part]
            taken += values[2] * flow[9 + c, :, part]
            yield c, dot(back, sums[c] - taken)

    def split(c, result):
        for k, out in enumerate(outs):
            for half in range(MODES // len(outs) // GROUP):
                first = k * (MODES // len(outs)) + half * GROUP
                yield k, out, c * (MODES // len(outs) // GROUP) + half, result[first : first + GROUP]

    for first in range(0, (chunks - 1) * width, width):
        for c, result in results(pl.ds(first, width)):
            for _, out, g, piece in split(c, result):
                out[:, pl.ds(BODY_TILES * g * LANES + first, width)] = piece
    tails = [None] * len(outs)
    for c, result in results(pl.ds((chunks - 1) * width, width)):
        for k, out, g, piece in split(c, result):
            out[:, pl.ds((BODY_TILES * (g + 1) - 1) * LANES, LANES)] = piece[:, :LANES]
            tail = turn(piece[:, LANES:], 8 * g)
            tails[k] = tail if g == 0 else jnp.where(lanes >= 8 * g, tail, tails[k])
    for out, tail in zip(outs, tails):
        out[:, pl.ds((BACK_TILES - 1) * LANES, LANES)] = tail


def trace_blocks(me):
    odd, late = lax.rem(me, 2), lax.rem(me, 4) // 2
    return 4 * late, 1 + 2 * odd, 4 - 4 * late, 3 - 2 * odd


def trace_partner(me, matching, size):
    step, start = ((2, 2), (1, 1), (2, 0), (1, 0))[matching]
    return (((me + start) ^ step) - start) % size


def update_kernel(plans, in0, in1, in2, in3, local_sum, table, updated, own, out0, out1, out2, out3, chunks):
    me = lax.axis_index("plane")
    rows_total = local_sum.shape[1]
    last = NODES - 1
    lanes = lane_ids(8)
    for step, source in zip(PARTNERS, (in0, in1, in2, in3)):
        chunks[me ^ step] = source[...]

    trace_plans = [
        tile_plan([(k, 0, 0, 32), (last, 32 * k, 32, 32), (k, 256, 64, 32), (0, 32 * k, 96, 32)], 1)[0]
        for k in range(NODES)
    ]

    blocks = trace_blocks(lax.axis_index("dom"))

    def wide(row):
        return jnp.broadcast_to(table[pl.ds(row, 1), :], (8, LANES))

    turned_round, partner = wide(15) == 1, wide(16)
    slot_edges = [wide(o) for o in blocks]
    for g in range(rows_total // GROUP):
        rows = group_rows(g)

        def load(source, tile, g=g):
            if source[0] == "tail":
                return turn(tile_at(chunks, (source[1],), slice(None), BACK_TILES - 1), -8 * g)
            return tile_at(chunks, (source[1],), slice(None), BODY_TILES * g + tile)

        turned = turner(load)
        new = {}
        for i in range(NODES):
            for t in range(SLAB_TILES):
                value = pieced(plans[i][t], turned, lanes)
                new[i, t] = tile_at(local_sum, (i,), rows, t) + step_size * value
                updated[i, rows, pl.ds(t * LANES, LANES)] = new[i, t]
        edges = turner(lambda i, tile, new=new: new[i, tile])
        raw = [pieced(plan, edges, lanes) for plan in trace_plans]
        seen = [jnp.where(turned_round, raw[last - k], raw[k]) for k in range(NODES)]
        for slot_edge, out in zip(slot_edges, (out0, out1, out2, out3)):
            for t in range(2):
                total = None
                for k in range(5 * t, min(5 * t + 5, NODES)):
                    value = pick(seen[k], slot_edge)
                    total = value if total is None else jnp.where(lanes >= 24 * (k - 5 * t), value, total)
                out[rows, pl.ds(t * LANES, LANES)] = total
        for k in range(NODES):
            own[k, rows, :] = pick(seen[k], partner)


def pick(value, index):
    return jnp.take_along_axis(value, index, axis=1, mode="promise_in_bounds")


def join_edges(table, updated, own, came, state):
    rows_total = updated.shape[1]
    last = NODES - 1
    lanes = lane_ids(8)
    blocks = trace_blocks(lax.axis_index("dom"))

    def wide(row):
        return jnp.broadcast_to(table[pl.ds(row, 1), :], (8, LANES))

    share = wide(17).astype(jnp.float32)
    quarter = lanes // 32
    own_has = wide(12) > 0
    has = [wide(10 + o) > 0 for o in blocks]
    slots = [wide(5 + o) for o in blocks]

    def spread(values, at, t):
        value = None
        for k in range(4 * t, min(4 * t + 4, NODES)):
            moved = turn(values[k], 32 * (k - 4 * t - at))
            value = jnp.where(quarter == k - 4 * t, moved, 0.0 if value is None else value)
        return value

    def edge_parts(values, i, t):
        parts = []
        if t == 0:
            parts.append(jnp.where(quarter == 0, values[i], 0.0))
        if i == last:
            parts.append(spread(values, 1, t))
        if t == 2:
            parts.append(jnp.where(quarter == 0, turn(values[i], -64), 0.0))
        if i == 0:
            parts.append(spread(values, 3, t))
        return parts

    shares, scale = [share] * NODES, {}
    for i in (0, 1, last):
        for t in range(SLAB_TILES):
            parts = edge_parts(shares, i, t)
            if parts:
                scale[i, t] = 1.0 / (1.0 + sum(parts[1:], parts[0]))

    for g in range(rows_total // GROUP):
        rows = group_rows(g)
        sums = []
        for k in range(NODES):
            total = jnp.where(own_has, own[k, rows, :], 0.0)
            for slot, there, source in zip(slots, has, came):
                value = pick(tile_at(source, (), rows, k // 5), slot + 24 * (k % 5))
                total = jnp.where(there, value, total)
            sums.append(total)
        for i in range(NODES):
            for t in range(SLAB_TILES):
                total = tile_at(updated, (i,), rows, t)
                parts = edge_parts(sums, i, t)
                for part in parts:
                    total += part
                if parts:
                    total *= scale[i if i in (0, last) else 1, t]
                state[i, rows, pl.ds(t * LANES, LANES)] = total


def next_kernel(plans, table, updated, own, r0, r1, r2, r3, state, out0, out1, out2, out3, xi, staged):
    me = lax.axis_index("plane")
    join_edges(table, updated, own, (r0, r1, r2, r3), state)
    make_sends(plans, range(updated.shape[1] // GROUP), state, xi, staged)
    hand_out(me, staged, (out0, out1, out2, out3))


def last_kernel(table, updated, own, r0, r1, r2, r3, out, state, given, sems):
    join_edges(table, updated, own, (r0, r1, r2, r3), state)
    comps, local, elements = given.shape[0], given.shape[3], given.shape[4]
    copies = []
    for i in range(NODES):
        for c in range(comps):
            rows = pl.ds(c * local, local)
            for t in range(SLAB_TILES):
                tile = tile_at(state, (i,), rows, t)
                for q in range(min(4, NODES - 4 * t)):
                    given[c, i, 4 * t + q] = turn(tile, -32 * q)[:, :elements]
        copies.append(pltpu.make_async_copy(given.at[:, i], out.at[:, i], sems.at[i]))
        copies[-1].start()
    for copy in copies:
        copy.wait()


def f32(*shape):
    return jax.ShapeDtypeStruct(shape, jnp.float32)


def kernel_call(body, outs, scratch, flops, moved, **more):
    return pl.pallas_call(
        body,
        out_shape=outs,
        scratch_shapes=scratch,
        compiler_params=pltpu.CompilerParams(vmem_limit_bytes=16 * 1024 * 1024),
        cost_estimate=pl.CostEstimate(flops=flops, bytes_accessed=moved, transcendentals=0),
        **more,
    )


def swapped(buffers):
    planes = range(len(buffers))
    return [buffers[0]] + [
        lax.ppermute(buffer, "plane", [(i, i ^ step) for i in planes])
        for buffer, step in zip(buffers[1:], PARTNERS[1:])
    ]


def packed_shards(adjoint, metric, base_flow, edge_list, flips):
    comps, local, nodes, _, elements = adjoint.shape
    planes = MODES // local
    points = nodes * nodes * elements // planes
    rows_total = comps * local
    partitions = lax.axis_size("dom")
    state_shape = (nodes, rows_total, SLAB_TILES * LANES)

    layouts = [send_segments(chunk, points) for chunk in range(planes)]
    plans = [tile_plan(segments, SEND_TILES) for segments, _ in layouts]
    gaps = [gap for _, gap in layouts]
    back_plans = return_segments(points)
    to_span, to_modes = span_weights(planes)
    slab_bands = eta_bands(0, SLAB_TILES * LANES, nodes * elements)
    chunk_bands = np.stack(
        [eta_bands((points - 2 * nodes * elements) * b, CHUNK_TILES * LANES, points) for b in range(planes)]
    )

    in_hbm = pl.BlockSpec(memory_space=pltpu.HBM)
    sends = [f32(rows_total, SEND_TILES * LANES)] * planes
    send_scratch = [
        pltpu.VMEM(state_shape, jnp.float32),
        pltpu.VMEM((planes, rows_total, SEND_TILES * LANES), jnp.float32),
    ]
    row_copies = [
        pltpu.VMEM((comps, nodes, nodes, local, elements), jnp.float32),
        pltpu.SemaphoreType.DMA((nodes,)),
    ]
    in_rows = pltpu.with_memory_space_constraint(adjoint.transpose(0, 2, 3, 1, 4), pltpu.HBM)
    state, *outgoing = kernel_call(
        functools.partial(first_kernel, plans),
        [f32(*state_shape), *sends],
        send_scratch + row_copies,
        4 * 10**6,
        4 * 10**6,
        in_specs=[in_hbm],
    )(in_rows)
    whole, two_fields = (12, MODES, CHUNK_TILES * LANES), (2, MODES, CHUNK_TILES * LANES)
    lay = base_flow.transpose(1, 0, 2)
    flows = kernel_call(
        functools.partial(flow_kernel, points),
        [f32(*whole)] * STEPS,
        [pltpu.VMEM((2, STEPS, lay.shape[2] // LANES, LANES), jnp.float32)],
        4 * 10**6,
        9 * 10**6,
        grid=(6,),
        in_specs=[
            pl.BlockSpec((2, *lay.shape[1:]), lambda pair: (pair, 0, 0)),
            pl.BlockSpec(metric.shape, lambda pair: (0, 0)),
        ],
        out_specs=[pl.BlockSpec(two_fields, lambda pair: (pair, 0, 0))] * STEPS,
    )(lay, metric)
    table = kernel_call(
        tables_kernel,
        jax.ShapeDtypeStruct((24, LANES), jnp.int32),
        [pltpu.VMEM((LANES, LANES), jnp.float32)],
        10**5,
        10**5,
    )(edge_list.transpose(1, 0, 2), flips.transpose(1, 0, 2))

    for step_index in range(STEPS):
        fields = [
            kernel_call(
                functools.partial(fields_kernel, gaps),
                f32(3, comps, local, CHUNK_TILES * LANES),
                [],
                2 * 10**6,
                10**6,
            )(came, chunk_bands)
            for came in swapped(outgoing)
        ]
        returning = kernel_call(
            advect_kernel,
            [f32(GROUP, BACK_TILES * LANES)] * planes,
            [],
            80 * 10**6,
            5 * 10**6,
        )(*fields, flows[step_index], to_span, to_modes)
        local_sum = kernel_call(
            diffuse_kernel,
            f32(*state_shape),
            [pltpu.VMEM((nodes, GROUP, SLAB_TILES * LANES), jnp.float32)] * 2,
            12 * 10**6,
            2 * 10**6,
        )(state, metric, slab_bands)
        updated, own, *leaving = kernel_call(
            functools.partial(update_kernel, back_plans),
            [f32(*state_shape), f32(nodes, rows_total, LANES)] + [f32(rows_total, 2 * LANES)] * 4,
            [pltpu.VMEM((planes, GROUP, BACK_TILES * LANES), jnp.float32)],
            2 * 10**6,
            3 * 10**6,
        )(*swapped(returning), local_sum, table)
        traces = [
            lax.ppermute(
                buffer, "dom", [(i, trace_partner(i, matching, partitions)) for i in range(partitions)]
            )
            for matching, buffer in enumerate(leaving)
        ]
        if step_index + 1 < STEPS:
            state, *outgoing = kernel_call(
                functools.partial(next_kernel, plans),
                [f32(*state_shape), *sends],
                send_scratch,
                6 * 10**6,
                4 * 10**6,
            )(table, updated, own, *traces)
        else:
            result = kernel_call(
                last_kernel,
                f32(comps, nodes, nodes, local, elements),
                [pltpu.VMEM(state_shape, jnp.float32), *row_copies],
                2 * 10**6,
                3 * 10**6,
                out_specs=in_hbm,
            )(table, updated, own, *traces)
    return result.transpose(0, 3, 1, 2, 4)


def plain_shards(adjoint, metric, base_flow, edge_list, flips):
    local_modes = adjoint.shape[1]
    deriv_table = cheb_table(adjoint.shape[2])
    span_basis, span_slope, forward, wave_sq = span_tables(MODES)
    wave_local = lax.dynamic_slice_in_dim(
        wave_sq, lax.axis_index("plane") * local_modes, local_modes, 0
    )
    adjoint_state = adjoint
    for step_index in range(STEPS):
        base_now = base_flow[step_index].reshape(12, MODES, -1)
        adjoint_state = advance(
            adjoint_state,
            metric,
            base_now,
            edge_list[0],
            flips[0],
            deriv_table,
            span_basis,
            span_slope,
            forward,
            wave_local,
        )
    return adjoint_state


def shards(adjoint, metric, base_flow, edge_list, flips):
    if adjoint.shape[1:] == (MODES // 4, NODES, NODES, 32) and (
        edge_list.shape[1:] == (5, 24) and lax.axis_size("dom") % 4 == 0
    ):
        return packed_shards(adjoint, metric, base_flow, edge_list, flips)
    return plain_shards(adjoint, metric, base_flow, edge_list, flips)


def solution(mesh):
    placed = (
        P(None, "plane", None, None, "dom"),
        P(None, "dom"),
        P(None, None, ("dom", "plane")),
        P("dom", None, None),
        P("dom", None, None),
    )
    return jax.shard_map(
        shards,
        mesh=mesh,
        in_specs=placed,
        out_specs=P(None, "plane", None, None, "dom"),
        check_vma=False,
    )
```

```python
import functools

import jax
import jax.numpy as jnp
import numpy as np
from jax import lax
from jax.experimental import pallas as pl
from jax.experimental.pallas import tpu as pltpu
from jax.sharding import PartitionSpec as P

MODES = 64
STEPS = 2


step_size = 0.01
viscosity = 0.02


def passed_along(shard, axis, by):
    size = lax.axis_size(axis)
    return lax.ppermute(shard, axis, [(i, (i + by) % size) for i in range(size)])


def cheb_table(node_count):
    order = node_count - 1
    node_ids = jnp.arange(node_count, dtype=jnp.int32)
    node_coords = -jnp.cos(jnp.pi * node_ids.astype(jnp.float32) / order)
    weight = jnp.where((node_ids == 0) | (node_ids == order), 2.0, 1.0).astype(jnp.float32)
    parity = jnp.where((node_ids[:, None] + node_ids[None, :]) % 2 == 0, 1.0, -1.0).astype(
        jnp.float32
    )
    on_diag = node_ids[:, None] == node_ids[None, :]
    differ = jnp.where(on_diag, 1.0, node_coords[:, None] - node_coords[None, :])
    off_diag = jnp.where(on_diag, 0.0, weight[:, None] / weight[None, :] * parity / differ)
    return off_diag - jnp.diag(jnp.sum(off_diag, axis=1))


def span_tables(modes):
    mode_ids = jnp.arange(modes, dtype=jnp.int32)
    wavenumber = (mode_ids + 1) // 2
    is_cosine = (mode_ids % 2 == 1) | (mode_ids == 0)
    span_ids = jnp.arange(modes, dtype=jnp.int32)
    phase_num = span_ids[:, None] * wavenumber[None, :] % modes
    angles = 2.0 * jnp.pi * phase_num.astype(jnp.float32) / modes
    cosines = jnp.cos(angles)
    sines = jnp.sin(angles)
    wave_f = wavenumber.astype(jnp.float32)
    span_basis = jnp.where(is_cosine[None, :], cosines, sines)
    span_slope = jnp.where(is_cosine[None, :], -wave_f[None, :] * sines, wave_f[None, :] * cosines)
    scaling = jnp.where((mode_ids == 0) | (mode_ids == modes - 1), 1.0 / modes, 2.0 / modes).astype(
        jnp.float32
    )
    forward = span_basis.T * scaling[:, None]
    return (span_basis, span_slope, forward, wave_f * wave_f)


def directional(field_data, metric, deriv_table, xi_row, eta_row):
    along_xi = jnp.einsum(
        "ai,cmije->cmaje", deriv_table, field_data, precision=lax.Precision.HIGHEST
    )
    along_eta = jnp.einsum(
        "bj,cmije->cmibe", deriv_table, field_data, precision=lax.Precision.HIGHEST
    )
    return metric[xi_row] * along_xi + metric[eta_row] * along_eta


def advect(coeffs, base_now, span_basis, span_slope, forward):
    values = jnp.einsum("nm,fmq->fnq", span_basis, coeffs, precision=lax.Precision.HIGHEST)
    along_z = jnp.einsum("nm,cmq->cnq", span_slope, coeffs[0:3], precision=lax.Precision.HIGHEST)
    products = []
    for comp in range(3):
        term = (
            base_now[0] * values[3 + comp]
            + base_now[1] * values[6 + comp]
            + base_now[2] * along_z[comp]
        )
        term = term - (
            values[0] * base_now[3 + comp]
            + values[1] * base_now[6 + comp]
            + values[2] * base_now[9 + comp]
        )
        products.append(term)
    return jnp.einsum("mn,cnq->cmq", forward, jnp.stack(products), precision=lax.Precision.HIGHEST)


def accumulate(field_data, edge_sums, counts):
    node_count = field_data.shape[2]
    last = node_count - 1
    total = field_data
    total = total.at[:, :, :, 0, :].add(edge_sums[:, :, :, 0, :])
    total = total.at[:, :, last, :, :].add(edge_sums[:, :, :, 1, :])
    total = total.at[:, :, :, last, :].add(edge_sums[:, :, :, 2, :])
    total = total.at[:, :, 0, :, :].add(edge_sums[:, :, :, 3, :])
    weight = jnp.ones((node_count, node_count, field_data.shape[4]), jnp.float32)
    weight = weight.at[:, 0, :].add(counts[0][None, :])
    weight = weight.at[last, :, :].add(counts[1][None, :])
    weight = weight.at[:, last, :].add(counts[2][None, :])
    weight = weight.at[0, :, :].add(counts[3][None, :])
    return total / weight


def assemble(field_data, edge_slots, flip_flags):
    components, local_modes, node_count, _, elements = field_data.shape
    last = node_count - 1
    row_count = components * local_modes * node_count
    traces = jnp.stack(
        [
            field_data[:, :, :, 0, :],
            field_data[:, :, last, :, :],
            field_data[:, :, :, last, :],
            field_data[:, :, 0, :, :],
        ],
        axis=3,
    )
    edge_table = traces.reshape(row_count, 4 * elements)
    blocks, capacity = edge_slots.shape
    half_span = (blocks - 1) // 2
    slot_edges = edge_slots.reshape(-1)
    occupied = (slot_edges >= 0).astype(jnp.float32)
    outgoing = jnp.take(edge_table, jnp.maximum(slot_edges, 0), axis=1) * occupied[None, :]

    def block_of(block_id):
        return outgoing[:, block_id * capacity : (block_id + 1) * capacity]

    own_pairs = (
        block_of(half_span)
        .reshape(row_count, capacity // 2, 2)[:, :, ::-1]
        .reshape(row_count, capacity)
    )
    received = {half_span: own_pairs}
    for block_id in range(blocks):
        if block_id != half_span:
            received[block_id] = passed_along(
                block_of(blocks - 1 - block_id), "dom", half_span - block_id
            )
    partners = jnp.concatenate([received[block_id] for block_id in range(blocks)], axis=1)
    shaped = partners.reshape(components * local_modes, node_count, blocks * capacity)
    shaped = (
        jnp.where(flip_flags.reshape(-1)[None, None, :] == 1, shaped[:, ::-1, :], shaped)
        * occupied[None, None, :]
    )
    onehot = (slot_edges[:, None] == jnp.arange(4 * elements, dtype=jnp.int32)[None, :]).astype(
        jnp.float32
    )
    edge_sums = jnp.dot(
        shaped.reshape(row_count, blocks * capacity), onehot, precision=lax.Precision.HIGHEST
    )
    edge_sums = edge_sums.reshape(components, local_modes, node_count, 4, elements)
    counts = jnp.sum(onehot, axis=0).reshape(4, elements)
    return accumulate(field_data, edge_sums, counts)


def advance(
    adjoint_state,
    metric,
    base_now,
    edge_slots,
    flip_flags,
    deriv_table,
    span_basis,
    span_slope,
    forward,
    wave_local,
):
    components, local_modes, node_count, _, elements = adjoint_state.shape
    points = node_count * node_count * elements
    grad_x = directional(adjoint_state, metric, deriv_table, 0, 2)
    grad_y = directional(adjoint_state, metric, deriv_table, 1, 3)
    stacked = jnp.concatenate([adjoint_state, grad_x, grad_y], axis=0).reshape(
        9, local_modes, points
    )
    gathered = lax.all_to_all(stacked, "plane", split_axis=2, concat_axis=1, tiled=True)
    advective = advect(gathered, base_now, span_basis, span_slope, forward)
    returned = lax.all_to_all(advective, "plane", split_axis=1, concat_axis=2, tiled=True).reshape(
        adjoint_state.shape
    )
    laplacian = directional(grad_x, metric, deriv_table, 0, 2) + directional(
        grad_y, metric, deriv_table, 1, 3
    )
    updated = adjoint_state + step_size * (
        returned + viscosity * (laplacian - wave_local[None, :, None, None, None] * adjoint_state)
    )
    return assemble(updated, edge_slots, flip_flags)


NODES = 9
LANES = 128
SLAB_TILES = 3
STATE_TILES = 7
SEND_TILES = 12
CHUNK_TILES = 6
BODY_TILES = 5
BACK_TILES = 31
GROUP = 8
PARTNERS = (0, 2, 1, 3)
STEP_VISC = step_size * viscosity


def cheb_numbers():
    order = NODES - 1
    coords = -np.cos(np.pi * np.arange(NODES) / order)
    weight = np.ones(NODES)
    weight[0] = weight[-1] = 2.0
    table = np.zeros((NODES, NODES))
    for a in range(NODES):
        for i in range(NODES):
            if a != i:
                table[a, i] = weight[a] / weight[i] * (-1.0) ** (a + i) / (coords[a] - coords[i])
    return table - np.diag(table.sum(axis=1))


DERIV = cheb_numbers()


def span_numbers():
    modes = np.arange(MODES)
    wave = (modes + 1) // 2
    is_cosine = (modes % 2 == 1) | (modes == 0)
    angles = 2.0 * np.pi * (np.arange(MODES)[:, None] * wave[None, :] % MODES) / MODES
    cosines, sines = np.cos(angles), np.sin(angles)
    basis = np.where(is_cosine, cosines, sines)
    slope = np.where(is_cosine, -wave * sines, wave * cosines)
    scaling = np.where((modes == 0) | (modes == MODES - 1), 1.0 / MODES, 2.0 / MODES)
    return basis, slope, basis.T * scaling[:, None]


def in_two(table):
    table = table.astype(np.float32)
    high = table.astype(jnp.bfloat16)
    low = (table - high.astype(np.float32)).astype(jnp.bfloat16)
    return high, low


def span_weights(planes):
    basis, slope, forward = span_numbers()
    local = MODES // planes
    to_span, to_modes = [], []
    for me in range(planes):
        came = np.concatenate([(me ^ step) * local + np.arange(local) for step in PARTNERS])
        high, low = in_two(np.concatenate([basis, slope])[:, came])
        to_span.append(np.concatenate([high, high, low], axis=1))
        high, low = in_two(forward[came])
        to_modes.append(np.concatenate([high, high, low], axis=1))
    return np.stack(to_span), np.stack(to_modes)


def eta_bands(first_lane, lanes, count):
    bands = np.zeros((24, lanes), np.float32)
    for lane in range(count):
        j = (first_lane + lane) % 288 // 32
        for d in range(-8, 9):
            if 0 <= j + d < NODES:
                bands[d + 8, lane] = DERIV[j, j + d]
    return bands


def tile_plan(segments, tiles):
    plan = [[] for _ in range(tiles)]
    for source, src, dst, length in segments:
        done = 0
        while done < length:
            s, d = src + done, dst + done
            size = min(length - done, LANES - s % LANES, LANES - d % LANES)
            plan[d // LANES].append((source, s // LANES, (d - s) % LANES, d % LANES, size))
            done += size
    return plan


def send_segments(chunk, points):
    ring, slab = STATE_TILES * LANES, NODES * 32
    turned = (points - 2 * slab) * chunk
    segments = []
    for r in range(3):
        start = (r * slab - turned) % ring
        first = min(slab, ring - start)
        segments.append((("state", 2 * chunk + r), 0, start, first))
        if first < slab:
            segments.append((("state", 2 * chunk + r), first, 0, slab - first))
    gap = (3 * slab - turned) % ring
    body = (points // LANES) * LANES
    lane = points * chunk
    for lane in range(points * chunk, points * (chunk + 1), 8):
        at = lane - points * chunk
        target = ring + at if at < body else gap + at - body
        source = ("xi", lane // slab)
        if segments[-1][0] == source and segments[-1][1] + segments[-1][3] == lane % slab and (
            segments[-1][2] + segments[-1][3] == target
        ):
            segments[-1] = (source, segments[-1][1], segments[-1][2], segments[-1][3] + 8)
        else:
            segments.append((source, lane % slab, target, 8))
    return segments, gap


def return_segments(points):
    slab = NODES * 32
    body = points // LANES * LANES
    plans = []
    for i in range(NODES):
        segments = []
        for chunk in range(4):
            for name, start, stop in (("body", 0, body), ("tail", body, points)):
                low = max(i * slab, chunk * points + start)
                high = min((i + 1) * slab, chunk * points + stop)
                if low < high:
                    segments.append(((name, chunk), low - chunk * points - start, low - i * slab, high - low))
        plans.append(tile_plan(segments, SLAB_TILES))
    return plans


def lane_ids(rows):
    return lax.broadcasted_iota(jnp.int32, (rows, LANES), 1)


def turn(value, shift):
    return value if shift % LANES == 0 else pltpu.roll(value, shift % LANES, 1)


def turner(load):
    made = {}

    def turned(source, tile, shift):
        key = source, tile, shift
        if key not in made:
            made[key] = turn(load(source, tile), shift)
        return made[key]

    return turned


def pieced(pieces, turned, lanes):
    total = None
    for source, tile, shift, low, size in pieces:
        value = turned(source, tile, shift)
        if total is None:
            total = value
        elif low + size == LANES:
            total = jnp.where(lanes >= low, value, total)
        else:
            total = jnp.where((lanes >= low) & (lanes < low + size), value, total)
    return total


def aligned(index, unit):
    return index if isinstance(index, int) else pl.multiple_of(index, unit)


def group_rows(g):
    return pl.ds(aligned(g * GROUP, GROUP), GROUP)


def tile_at(ref, lead, rows, tile):
    return ref[(*lead, rows, pl.ds(tile * LANES, LANES))]


def along_i(tiles):
    return [
        sum(tiles[i] * float(DERIV[a, i]) for i in range(1, NODES)) + tiles[0] * float(DERIV[a, 0])
        for a in range(NODES)
    ]


def turned_tiles(tiles, lanes):
    out = [tiles]
    for s in range(1, 4):
        spun = [pltpu.roll(t, LANES - 32 * s, 1) for t in tiles]
        out.append(
            [
                jnp.where(lanes < LANES - 32 * s, spun[t], spun[(t + 1) % len(tiles)])
                for t in range(len(tiles))
            ]
        )
    return out


def along_j(turned, ring, tile, band, used):
    total = None
    for d in used:
        term = turned[d % 4][(tile + d // 4) % ring] * band(d)
        total = term if total is None else total + term
    return total


def make_xi(groups, state, xi):
    for g in groups:
        rows = group_rows(g)
        for t in range(SLAB_TILES):
            for a, value in enumerate(along_i([tile_at(state, (i,), rows, t) for i in range(NODES)])):
                xi[a, rows, pl.ds(t * LANES, LANES)] = value


def make_buffer(plan, groups, state, xi, put):
    lanes = lane_ids(GROUP)
    for g in groups:
        rows = group_rows(g)

        def load(source, tile, rows=rows):
            return tile_at(state if source[0] == "state" else xi, (source[1],), rows, tile)

        turned = turner(load)
        for t, pieces in enumerate(plan):
            put(rows, pl.ds(t * LANES, LANES), pieced(pieces, turned, lanes))


def make_first(plans, state, xi, out):
    target = lax.axis_index("plane") ^ PARTNERS[1]

    def put(rows, at, value):
        out[rows, at] = value

    for chunk, plan in enumerate(plans):
        pl.when(target == chunk)(
            functools.partial(make_buffer, plan, range(state.shape[1] // GROUP), state, xi, put)
        )


def rest_kernel(plans, state, xi, out0, out2, out3, staged):
    me = lax.axis_index("plane")
    for chunk, plan in enumerate(plans):

        def put(rows, at, value, chunk=chunk):
            staged[chunk, rows, at] = value

        make_buffer(plan, range(state.shape[1] // GROUP), state, xi, put)
    for k, out in ((0, out0), (2, out2), (3, out3)):
        out[...] = staged[me ^ PARTNERS[k]]


def first_kernel(plans, adjoint, state, xi, out, taken, sems):
    comps, local = taken.shape[0], taken.shape[3]

    def copy(c):
        return pltpu.make_async_copy(adjoint.at[c], taken.at[c], sems.at[c])

    for c in range(comps):
        copy(c).start()

    for c in range(comps):
        copy(c).wait()
        rows = pl.ds(c * local, local)
        for i in range(NODES):
            for t in range(SLAB_TILES):
                parts = [taken[c, i, j] for j in range(4 * t, min(4 * t + 4, NODES))]
                parts += [jnp.zeros_like(parts[0])] * (4 - len(parts))
                state[i, rows, pl.ds(t * LANES, LANES)] = jnp.concatenate(parts, axis=1)
        make_xi(range(c * local // GROUP, (c + 1) * local // GROUP), state, xi)
    make_first(plans, state, xi, out)


def metric_rows(metric):
    wide = jnp.concatenate([metric[...]] * (LANES // metric.shape[1]), axis=1)
    return jnp.concatenate([wide, wide], axis=0)


def flow_kernel(points, flow, metric, out0, out1, flat):
    me = lax.axis_index("plane")
    lanes, subs = lane_ids(8), lax.broadcasted_iota(jnp.int32, (8, LANES), 0)
    shift = lax.rem(LANES - lax.rem(me * points, LANES), LANES)
    turned = pltpu.roll(metric_rows(metric), shift, 1)
    ahead = pl.program_id(0) == 0
    first_first = jnp.where(ahead, turned[0:1], 1.0)
    first_second = jnp.where(ahead, turned[1:2], 0.0)
    second_first = jnp.where(ahead, turned[2:3], 0.0)
    second_second = jnp.where(ahead, turned[3:4], 1.0)
    per_sixteen = 16 * points // LANES
    last = CHUNK_TILES - 1

    for f in range(2):
        for s in range(STEPS):
            flat[f, s] = flow[f, s].reshape(flat.shape[2:])

    for s, out in enumerate((out0, out1)):
        for half in range(2):
            moved = (lanes + 64 * half + 8 * subs) & (LANES - 1)
            kept = lanes < LANES - 64 * half - 8 * subs

            def some_rows(h, _, s=s, half=half, out=out, moved=moved, kept=kept):
                rows = pl.ds(pl.multiple_of(16 * h + 8 * half, 8), 8)

                def field(f):
                    spun = []
                    for k in range(CHUNK_TILES):
                        start = per_sixteen * h + 40 * half + k
                        spun.append(pick(flat[f, s, pl.ds(start, 8, stride=5), :], moved))
                    return [jnp.where(kept, spun[k], spun[k + 1]) for k in range(last)] + [spun[last]]

                for t, (one, two) in enumerate(zip(field(0), field(1))):
                    out[0, rows, pl.ds(t * LANES, LANES)] = one * first_first + two * first_second
                    out[1, rows, pl.ds(t * LANES, LANES)] = one * second_first + two * second_second
                return 0

            lax.fori_loop(0, MODES // 16, some_rows, 0)


def tables_kernel(edges, flags, table, square):
    blocks, _, capacity = edges.shape
    lanes = lane_ids(capacity)
    slots = lax.broadcasted_iota(jnp.int32, (capacity, LANES), 0)
    here = slots == lax.rem(lanes, capacity)
    flag = jnp.zeros((1, LANES), jnp.int32)
    count = jnp.zeros((1, LANES), jnp.int32)
    table[...] = jnp.zeros(table.shape, jnp.int32)
    square[...] = jnp.zeros(square.shape, jnp.float32)
    for o in range(blocks):
        square[o : o + 1, 0:capacity] = edges[o].astype(jnp.float32)
        square[blocks + o : blocks + o + 1, 0:capacity] = flags[o].astype(jnp.float32)
    columns = square[...].T[0:capacity].astype(jnp.int32)
    for o in range(blocks):
        column = jnp.broadcast_to(columns[:, o : o + 1], (capacity, LANES))
        held = column == lanes

        def summed(mask, value):
            return jnp.sum(jnp.where(mask, value, 0), axis=0, keepdims=True)

        table[o : o + 1, :] = summed(here, jnp.maximum(column, 0))
        table[5 + o : 6 + o, :] = summed(held, slots)
        present = summed(held, jnp.ones_like(slots))
        table[10 + o : 11 + o, :] = present
        flag += summed(held, jnp.broadcast_to(columns[:, blocks + o : blocks + o + 1], (capacity, LANES)))
        count += present
        if o == blocks // 2:
            partner = slots + 1 - 2 * lax.rem(slots, 2)
            slot_of = jnp.broadcast_to(summed(held, partner), (capacity, LANES))
            partner_edge = summed(slots == slot_of, jnp.maximum(column, 0))
            table[16:17, :] = jnp.where(present > 0, partner_edge, 0)
    table[15:16, :] = flag
    table[17:18, :] = count


def diffuse_kernel(state, metric, bands, local_sum, first, second):
    me = lax.axis_index("plane")
    rows_total = state.shape[1]
    lanes = lane_ids(8)
    local = rows_total // 3
    wide = metric_rows(metric)
    xi_x, xi_y, eta_x, eta_y = (wide[r : r + 1] for r in range(4))
    g_ii = xi_x * xi_x + xi_y * xi_y
    g_ij = xi_x * eta_x + xi_y * eta_y
    g_jj = eta_x * eta_x + eta_y * eta_y
    used = [[d for d in range(-8, 9) if any(0 <= j + d < NODES for j in range(4 * t, min(4 * t + 4, NODES)))]
            for t in range(SLAB_TILES)]

    def eta_of(tiles):
        turned = turned_tiles(tiles, lanes)
        return [
            along_j(turned, SLAB_TILES, t, lambda d, t=t: tile_at(bands, (), pl.ds(d + 8, 1), t), used[t])
            for t in range(SLAB_TILES)
        ]

    def some_rows(g, _):
        rows = pl.ds(pl.multiple_of(g * 8, 8), 8)
        first_mode = me * local + lax.rem(g * 8, local)
        wave = ((first_mode + lax.broadcasted_iota(jnp.int32, (8, LANES), 0) + 1) // 2).astype(jnp.float32)
        wave_sq = wave * wave
        for t in range(SLAB_TILES):
            for a, value in enumerate(along_i([tile_at(state, (i,), rows, t) for i in range(NODES)])):
                first[a, :, pl.ds(t * LANES, LANES)] = value
        for i in range(NODES):
            eta = eta_of([tile_at(state, (i,), rows, t) for t in range(SLAB_TILES)])
            mixed = []
            for t in range(SLAB_TILES):
                xi = first[i, :, pl.ds(t * LANES, LANES)]
                first[i, :, pl.ds(t * LANES, LANES)] = g_ii * xi + g_ij * eta[t]
                mixed.append(g_ij * xi + g_jj * eta[t])
            for t, value in enumerate(eta_of(mixed)):
                second[i, :, pl.ds(t * LANES, LANES)] = value
        for t in range(SLAB_TILES):
            tiles = [first[i, :, pl.ds(t * LANES, LANES)] for i in range(NODES)]
            for a, value in enumerate(along_i(tiles)):
                now = tile_at(state, (a,), rows, t)
                laplacian = value + second[a, :, pl.ds(t * LANES, LANES)]
                local_sum[a, rows, pl.ds(t * LANES, LANES)] = now + STEP_VISC * (laplacian - wave_sq * now)
        return 0

    lax.fori_loop(0, rows_total // 8, some_rows, 0)


def halves(value):
    high = value.astype(jnp.bfloat16)
    return high, (value - high.astype(jnp.float32)).astype(jnp.bfloat16)


def fields_kernel(gaps, source, bands, *refs):
    fields = refs[-1]
    me = lax.axis_index("plane")
    rows_total = source.shape[0]
    local = fields.shape[2]
    lanes = lane_ids(GROUP)
    gap = sum(jnp.where(me == b, g, 0) for b, g in enumerate(gaps))
    gap_tile, gap_lane = gap // LANES, lax.rem(gap, LANES)

    for g in range(rows_total // GROUP):
        rows = group_rows(g)
        c = g * GROUP // local
        target = pl.ds(g * GROUP % local, GROUP)
        tiles = [tile_at(source, (), rows, t) for t in range(STATE_TILES)]
        turned = turned_tiles(tiles, lanes)
        for t in range(CHUNK_TILES):
            at = pl.ds(t * LANES, LANES)
            fields[0, c, target, at] = tiles[t]
            fields[2, c, target, at] = along_j(
                turned, STATE_TILES, t, lambda d, at=at: bands[me, pl.ds(d + 8, 1), at], range(-8, 9)
            )
        for t in range(BODY_TILES):
            fields[1, c, target, pl.ds(t * LANES, LANES)] = tile_at(source, (), rows, STATE_TILES + t)
        tail = source[rows, pl.ds(pl.multiple_of(gap_tile * LANES, LANES), LANES)]
        fields[1, c, target, pl.ds(BODY_TILES * LANES, LANES)] = pltpu.roll(
            tail, lax.rem(LANES - gap_lane, LANES), 1
        )


def advect_kernel(fields0, fields1, fields2, fields3, flow, to_span, to_modes, *outs):
    me = lax.axis_index("plane")
    comps = fields0.shape[1]
    both = to_span[me]
    basis = both[:MODES]
    back = to_modes[me]
    width = 2 * LANES
    chunks = CHUNK_TILES * LANES // width
    lanes = lane_ids(GROUP)

    def dot(a, value):
        high, low = halves(value)
        stacked = jnp.concatenate([high, low, high], axis=0)
        return jnp.dot(a, stacked, preferred_element_type=jnp.float32)

    def results(part):
        def field(kind, c):
            return jnp.concatenate(
                [fields[kind, c, :, part] for fields in (fields0, fields1, fields2, fields3)], axis=0
            )

        values, sums = [], []
        for c in range(comps):
            out = dot(both, field(0, c))
            values.append(out[:MODES])
            along_x = flow[0, :, part] * dot(basis, field(1, c))
            along_y = flow[1, :, part] * dot(basis, field(2, c))
            sums.append(along_x + along_y + flow[2, :, part] * out[MODES:])
        for c in range(comps):
            taken = values[0] * flow[3 + c, :, part]
            taken += values[1] * flow[6 + c, :, part]
            taken += values[2] * flow[9 + c, :, part]
            yield c, dot(back, sums[c] - taken)

    def split(c, result):
        for k, out in enumerate(outs):
            for half in range(MODES // len(outs) // GROUP):
                first = k * (MODES // len(outs)) + half * GROUP
                yield k, out, c * (MODES // len(outs) // GROUP) + half, result[first : first + GROUP]

    for first in range(0, (chunks - 1) * width, width):
        for c, result in results(pl.ds(first, width)):
            for _, out, g, piece in split(c, result):
                out[:, pl.ds(BODY_TILES * g * LANES + first, width)] = piece
    tails = [None] * len(outs)
    for c, result in results(pl.ds((chunks - 1) * width, width)):
        for k, out, g, piece in split(c, result):
            out[:, pl.ds((BODY_TILES * (g + 1) - 1) * LANES, LANES)] = piece[:, :LANES]
            tail = turn(piece[:, LANES:], 8 * g)
            tails[k] = tail if g == 0 else jnp.where(lanes >= 8 * g, tail, tails[k])
    for out, tail in zip(outs, tails):
        out[:, pl.ds((BACK_TILES - 1) * LANES, LANES)] = tail


def trace_blocks(me):
    odd, late = lax.rem(me, 2), lax.rem(me, 4) // 2
    return 4 * late, 1 + 2 * odd, 4 - 4 * late, 3 - 2 * odd


def trace_partner(me, matching, size):
    step, start = ((2, 2), (1, 1), (2, 0), (1, 0))[matching]
    return (((me + start) ^ step) - start) % size


def update_kernel(plans, in0, in1, in2, in3, local_sum, table, updated, own, out0, out1, out2, out3, chunks, traces):
    me = lax.axis_index("plane")
    rows_total = local_sum.shape[1]
    last = NODES - 1
    lanes = lane_ids(8)
    for step, source in zip(PARTNERS, (in0, in1, in2, in3)):
        chunks[me ^ step] = source[...]

    trace_plans = [
        tile_plan([(k, 0, 0, 32), (last, 32 * k, 32, 32), (k, 256, 64, 32), (0, 32 * k, 96, 32)], 1)[0]
        for k in range(NODES)
    ]

    blocks = trace_blocks(lax.axis_index("dom"))

    def wide(row):
        return jnp.broadcast_to(table[pl.ds(row, 1), :], (8, LANES))

    turned_round, partner = wide(15) == 1, wide(16)
    slot_edges = [wide(o) for o in blocks]
    groups = range(rows_total // GROUP)
    for g in groups:
        rows = group_rows(g)

        def load(source, tile, g=g):
            if source[0] == "tail":
                return turn(tile_at(chunks, (source[1],), slice(None), BACK_TILES - 1), -8 * g)
            return tile_at(chunks, (source[1],), slice(None), BODY_TILES * g + tile)

        turned = turner(load)
        for i in range(NODES):
            for t in range(SLAB_TILES):
                value = pieced(plans[i][t], turned, lanes)
                updated[i, rows, pl.ds(t * LANES, LANES)] = (
                    tile_at(local_sum, (i,), rows, t) + step_size * value
                )
    for g in groups:
        rows = group_rows(g)
        edges = turner(lambda i, tile, rows=rows: tile_at(updated, (i,), rows, tile))
        raw = [pieced(plan, edges, lanes) for plan in trace_plans]
        for k in range(NODES):
            traces[k, rows, :] = jnp.where(turned_round, raw[last - k], raw[k])
    for g in groups:
        rows = group_rows(g)
        for slot_edge, out in zip(slot_edges, (out0, out1, out2, out3)):
            for t in range(2):
                total = None
                for k in range(5 * t, min(5 * t + 5, NODES)):
                    value = pick(traces[k, rows, :], slot_edge)
                    total = value if total is None else jnp.where(lanes >= 24 * (k - 5 * t), value, total)
                out[rows, pl.ds(t * LANES, LANES)] = total
        for k in range(NODES):
            own[k, rows, :] = pick(traces[k, rows, :], partner)


def pick(value, index):
    return jnp.take_along_axis(value, index, axis=1, mode="promise_in_bounds")


def join_edges(table, updated, own, came, sums, put):
    rows_total = updated.shape[1]
    last = NODES - 1
    lanes = lane_ids(8)
    blocks = trace_blocks(lax.axis_index("dom"))

    def wide(row):
        return jnp.broadcast_to(table[pl.ds(row, 1), :], (8, LANES))

    share = wide(17).astype(jnp.float32)
    quarter = lanes // 32
    own_has = wide(12) > 0
    has = [wide(10 + o) > 0 for o in blocks]
    slots = [wide(5 + o) for o in blocks]

    def spread(values, at, t):
        value = None
        for k in range(4 * t, min(4 * t + 4, NODES)):
            moved = turn(values[k], 32 * (k - 4 * t - at))
            value = jnp.where(quarter == k - 4 * t, moved, 0.0 if value is None else value)
        return value

    def edge_parts(values, i, t):
        parts = []
        if t == 0:
            parts.append(jnp.where(quarter == 0, values[i], 0.0))
        if i == last:
            parts.append(spread(values, 1, t))
        if t == 2:
            parts.append(jnp.where(quarter == 0, turn(values[i], -64), 0.0))
        if i == 0:
            parts.append(spread(values, 3, t))
        return parts

    shares, scale = [share] * NODES, {}
    for i in (0, 1, last):
        for t in range(SLAB_TILES):
            parts = edge_parts(shares, i, t)
            if parts:
                scale[i, t] = 1.0 / (1.0 + sum(parts[1:], parts[0]))

    groups = range(rows_total // GROUP)
    for g in groups:
        rows = group_rows(g)
        for k in range(NODES):
            total = jnp.where(own_has, own[k, rows, :], 0.0)
            for slot, there, source in zip(slots, has, came):
                value = pick(tile_at(source, (), rows, k // 5), slot + 24 * (k % 5))
                total = jnp.where(there, value, total)
            sums[k, rows, :] = total
    for g in groups:
        rows = group_rows(g)
        values = [sums[k, rows, :] for k in range(NODES)]
        for i in range(NODES):
            for t in range(SLAB_TILES):
                parts = edge_parts(values, i, t)
                if parts:
                    total = tile_at(updated, (i,), rows, t)
                    for part in parts:
                        total += part
                    put(g, i, t, total * scale[i if i in (0, last) else 1, t])


def next_kernel(plans, table, updated, own, r0, r1, r2, r3, state, xi, out, sums):
    def put(g, i, t, value):
        state[i, group_rows(g), pl.ds(t * LANES, LANES)] = value

    for i in range(1, NODES - 1):
        state[i, :, pl.ds(LANES, LANES)] = updated[i, :, pl.ds(LANES, LANES)]
    join_edges(table, updated, own, (r0, r1, r2, r3), sums, put)
    make_xi(range(updated.shape[1] // GROUP), state, xi)
    make_first(plans, state, xi, out)


def inner_kernel(updated, out, given, sems):
    comps, local, elements = given.shape[0], given.shape[3], given.shape[4]
    inner = pl.ds(1, NODES - 2)
    copies = []
    for i in range(1, NODES - 1):
        for c in range(comps):
            rows = pl.ds(c * local, local)
            for j in range(1, NODES - 1):
                tile = tile_at(updated, (i,), rows, j // 4)
                given[c, i, j] = turn(tile, -32 * (j % 4))[:, :elements]
        copies.append(pltpu.make_async_copy(given.at[:, i, inner], out.at[:, i, inner], sems.at[i]))
        copies[-1].start()
    for copy in copies:
        copy.wait()


def last_kernel(table, updated, own, r0, r1, r2, r3, _, out, given, sums, sems):
    local, elements = given.shape[3], given.shape[4]
    last = NODES - 1

    def put(g, i, t, value):
        c, rows = g * GROUP // local, pl.ds(g * GROUP % local, GROUP)
        for j in range(4 * t, min(4 * t + 4, NODES)):
            if i in (0, last) or j in (0, last):
                given[c, i, j, rows, :] = turn(value, -32 * (j % 4))[:, :elements]

    join_edges(table, updated, own, (r0, r1, r2, r3), sums, put)
    inner = pl.ds(1, NODES - 2)
    places = [(slice(None), 0), (slice(None), last), (slice(None), inner, 0), (slice(None), inner, last)]
    copies = [
        pltpu.make_async_copy(given.at[place], out.at[place], sems.at[n]) for n, place in enumerate(places)
    ]
    for copy in copies:
        copy.start()
    for copy in copies:
        copy.wait()


def f32(*shape):
    return jax.ShapeDtypeStruct(shape, jnp.float32)


def kernel_call(body, outs, scratch, flops, moved, **more):
    return pl.pallas_call(
        body,
        out_shape=outs,
        scratch_shapes=scratch,
        compiler_params=pltpu.CompilerParams(vmem_limit_bytes=16 * 1024 * 1024),
        cost_estimate=pl.CostEstimate(flops=flops, bytes_accessed=moved, transcendentals=0),
        **more,
    )


def swapped(buffers):
    planes = range(len(buffers))
    return [buffers[0]] + [
        lax.ppermute(buffer, "plane", [(i, i ^ step) for i in planes])
        for buffer, step in zip(buffers[1:], PARTNERS[1:])
    ]


def packed_shards(adjoint, metric, base_flow, edge_list, flips):
    comps, local, nodes, _, elements = adjoint.shape
    planes = MODES // local
    points = nodes * nodes * elements // planes
    rows_total = comps * local
    partitions = lax.axis_size("dom")
    state_shape = (nodes, rows_total, SLAB_TILES * LANES)

    layouts = [send_segments(chunk, points) for chunk in range(planes)]
    plans = [tile_plan(segments, SEND_TILES) for segments, _ in layouts]
    gaps = [gap for _, gap in layouts]
    back_plans = return_segments(points)
    to_span, to_modes = span_weights(planes)
    slab_bands = eta_bands(0, SLAB_TILES * LANES, nodes * elements)
    chunk_bands = np.stack(
        [eta_bands((points - 2 * nodes * elements) * b, CHUNK_TILES * LANES, points) for b in range(planes)]
    )

    in_hbm, vmem = (pl.BlockSpec(memory_space=space) for space in (pltpu.HBM, pltpu.VMEM))
    buffer = f32(rows_total, SEND_TILES * LANES)
    row_copies = [
        pltpu.VMEM((comps, nodes, nodes, local, elements), jnp.float32),
        pltpu.SemaphoreType.DMA((nodes,)),
    ]
    edge_scratch = pltpu.VMEM((nodes, rows_total, LANES), jnp.float32)

    def with_rest(state, xi, first):
        own, *others = kernel_call(
            functools.partial(rest_kernel, plans),
            [buffer] * (planes - 1),
            [pltpu.VMEM((planes, *buffer.shape), jnp.float32)],
            10**6,
            2 * 10**6,
        )(state, xi)
        return [own, first, *others]

    in_rows = pltpu.with_memory_space_constraint(adjoint.transpose(0, 2, 3, 1, 4), pltpu.HBM)
    state, xi, first = kernel_call(
        functools.partial(first_kernel, plans),
        [f32(*state_shape), f32(*state_shape), buffer],
        row_copies,
        4 * 10**6,
        4 * 10**6,
        in_specs=[in_hbm],
    )(in_rows)
    outgoing = with_rest(state, xi, first)
    whole, two_fields = (12, MODES, CHUNK_TILES * LANES), (2, MODES, CHUNK_TILES * LANES)
    lay = base_flow.transpose(1, 0, 2)
    flows = kernel_call(
        functools.partial(flow_kernel, points),
        [f32(*whole)] * STEPS,
        [pltpu.VMEM((2, STEPS, lay.shape[2] // LANES, LANES), jnp.float32)],
        4 * 10**6,
        9 * 10**6,
        grid=(6,),
        in_specs=[
            pl.BlockSpec((2, *lay.shape[1:]), lambda pair: (pair, 0, 0)),
            pl.BlockSpec(metric.shape, lambda pair: (0, 0)),
        ],
        out_specs=[pl.BlockSpec(two_fields, lambda pair: (pair, 0, 0))] * STEPS,
    )(lay, metric)
    table = kernel_call(
        tables_kernel,
        jax.ShapeDtypeStruct((24, LANES), jnp.int32),
        [pltpu.VMEM((LANES, LANES), jnp.float32)],
        10**5,
        10**5,
    )(edge_list.transpose(1, 0, 2), flips.transpose(1, 0, 2))

    for step_index in range(STEPS):
        fields = []
        for came in swapped(outgoing):
            before = fields[1:][-1:]
            fields.append(
                kernel_call(
                    functools.partial(fields_kernel, gaps),
                    f32(3, comps, local, CHUNK_TILES * LANES),
                    [],
                    2 * 10**6,
                    10**6,
                    in_specs=[vmem, vmem] + [pl.BlockSpec(memory_space=pl.ANY)] * len(before),
                )(came, chunk_bands, *before)
            )
        returning = kernel_call(
            advect_kernel,
            [f32(GROUP, BACK_TILES * LANES)] * planes,
            [],
            80 * 10**6,
            5 * 10**6,
        )(*fields, flows[step_index], to_span, to_modes)
        local_sum = kernel_call(
            diffuse_kernel,
            f32(*state_shape),
            [pltpu.VMEM((nodes, GROUP, SLAB_TILES * LANES), jnp.float32)] * 2,
            12 * 10**6,
            2 * 10**6,
        )(state, metric, slab_bands)
        updated, own, *leaving = kernel_call(
            functools.partial(update_kernel, back_plans),
            [f32(*state_shape), f32(nodes, rows_total, LANES)] + [f32(rows_total, 2 * LANES)] * 4,
            [pltpu.VMEM((planes, GROUP, BACK_TILES * LANES), jnp.float32), edge_scratch],
            2 * 10**6,
            3 * 10**6,
        )(*swapped(returning), local_sum, table)
        traces = [
            lax.ppermute(
                buffer, "dom", [(i, trace_partner(i, matching, partitions)) for i in range(partitions)]
            )
            for matching, buffer in enumerate(leaving)
        ]
        if step_index + 1 < STEPS:
            state, xi, first = kernel_call(
                functools.partial(next_kernel, plans),
                [f32(*state_shape), f32(*state_shape), buffer],
                [edge_scratch],
                6 * 10**6,
                4 * 10**6,
            )(table, updated, own, *traces)
            outgoing = with_rest(state, xi, first)
        else:
            inner = kernel_call(
                inner_kernel,
                f32(comps, nodes, nodes, local, elements),
                row_copies,
                10**6,
                2 * 10**6,
                out_specs=in_hbm,
            )(updated)
            result = kernel_call(
                last_kernel,
                f32(comps, nodes, nodes, local, elements),
                [row_copies[0], edge_scratch, row_copies[1]],
                2 * 10**6,
                3 * 10**6,
                in_specs=[vmem] * 7 + [in_hbm],
                out_specs=in_hbm,
                input_output_aliases={7: 0},
            )(table, updated, own, *traces, inner)
    return result.transpose(0, 3, 1, 2, 4)


def plain_shards(adjoint, metric, base_flow, edge_list, flips):
    local_modes = adjoint.shape[1]
    deriv_table = cheb_table(adjoint.shape[2])
    span_basis, span_slope, forward, wave_sq = span_tables(MODES)
    wave_local = lax.dynamic_slice_in_dim(
        wave_sq, lax.axis_index("plane") * local_modes, local_modes, 0
    )
    adjoint_state = adjoint
    for step_index in range(STEPS):
        base_now = base_flow[step_index].reshape(12, MODES, -1)
        adjoint_state = advance(
            adjoint_state,
            metric,
            base_now,
            edge_list[0],
            flips[0],
            deriv_table,
            span_basis,
            span_slope,
            forward,
            wave_local,
        )
    return adjoint_state


def shards(adjoint, metric, base_flow, edge_list, flips):
    if adjoint.shape[1:] == (MODES // 4, NODES, NODES, 32) and (
        edge_list.shape[1:] == (5, 24) and lax.axis_size("dom") % 4 == 0
    ):
        return packed_shards(adjoint, metric, base_flow, edge_list, flips)
    return plain_shards(adjoint, metric, base_flow, edge_list, flips)


def solution(mesh):
    placed = (
        P(None, "plane", None, None, "dom"),
        P(None, "dom"),
        P(None, None, ("dom", "plane")),
        P("dom", None, None),
        P("dom", None, None),
    )
    return jax.shard_map(
        shards,
        mesh=mesh,
        in_specs=placed,
        out_specs=P(None, "plane", None, None, "dom"),
        check_vma=False,
    )
```

```python
import functools

import jax
import jax.numpy as jnp
import numpy as np
from jax import lax
from jax.experimental import pallas as pl
from jax.experimental.pallas import tpu as pltpu
from jax.sharding import PartitionSpec as P

MODES = 64
STEPS = 2


step_size = 0.01
viscosity = 0.02


def passed_along(shard, axis, by):
    size = lax.axis_size(axis)
    return lax.ppermute(shard, axis, [(i, (i + by) % size) for i in range(size)])


def cheb_table(node_count):
    order = node_count - 1
    node_ids = jnp.arange(node_count, dtype=jnp.int32)
    node_coords = -jnp.cos(jnp.pi * node_ids.astype(jnp.float32) / order)
    weight = jnp.where((node_ids == 0) | (node_ids == order), 2.0, 1.0).astype(jnp.float32)
    parity = jnp.where((node_ids[:, None] + node_ids[None, :]) % 2 == 0, 1.0, -1.0).astype(
        jnp.float32
    )
    on_diag = node_ids[:, None] == node_ids[None, :]
    differ = jnp.where(on_diag, 1.0, node_coords[:, None] - node_coords[None, :])
    off_diag = jnp.where(on_diag, 0.0, weight[:, None] / weight[None, :] * parity / differ)
    return off_diag - jnp.diag(jnp.sum(off_diag, axis=1))


def span_tables(modes):
    mode_ids = jnp.arange(modes, dtype=jnp.int32)
    wavenumber = (mode_ids + 1) // 2
    is_cosine = (mode_ids % 2 == 1) | (mode_ids == 0)
    span_ids = jnp.arange(modes, dtype=jnp.int32)
    phase_num = span_ids[:, None] * wavenumber[None, :] % modes
    angles = 2.0 * jnp.pi * phase_num.astype(jnp.float32) / modes
    cosines = jnp.cos(angles)
    sines = jnp.sin(angles)
    wave_f = wavenumber.astype(jnp.float32)
    span_basis = jnp.where(is_cosine[None, :], cosines, sines)
    span_slope = jnp.where(is_cosine[None, :], -wave_f[None, :] * sines, wave_f[None, :] * cosines)
    scaling = jnp.where((mode_ids == 0) | (mode_ids == modes - 1), 1.0 / modes, 2.0 / modes).astype(
        jnp.float32
    )
    forward = span_basis.T * scaling[:, None]
    return (span_basis, span_slope, forward, wave_f * wave_f)


def directional(field_data, metric, deriv_table, xi_row, eta_row):
    along_xi = jnp.einsum(
        "ai,cmije->cmaje", deriv_table, field_data, precision=lax.Precision.HIGHEST
    )
    along_eta = jnp.einsum(
        "bj,cmije->cmibe", deriv_table, field_data, precision=lax.Precision.HIGHEST
    )
    return metric[xi_row] * along_xi + metric[eta_row] * along_eta


def advect(coeffs, base_now, span_basis, span_slope, forward):
    values = jnp.einsum("nm,fmq->fnq", span_basis, coeffs, precision=lax.Precision.HIGHEST)
    along_z = jnp.einsum("nm,cmq->cnq", span_slope, coeffs[0:3], precision=lax.Precision.HIGHEST)
    products = []
    for comp in range(3):
        term = (
            base_now[0] * values[3 + comp]
            + base_now[1] * values[6 + comp]
            + base_now[2] * along_z[comp]
        )
        term = term - (
            values[0] * base_now[3 + comp]
            + values[1] * base_now[6 + comp]
            + values[2] * base_now[9 + comp]
        )
        products.append(term)
    return jnp.einsum("mn,cnq->cmq", forward, jnp.stack(products), precision=lax.Precision.HIGHEST)


def accumulate(field_data, edge_sums, counts):
    node_count = field_data.shape[2]
    last = node_count - 1
    total = field_data
    total = total.at[:, :, :, 0, :].add(edge_sums[:, :, :, 0, :])
    total = total.at[:, :, last, :, :].add(edge_sums[:, :, :, 1, :])
    total = total.at[:, :, :, last, :].add(edge_sums[:, :, :, 2, :])
    total = total.at[:, :, 0, :, :].add(edge_sums[:, :, :, 3, :])
    weight = jnp.ones((node_count, node_count, field_data.shape[4]), jnp.float32)
    weight = weight.at[:, 0, :].add(counts[0][None, :])
    weight = weight.at[last, :, :].add(counts[1][None, :])
    weight = weight.at[:, last, :].add(counts[2][None, :])
    weight = weight.at[0, :, :].add(counts[3][None, :])
    return total / weight


def assemble(field_data, edge_slots, flip_flags):
    components, local_modes, node_count, _, elements = field_data.shape
    last = node_count - 1
    row_count = components * local_modes * node_count
    traces = jnp.stack(
        [
            field_data[:, :, :, 0, :],
            field_data[:, :, last, :, :],
            field_data[:, :, :, last, :],
            field_data[:, :, 0, :, :],
        ],
        axis=3,
    )
    edge_table = traces.reshape(row_count, 4 * elements)
    blocks, capacity = edge_slots.shape
    half_span = (blocks - 1) // 2
    slot_edges = edge_slots.reshape(-1)
    occupied = (slot_edges >= 0).astype(jnp.float32)
    outgoing = jnp.take(edge_table, jnp.maximum(slot_edges, 0), axis=1) * occupied[None, :]

    def block_of(block_id):
        return outgoing[:, block_id * capacity : (block_id + 1) * capacity]

    own_pairs = (
        block_of(half_span)
        .reshape(row_count, capacity // 2, 2)[:, :, ::-1]
        .reshape(row_count, capacity)
    )
    received = {half_span: own_pairs}
    for block_id in range(blocks):
        if block_id != half_span:
            received[block_id] = passed_along(
                block_of(blocks - 1 - block_id), "dom", half_span - block_id
            )
    partners = jnp.concatenate([received[block_id] for block_id in range(blocks)], axis=1)
    shaped = partners.reshape(components * local_modes, node_count, blocks * capacity)
    shaped = (
        jnp.where(flip_flags.reshape(-1)[None, None, :] == 1, shaped[:, ::-1, :], shaped)
        * occupied[None, None, :]
    )
    onehot = (slot_edges[:, None] == jnp.arange(4 * elements, dtype=jnp.int32)[None, :]).astype(
        jnp.float32
    )
    edge_sums = jnp.dot(
        shaped.reshape(row_count, blocks * capacity), onehot, precision=lax.Precision.HIGHEST
    )
    edge_sums = edge_sums.reshape(components, local_modes, node_count, 4, elements)
    counts = jnp.sum(onehot, axis=0).reshape(4, elements)
    return accumulate(field_data, edge_sums, counts)


def advance(
    adjoint_state,
    metric,
    base_now,
    edge_slots,
    flip_flags,
    deriv_table,
    span_basis,
    span_slope,
    forward,
    wave_local,
):
    components, local_modes, node_count, _, elements = adjoint_state.shape
    points = node_count * node_count * elements
    grad_x = directional(adjoint_state, metric, deriv_table, 0, 2)
    grad_y = directional(adjoint_state, metric, deriv_table, 1, 3)
    stacked = jnp.concatenate([adjoint_state, grad_x, grad_y], axis=0).reshape(
        9, local_modes, points
    )
    gathered = lax.all_to_all(stacked, "plane", split_axis=2, concat_axis=1, tiled=True)
    advective = advect(gathered, base_now, span_basis, span_slope, forward)
    returned = lax.all_to_all(advective, "plane", split_axis=1, concat_axis=2, tiled=True).reshape(
        adjoint_state.shape
    )
    laplacian = directional(grad_x, metric, deriv_table, 0, 2) + directional(
        grad_y, metric, deriv_table, 1, 3
    )
    updated = adjoint_state + step_size * (
        returned + viscosity * (laplacian - wave_local[None, :, None, None, None] * adjoint_state)
    )
    return assemble(updated, edge_slots, flip_flags)


NODES = 9
LANES = 128
SLAB_TILES = 3
STATE_TILES = 7
RING_TILES = 6
BASE_TILES = 11
SEND_TILES = 12
CHUNK_TILES = 6
BODY_TILES = 5
BACK_TILES = 31
GROUP = 8
PARTNERS = (0, 2, 1, 3)
FIELDS_ORDER = (0, 1, 2, 3)
STEP_VISC = step_size * viscosity


def cheb_numbers():
    order = NODES - 1
    coords = -np.cos(np.pi * np.arange(NODES) / order)
    weight = np.ones(NODES)
    weight[0] = weight[-1] = 2.0
    table = np.zeros((NODES, NODES))
    for a in range(NODES):
        for i in range(NODES):
            if a != i:
                table[a, i] = weight[a] / weight[i] * (-1.0) ** (a + i) / (coords[a] - coords[i])
    return table - np.diag(table.sum(axis=1))


DERIV = cheb_numbers()


def span_numbers():
    modes = np.arange(MODES)
    wave = (modes + 1) // 2
    is_cosine = (modes % 2 == 1) | (modes == 0)
    angles = 2.0 * np.pi * (np.arange(MODES)[:, None] * wave[None, :] % MODES) / MODES
    cosines, sines = np.cos(angles), np.sin(angles)
    basis = np.where(is_cosine, cosines, sines)
    slope = np.where(is_cosine, -wave * sines, wave * cosines)
    scaling = np.where((modes == 0) | (modes == MODES - 1), 1.0 / MODES, 2.0 / MODES)
    return basis, slope, basis.T * scaling[:, None]


def in_two(table):
    table = table.astype(np.float32)
    high = table.astype(jnp.bfloat16)
    low = (table - high.astype(np.float32)).astype(jnp.bfloat16)
    return high, low


def span_weights(planes):
    basis, slope, forward = span_numbers()
    local = MODES // planes
    to_span, to_span_last, to_modes = [], [], []
    for me in range(planes):
        came = np.concatenate([(me ^ step) * local + np.arange(local) for step in PARTNERS])
        high, low = in_two(np.concatenate([basis, slope])[:, came])
        early, last = slice(0, MODES - local), slice(MODES - local, MODES)
        for table, columns in ((to_span, early), (to_span_last, last)):
            table.append(np.concatenate([high[:, columns], high[:, columns], low[:, columns]], axis=1))
        high, low = in_two(forward[came])
        to_modes.append(np.concatenate([high, high, low], axis=1))
    return np.stack(to_span), np.stack(to_span_last), np.stack(to_modes)


def eta_bands(first_lane, lanes, count):
    bands = np.zeros((24, lanes), np.float32)
    for lane in range(count):
        j = (first_lane + lane) % 288 // 32
        for d in range(-8, 9):
            if 0 <= j + d < NODES:
                bands[d + 8, lane] = DERIV[j, j + d]
    return bands


def tile_plan(segments, tiles):
    plan = [[] for _ in range(tiles)]
    for source, src, dst, length in segments:
        done = 0
        while done < length:
            s, d = src + done, dst + done
            size = min(length - done, LANES - s % LANES, LANES - d % LANES)
            plan[d // LANES].append((source, s // LANES, (d - s) % LANES, d % LANES, size))
            done += size
    return plan


def end_part(chunk, points):
    part = points - 2 * NODES * 32
    if chunk == 0:
        return 2, 0, points - part, part, 3
    if chunk == 3:
        return 6, NODES * 32 - part, 0, part, -7
    return None


def send_segments(chunk, points):
    ring, slab = STATE_TILES * LANES, NODES * 32
    turned = (points - 2 * slab) * chunk
    part = end_part(chunk, points)
    segments = []

    def add(source, src, dst, length):
        split = RING_TILES * LANES
        if dst < split < dst + length:
            add(source, src, dst, split - dst)
            add(source, src + split - dst, split, length - split + dst)
        else:
            segments.append((source, src, dst + (BASE_TILES - RING_TILES) * LANES * (dst >= split), length))

    if part is None:
        for r in range(3):
            start = (r * slab - turned) % ring
            first = min(slab, ring - start)
            add(("state", 2 * chunk + r), 0, start, first)
            if first < slab:
                add(("state", 2 * chunk + r), first, 0, slab - first)
        gap = (3 * slab - turned) % ring
    else:
        for i in range(NODES):
            low, high = max(i * slab, points * chunk), min((i + 1) * slab, points * (chunk + 1))
            if low < high:
                add(("state", i), low - i * slab, low - points * chunk, high - low)
        i, src, lane, length, ahead = part
        start = (lane + 32 * ahead) % ring
        add(("eta", i), src, start, length)
        gap = start + length
    body = points // LANES * LANES
    for i in range(NODES):
        low, high = max(i * slab, points * chunk), min((i + 1) * slab, points * (chunk + 1))
        cut = points * chunk + body
        if low < min(high, cut):
            segments.append(
                (("xi", i), low - i * slab, RING_TILES * LANES + low - points * chunk, min(high, cut) - low)
            )
        if max(low, cut) < high:
            low = max(low, cut)
            add(("xi", i), low - i * slab, gap + low - cut, high - low)
    return segments, gap


def chunk_eta_bands(chunk, points):
    bands = eta_bands((points - 2 * NODES * 32) * chunk, CHUNK_TILES * LANES, points)
    part = end_part(chunk, points)
    if part is not None:
        _, _, lane, length, ahead = part
        bands[:, lane : lane + length] = 0.0
        bands[ahead + 8, lane : lane + length] = 1.0
    return bands


def return_segments(points):
    slab = NODES * 32
    body = points // LANES * LANES
    plans = []
    for i in range(NODES):
        segments = []
        for chunk in range(4):
            for name, start, stop in (("body", 0, body), ("tail", body, points)):
                low = max(i * slab, chunk * points + start)
                high = min((i + 1) * slab, chunk * points + stop)
                if low < high:
                    segments.append(((name, chunk), low - chunk * points - start, low - i * slab, high - low))
        plans.append(tile_plan(segments, SLAB_TILES))
    return plans


def lane_ids(rows):
    return lax.broadcasted_iota(jnp.int32, (rows, LANES), 1)


def turn(value, shift):
    return value if shift % LANES == 0 else pltpu.roll(value, shift % LANES, 1)


def turner(load):
    made = {}

    def turned(source, tile, shift):
        key = source, tile, shift
        if key not in made:
            made[key] = turn(load(source, tile), shift)
        return made[key]

    return turned


def pieced(pieces, turned, lanes):
    total = None
    for source, tile, shift, low, size in pieces:
        value = turned(source, tile, shift)
        if total is None:
            total = value
        elif low + size == LANES:
            total = jnp.where(lanes >= low, value, total)
        else:
            total = jnp.where((lanes >= low) & (lanes < low + size), value, total)
    return total


def aligned(index, unit):
    return index if isinstance(index, int) else pl.multiple_of(index, unit)


def group_rows(g):
    return pl.ds(aligned(g * GROUP, GROUP), GROUP)


def tile_at(ref, lead, rows, tile):
    return ref[(*lead, rows, pl.ds(tile * LANES, LANES))]


def along_i(tiles):
    return [
        sum(tiles[i] * float(DERIV[a, i]) for i in range(1, NODES)) + tiles[0] * float(DERIV[a, 0])
        for a in range(NODES)
    ]


def turned_tiles(tiles, lanes):
    out = [tiles]
    for s in range(1, 4):
        spun = [pltpu.roll(t, LANES - 32 * s, 1) for t in tiles]
        out.append(
            [
                jnp.where(lanes < LANES - 32 * s, spun[t], spun[(t + 1) % len(tiles)])
                for t in range(len(tiles))
            ]
        )
    return out


def along_j(turned, ring, tile, band, used):
    total = None
    for d in used:
        term = turned[d % 4][(tile + d // 4) % ring] * band(d)
        total = term if total is None else total + term
    return total


def make_xi(groups, state, xi):
    for g in groups:
        rows = group_rows(g)
        for t in range(SLAB_TILES):
            for a, value in enumerate(along_i([tile_at(state, (i,), rows, t) for i in range(NODES)])):
                xi[a, rows, pl.ds(t * LANES, LANES)] = value


def used_offsets(tile):
    nodes = range(4 * tile, min(4 * tile + 4, NODES))
    return [d for d in range(-8, 9) if any(0 <= j + d < NODES for j in nodes)]


def make_buffer(plan, groups, state, xi, bands, put):
    lanes = lane_ids(GROUP)
    for g in groups:
        rows = group_rows(g)

        def load(source, tile, rows=rows):
            name, i = source
            if name != "eta":
                return tile_at(state if name == "state" else xi, (i,), rows, tile)
            turned = turned_tiles([tile_at(state, (i,), rows, t) for t in range(SLAB_TILES)], lanes)
            return along_j(
                turned, SLAB_TILES, tile, lambda d: tile_at(bands, (), pl.ds(d + 8, 1), tile), used_offsets(tile)
            )

        turned = turner(load)
        for t, pieces in enumerate(plan):
            value = pieced(pieces, turned, lanes) if pieces else jnp.zeros((GROUP, LANES), jnp.float32)
            put(rows, t, value)


def make_first(plans, state, xi, bands, out):
    target = lax.axis_index("plane") ^ PARTNERS[1]

    def put(rows, t, value):
        out[rows, pl.ds(t * LANES, LANES)] = value

    for chunk, plan in enumerate(plans):
        groups = range(state.shape[1] // GROUP)
        pl.when(target == chunk)(functools.partial(make_buffer, plan, groups, state, xi, bands, put))


def rest_kernel(plans, state, xi, bands, out0, out2, out3, extra3, staged):
    me = lax.axis_index("plane")
    for chunk, plan in enumerate(plans):

        def put(rows, t, value, chunk=chunk):
            staged[chunk, rows, pl.ds(t * LANES, LANES)] = value

        make_buffer(plan, range(state.shape[1] // GROUP), state, xi, bands, put)
    base, last = pl.ds(0, BASE_TILES * LANES), pl.ds(BASE_TILES * LANES, LANES)
    out0[...] = staged[me ^ PARTNERS[0]]
    out2[...] = staged[me ^ PARTNERS[2]]
    out3[...] = staged[me ^ PARTNERS[3], :, base]
    extra3[...] = staged[me ^ PARTNERS[3], :, last]


def first_kernel(plans, adjoint, far_bands, state, xi, out, taken, sems, bands):
    comps, local = taken.shape[0], taken.shape[3]

    def copy(c):
        return pltpu.make_async_copy(adjoint.at[c], taken.at[c], sems.at[c])

    for c in range(comps):
        copy(c).start()
    fetch = pltpu.make_async_copy(far_bands, bands, sems.at[comps])
    fetch.start()

    for c in range(comps):
        copy(c).wait()
        rows = pl.ds(c * local, local)
        for i in range(NODES):
            for t in range(SLAB_TILES):
                parts = [taken[c, i, j] for j in range(4 * t, min(4 * t + 4, NODES))]
                parts += [jnp.zeros_like(parts[0])] * (4 - len(parts))
                state[i, rows, pl.ds(t * LANES, LANES)] = jnp.concatenate(parts, axis=1)
        make_xi(range(c * local // GROUP, (c + 1) * local // GROUP), state, xi)
    fetch.wait()
    make_first(plans, state, xi, bands, out)


def metric_rows(metric):
    wide = jnp.concatenate([metric[...]] * (LANES // metric.shape[1]), axis=1)
    return jnp.concatenate([wide, wide], axis=0)


def flow_kernel(points, flow, metric, out0, out1, flat):
    me = lax.axis_index("plane")
    lanes, subs = lane_ids(8), lax.broadcasted_iota(jnp.int32, (8, LANES), 0)
    shift = lax.rem(LANES - lax.rem(me * points, LANES), LANES)
    turned = pltpu.roll(metric_rows(metric), shift, 1)
    ahead = pl.program_id(0) == 0
    first_first = jnp.where(ahead, turned[0:1], 1.0)
    first_second = jnp.where(ahead, turned[1:2], 0.0)
    second_first = jnp.where(ahead, turned[2:3], 0.0)
    second_second = jnp.where(ahead, turned[3:4], 1.0)
    per_sixteen = 16 * points // LANES
    last = CHUNK_TILES - 1

    for f in range(2):
        for s in range(STEPS):
            flat[f, s] = flow[f, s].reshape(flat.shape[2:])

    for s, out in enumerate((out0, out1)):
        for half in range(2):
            moved = (lanes + 64 * half + 8 * subs) & (LANES - 1)
            kept = lanes < LANES - 64 * half - 8 * subs

            def some_rows(h, _, s=s, half=half, out=out, moved=moved, kept=kept):
                rows = pl.ds(pl.multiple_of(16 * h + 8 * half, 8), 8)

                def field(f):
                    spun = []
                    for k in range(CHUNK_TILES):
                        start = per_sixteen * h + 40 * half + k
                        spun.append(pick(flat[f, s, pl.ds(start, 8, stride=5), :], moved))
                    return [jnp.where(kept, spun[k], spun[k + 1]) for k in range(last)] + [spun[last]]

                for t, (one, two) in enumerate(zip(field(0), field(1))):
                    out[0, rows, pl.ds(t * LANES, LANES)] = one * first_first + two * first_second
                    out[1, rows, pl.ds(t * LANES, LANES)] = one * second_first + two * second_second
                return 0

            lax.fori_loop(0, MODES // 16, some_rows, 0)


def tables_kernel(edges, flags, table, square):
    blocks, _, capacity = edges.shape
    lanes = lane_ids(capacity)
    slots = lax.broadcasted_iota(jnp.int32, (capacity, LANES), 0)
    here = slots == lax.rem(lanes, capacity)
    flag = jnp.zeros((1, LANES), jnp.int32)
    count = jnp.zeros((1, LANES), jnp.int32)
    table[...] = jnp.zeros(table.shape, jnp.int32)
    square[...] = jnp.zeros(square.shape, jnp.float32)
    for o in range(blocks):
        square[o : o + 1, 0:capacity] = edges[o].astype(jnp.float32)
        square[blocks + o : blocks + o + 1, 0:capacity] = flags[o].astype(jnp.float32)
    columns = square[...].T[0:capacity].astype(jnp.int32)
    for o in range(blocks):
        column = jnp.broadcast_to(columns[:, o : o + 1], (capacity, LANES))
        held = column == lanes

        def summed(mask, value):
            return jnp.sum(jnp.where(mask, value, 0), axis=0, keepdims=True)

        table[o : o + 1, :] = summed(here, jnp.maximum(column, 0))
        table[5 + o : 6 + o, :] = summed(held, slots)
        present = summed(held, jnp.ones_like(slots))
        table[10 + o : 11 + o, :] = present
        flag += summed(held, jnp.broadcast_to(columns[:, blocks + o : blocks + o + 1], (capacity, LANES)))
        count += present
        if o == blocks // 2:
            partner = slots + 1 - 2 * lax.rem(slots, 2)
            slot_of = jnp.broadcast_to(summed(held, partner), (capacity, LANES))
            partner_edge = summed(slots == slot_of, jnp.maximum(column, 0))
            table[16:17, :] = jnp.where(present > 0, partner_edge, 0)
    table[15:16, :] = flag
    table[17:18, :] = count


def diffuse_kernel(state, metric, bands, local_sum, first, second):
    me = lax.axis_index("plane")
    rows_total = state.shape[1]
    lanes = lane_ids(8)
    local = rows_total // 3
    wide = metric_rows(metric)
    xi_x, xi_y, eta_x, eta_y = (wide[r : r + 1] for r in range(4))
    g_ii = xi_x * xi_x + xi_y * xi_y
    g_ij = xi_x * eta_x + xi_y * eta_y
    g_jj = eta_x * eta_x + eta_y * eta_y
    def eta_of(tiles):
        turned = turned_tiles(tiles, lanes)
        return [
            along_j(turned, SLAB_TILES, t, lambda d, t=t: tile_at(bands, (), pl.ds(d + 8, 1), t), used_offsets(t))
            for t in range(SLAB_TILES)
        ]

    def some_rows(g, _):
        rows = pl.ds(pl.multiple_of(g * 8, 8), 8)
        first_mode = me * local + lax.rem(g * 8, local)
        wave = ((first_mode + lax.broadcasted_iota(jnp.int32, (8, LANES), 0) + 1) // 2).astype(jnp.float32)
        wave_sq = wave * wave
        for t in range(SLAB_TILES):
            for a, value in enumerate(along_i([tile_at(state, (i,), rows, t) for i in range(NODES)])):
                first[a, :, pl.ds(t * LANES, LANES)] = value
        for i in range(NODES):
            eta = eta_of([tile_at(state, (i,), rows, t) for t in range(SLAB_TILES)])
            mixed = []
            for t in range(SLAB_TILES):
                xi = first[i, :, pl.ds(t * LANES, LANES)]
                first[i, :, pl.ds(t * LANES, LANES)] = g_ii * xi + g_ij * eta[t]
                mixed.append(g_ij * xi + g_jj * eta[t])
            for t, value in enumerate(eta_of(mixed)):
                second[i, :, pl.ds(t * LANES, LANES)] = value
        for t in range(SLAB_TILES):
            tiles = [first[i, :, pl.ds(t * LANES, LANES)] for i in range(NODES)]
            for a, value in enumerate(along_i(tiles)):
                now = tile_at(state, (a,), rows, t)
                laplacian = value + second[a, :, pl.ds(t * LANES, LANES)]
                local_sum[a, rows, pl.ds(t * LANES, LANES)] = now + STEP_VISC * (laplacian - wave_sq * now)
        return 0

    lax.fori_loop(0, rows_total // 8, some_rows, 0)


def halves(value):
    high = value.astype(jnp.bfloat16)
    return high, (value - high.astype(jnp.float32)).astype(jnp.bfloat16)


def fields_kernel(gaps, split, source, *refs):
    extra, bands = (refs[0], refs[1]) if split else (None, refs[0])
    fields = refs[-1]
    me = lax.axis_index("plane")
    rows_total = source.shape[0]
    local = fields.shape[2]
    lanes = lane_ids(GROUP)
    gap = sum(jnp.where(me == b, g, 0) for b, g in enumerate(gaps))
    gap_late, gap_shift = gap >= RING_TILES * LANES, lax.rem(LANES - lax.rem(gap, LANES), LANES)

    for g in range(rows_total // GROUP):
        rows = group_rows(g)
        c = g * GROUP // local
        target = pl.ds(g * GROUP % local, GROUP)
        tiles = [tile_at(source, (), rows, t) for t in range(RING_TILES)]
        tiles.append(extra[rows, :] if split else tile_at(source, (), rows, BASE_TILES))
        turned = turned_tiles(tiles, lanes)
        for t in range(CHUNK_TILES):
            at = pl.ds(t * LANES, LANES)
            fields[0, c, target, at] = tiles[t]
            fields[2, c, target, at] = along_j(
                turned, STATE_TILES, t, lambda d, at=at: bands[me, pl.ds(d + 8, 1), at], range(-8, 9)
            )
        for t in range(BODY_TILES):
            fields[1, c, target, pl.ds(t * LANES, LANES)] = tile_at(source, (), rows, RING_TILES + t)
        tail = jnp.where(gap_late, tiles[RING_TILES], tiles[RING_TILES - 1])
        fields[1, c, target, pl.ds(BODY_TILES * LANES, LANES)] = pltpu.roll(tail, gap_shift, 1)


def span_dot(a, value):
    high, low = halves(value)
    stacked = jnp.concatenate([high, low, high], axis=0)
    return jnp.dot(a, stacked, preferred_element_type=jnp.float32)


LANE_PARTS = [pl.ds(first, 2 * LANES) for first in range(0, CHUNK_TILES * LANES, 2 * LANES)]


def products(sources, flow, both, part):
    def field(kind, c):
        return jnp.concatenate([fields[kind, c, :, part] for fields in sources], axis=0)

    comps, basis = sources[0].shape[1], both[:MODES]
    values, sums = [], []
    for c in range(comps):
        out = span_dot(both, field(0, c))
        values.append(out[:MODES])
        along_x = flow[0, :, part] * span_dot(basis, field(1, c))
        along_y = flow[1, :, part] * span_dot(basis, field(2, c))
        sums.append(along_x + along_y + flow[2, :, part] * out[MODES:])
    for c in range(comps):
        taken = values[0] * flow[3 + c, :, part]
        taken += values[1] * flow[6 + c, :, part]
        taken += values[2] * flow[9 + c, :, part]
        yield c, sums[c] - taken


def early_kernel(fields0, fields1, fields2, flow, to_span, early):
    both = to_span[lax.axis_index("plane")]
    for part in LANE_PARTS:
        for c, product in products((fields0, fields1, fields2), flow, both, part):
            early[c, :, part] = product


def advect_kernel(fields3, early, flow, to_span, to_modes, *outs):
    me = lax.axis_index("plane")
    both, back = to_span[me], to_modes[me]
    lanes = lane_ids(GROUP)
    local = MODES // len(outs)
    tails = [None] * len(outs)
    for n, part in enumerate(LANE_PARTS):
        for c, product in products((fields3,), flow, both, part):
            result = span_dot(back, product + early[c, :, part])
            for k, out in enumerate(outs):
                for half in range(local // GROUP):
                    g = c * (local // GROUP) + half
                    piece = result[k * local + half * GROUP : k * local + (half + 1) * GROUP]
                    first = (BODY_TILES * g + 2 * n) * LANES
                    if n < len(LANE_PARTS) - 1:
                        out[:, pl.ds(first, 2 * LANES)] = piece
                        continue
                    out[:, pl.ds(first, LANES)] = piece[:, :LANES]
                    tail = turn(piece[:, LANES:], 8 * g)
                    tails[k] = tail if g == 0 else jnp.where(lanes >= 8 * g, tail, tails[k])
    for out, tail in zip(outs, tails):
        out[:, pl.ds((BACK_TILES - 1) * LANES, LANES)] = tail


def trace_blocks(me):
    odd, late = lax.rem(me, 2), lax.rem(me, 4) // 2
    return 4 * late, 1 + 2 * odd, 4 - 4 * late, 3 - 2 * odd


def trace_partner(me, matching, size):
    step, start = ((2, 2), (1, 1), (2, 0), (1, 0))[matching]
    return (((me + start) ^ step) - start) % size


def update_kernel(plans, in0, in1, in2, in3, local_sum, table, updated, own, out0, out1, out2, out3, chunks, traces):
    me = lax.axis_index("plane")
    rows_total = local_sum.shape[1]
    last = NODES - 1
    lanes = lane_ids(8)
    for step, source in zip(PARTNERS, (in0, in1, in2, in3)):
        chunks[me ^ step] = source[...]

    trace_plans = [
        tile_plan([(k, 0, 0, 32), (last, 32 * k, 32, 32), (k, 256, 64, 32), (0, 32 * k, 96, 32)], 1)[0]
        for k in range(NODES)
    ]

    blocks = trace_blocks(lax.axis_index("dom"))

    def wide(row):
        return jnp.broadcast_to(table[pl.ds(row, 1), :], (8, LANES))

    turned_round, partner = wide(15) == 1, wide(16)
    slot_edges = [wide(o) for o in blocks]
    groups = range(rows_total // GROUP)
    for g in groups:
        rows = group_rows(g)

        def load(source, tile, g=g):
            if source[0] == "tail":
                return turn(tile_at(chunks, (source[1],), slice(None), BACK_TILES - 1), -8 * g)
            return tile_at(chunks, (source[1],), slice(None), BODY_TILES * g + tile)

        turned = turner(load)
        for i in range(NODES):
            for t in range(SLAB_TILES):
                value = pieced(plans[i][t], turned, lanes)
                updated[i, rows, pl.ds(t * LANES, LANES)] = (
                    tile_at(local_sum, (i,), rows, t) + step_size * value
                )
    for g in groups:
        rows = group_rows(g)
        edges = turner(lambda i, tile, rows=rows: tile_at(updated, (i,), rows, tile))
        raw = [pieced(plan, edges, lanes) for plan in trace_plans]
        for k in range(NODES):
            traces[k, rows, :] = jnp.where(turned_round, raw[last - k], raw[k])
    for g in groups:
        rows = group_rows(g)
        for slot_edge, out in zip(slot_edges, (out0, out1, out2, out3)):
            for t in range(2):
                total = None
                for k in range(5 * t, min(5 * t + 5, NODES)):
                    value = pick(traces[k, rows, :], slot_edge)
                    total = value if total is None else jnp.where(lanes >= 24 * (k - 5 * t), value, total)
                out[rows, pl.ds(t * LANES, LANES)] = total
        for k in range(NODES):
            own[k, rows, :] = pick(traces[k, rows, :], partner)


def pick(value, index):
    return jnp.take_along_axis(value, index, axis=1, mode="promise_in_bounds")


def join_edges(table, updated, own, came, sums, put):
    rows_total = updated.shape[1]
    last = NODES - 1
    lanes = lane_ids(8)
    blocks = trace_blocks(lax.axis_index("dom"))

    def wide(row):
        return jnp.broadcast_to(table[pl.ds(row, 1), :], (8, LANES))

    share = wide(17).astype(jnp.float32)
    quarter = lanes // 32
    own_has = wide(12) > 0
    has = [wide(10 + o) > 0 for o in blocks]
    slots = [wide(5 + o) for o in blocks]

    def spread(values, at, t):
        value = None
        for k in range(4 * t, min(4 * t + 4, NODES)):
            moved = turn(values[k], 32 * (k - 4 * t - at))
            value = jnp.where(quarter == k - 4 * t, moved, 0.0 if value is None else value)
        return value

    def edge_parts(values, i, t):
        parts = []
        if t == 0:
            parts.append(jnp.where(quarter == 0, values[i], 0.0))
        if i == last:
            parts.append(spread(values, 1, t))
        if t == 2:
            parts.append(jnp.where(quarter == 0, turn(values[i], -64), 0.0))
        if i == 0:
            parts.append(spread(values, 3, t))
        return parts

    shares, scale = [share] * NODES, {}
    for i in (0, 1, last):
        for t in range(SLAB_TILES):
            parts = edge_parts(shares, i, t)
            if parts:
                scale[i, t] = 1.0 / (1.0 + sum(parts[1:], parts[0]))

    groups = range(rows_total // GROUP)
    for g in groups:
        rows = group_rows(g)
        for k in range(NODES):
            total = jnp.where(own_has, own[k, rows, :], 0.0)
            for slot, there, source in zip(slots, has, came):
                value = pick(tile_at(source, (), rows, k // 5), slot + 24 * (k % 5))
                total = jnp.where(there, value, total)
            sums[k, rows, :] = total
    for g in groups:
        rows = group_rows(g)
        values = [sums[k, rows, :] for k in range(NODES)]
        for i in range(NODES):
            for t in range(SLAB_TILES):
                parts = edge_parts(values, i, t)
                if parts:
                    total = tile_at(updated, (i,), rows, t)
                    for part in parts:
                        total += part
                    put(g, i, t, total * scale[i if i in (0, last) else 1, t])


def next_kernel(plans, table, updated, own, r0, r1, r2, r3, bands, state, xi, out, sums):
    def put(g, i, t, value):
        state[i, group_rows(g), pl.ds(t * LANES, LANES)] = value

    for i in range(1, NODES - 1):
        state[i, :, pl.ds(LANES, LANES)] = updated[i, :, pl.ds(LANES, LANES)]
    join_edges(table, updated, own, (r0, r1, r2, r3), sums, put)
    make_xi(range(updated.shape[1] // GROUP), state, xi)
    make_first(plans, state, xi, bands, out)


def last_kernel(table, updated, own, r0, r1, r2, r3, out, state, sums, given, sems):
    comps, local, elements = given.shape[0], given.shape[3], given.shape[4]

    def put(g, i, t, value):
        state[i, group_rows(g), pl.ds(t * LANES, LANES)] = value

    join_edges(table, updated, own, (r0, r1, r2, r3), sums, put)
    copies = []
    for i in range(NODES):
        for c in range(comps):
            rows = pl.ds(c * local, local)
            for t in range(SLAB_TILES):
                joined = t != 1 or i in (0, NODES - 1)
                tile = tile_at(state if joined else updated, (i,), rows, t)
                for q in range(min(4, NODES - 4 * t)):
                    given[c, i, 4 * t + q] = turn(tile, -32 * q)[:, :elements]
        copies.append(pltpu.make_async_copy(given.at[:, i], out.at[:, i], sems.at[i]))
        copies[-1].start()
    for copy in copies:
        copy.wait()


def f32(*shape):
    return jax.ShapeDtypeStruct(shape, jnp.float32)


def kernel_call(body, outs, scratch, flops, moved, **more):
    return pl.pallas_call(
        body,
        out_shape=outs,
        scratch_shapes=scratch,
        compiler_params=pltpu.CompilerParams(vmem_limit_bytes=16 * 1024 * 1024),
        cost_estimate=pl.CostEstimate(flops=flops, bytes_accessed=moved, transcendentals=0),
        **more,
    )


def swapped(buffers):
    return [buffers[0]] + [swap(buffer, step) for buffer, step in zip(buffers[1:], PARTNERS[1:])]


def swap(buffer, step, wanted=range(4)):
    return lax.ppermute(buffer, "plane", sorted((i ^ step, i) for i in wanted))


def packed_shards(adjoint, metric, base_flow, edge_list, flips):
    comps, local, nodes, _, elements = adjoint.shape
    planes = MODES // local
    points = nodes * nodes * elements // planes
    rows_total = comps * local
    partitions = lax.axis_size("dom")
    state_shape = (nodes, rows_total, SLAB_TILES * LANES)

    layouts = [send_segments(chunk, points) for chunk in range(planes)]
    plans = [tile_plan(segments, SEND_TILES) for segments, _ in layouts]
    gaps = [gap for _, gap in layouts]
    back_plans = return_segments(points)
    to_span, to_span_last, to_modes = span_weights(planes)
    slab_bands = eta_bands(0, SLAB_TILES * LANES, nodes * elements)
    middle = [chunk for chunk, plan in enumerate(plans) if plan[-1]]
    chunk_bands = np.stack([chunk_eta_bands(b, points) for b in range(planes)])

    in_hbm, vmem = (pl.BlockSpec(memory_space=space) for space in (pltpu.HBM, pltpu.VMEM))
    buffer, base, extra = (f32(rows_total, tiles * LANES) for tiles in (SEND_TILES, BASE_TILES, 1))
    row_copies = [
        pltpu.VMEM((comps, nodes, nodes, local, elements), jnp.float32),
        pltpu.SemaphoreType.DMA((nodes,)),
    ]
    edge_scratch = pltpu.VMEM((nodes, rows_total, LANES), jnp.float32)

    def forward(state, xi, first):
        own, second, third, last_tile = kernel_call(
            functools.partial(rest_kernel, plans),
            [buffer, buffer, base, extra],
            [pltpu.VMEM((planes, *buffer.shape), jnp.float32)],
            10**6,
            2 * 10**6,
        )(state, xi, slab_bands)
        came = swapped([own, first, second, third])
        return [(part,) for part in came[:-1]] + [(came[-1], swap(last_tile, PARTNERS[-1], middle))]

    in_rows = pltpu.with_memory_space_constraint(adjoint.transpose(0, 2, 3, 1, 4), pltpu.HBM)
    state, *prepared = kernel_call(
        functools.partial(first_kernel, plans),
        [f32(*state_shape), f32(*state_shape), buffer],
        row_copies + [pltpu.VMEM(slab_bands.shape, jnp.float32)],
        4 * 10**6,
        4 * 10**6,
        in_specs=[in_hbm, in_hbm],
    )(in_rows, pltpu.with_memory_space_constraint(jnp.asarray(slab_bands), pltpu.HBM))
    incoming = forward(state, *prepared)
    whole, two_fields = (12, MODES, CHUNK_TILES * LANES), (2, MODES, CHUNK_TILES * LANES)
    lay = base_flow.transpose(1, 0, 2)
    flows = kernel_call(
        functools.partial(flow_kernel, points),
        [f32(*whole)] * STEPS,
        [pltpu.VMEM((2, STEPS, lay.shape[2] // LANES, LANES), jnp.float32)],
        4 * 10**6,
        9 * 10**6,
        grid=(6,),
        in_specs=[
            pl.BlockSpec((2, *lay.shape[1:]), lambda pair: (pair, 0, 0)),
            pl.BlockSpec(metric.shape, lambda pair: (0, 0)),
        ],
        out_specs=[pl.BlockSpec(two_fields, lambda pair: (pair, 0, 0))] * STEPS,
    )(lay, metric)
    table = kernel_call(
        tables_kernel,
        jax.ShapeDtypeStruct((24, LANES), jnp.int32),
        [pltpu.VMEM((LANES, LANES), jnp.float32)],
        10**5,
        10**5,
    )(edge_list.transpose(1, 0, 2), flips.transpose(1, 0, 2))

    for step_index in range(STEPS):
        fields = [None] * planes
        before = []
        for k in FIELDS_ORDER:
            parts = incoming[k]
            fields[k] = kernel_call(
                functools.partial(fields_kernel, gaps, len(parts) > 1),
                f32(3, comps, local, CHUNK_TILES * LANES),
                [],
                2 * 10**6,
                10**6,
                in_specs=[vmem] * (len(parts) + 1) + [pl.BlockSpec(memory_space=pl.ANY)] * len(before),
            )(*parts, chunk_bands, *before)
            before = [fields[k]] if k > 0 else []
        early = kernel_call(
            early_kernel, f32(comps, MODES, CHUNK_TILES * LANES), [], 50 * 10**6, 5 * 10**6
        )(*fields[:-1], flows[step_index], to_span)
        returning = kernel_call(
            advect_kernel,
            [f32(GROUP, BACK_TILES * LANES)] * planes,
            [],
            30 * 10**6,
            5 * 10**6,
        )(fields[-1], early, flows[step_index], to_span_last, to_modes)
        local_sum = kernel_call(
            diffuse_kernel,
            f32(*state_shape),
            [pltpu.VMEM((nodes, GROUP, SLAB_TILES * LANES), jnp.float32)] * 2,
            12 * 10**6,
            2 * 10**6,
        )(state, metric, slab_bands)
        updated, own, *leaving = kernel_call(
            functools.partial(update_kernel, back_plans),
            [f32(*state_shape), f32(nodes, rows_total, LANES)] + [f32(rows_total, 2 * LANES)] * 4,
            [pltpu.VMEM((planes, GROUP, BACK_TILES * LANES), jnp.float32), edge_scratch],
            2 * 10**6,
            3 * 10**6,
        )(*swapped(returning), local_sum, table)
        traces = [
            lax.ppermute(
                buffer, "dom", [(i, trace_partner(i, matching, partitions)) for i in range(partitions)]
            )
            for matching, buffer in enumerate(leaving)
        ]
        if step_index + 1 < STEPS:
            state, *prepared = kernel_call(
                functools.partial(next_kernel, plans),
                [f32(*state_shape), f32(*state_shape), buffer],
                [edge_scratch],
                6 * 10**6,
                4 * 10**6,
            )(table, updated, own, *traces, slab_bands)
            incoming = forward(state, *prepared)
        else:
            result = kernel_call(
                last_kernel,
                f32(comps, nodes, nodes, local, elements),
                [pltpu.VMEM(state_shape, jnp.float32), edge_scratch, *row_copies],
                2 * 10**6,
                3 * 10**6,
                out_specs=in_hbm,
            )(table, updated, own, *traces)
    return result.transpose(0, 3, 1, 2, 4)


def plain_shards(adjoint, metric, base_flow, edge_list, flips):
    local_modes = adjoint.shape[1]
    deriv_table = cheb_table(adjoint.shape[2])
    span_basis, span_slope, forward, wave_sq = span_tables(MODES)
    wave_local = lax.dynamic_slice_in_dim(
        wave_sq, lax.axis_index("plane") * local_modes, local_modes, 0
    )
    adjoint_state = adjoint
    for step_index in range(STEPS):
        base_now = base_flow[step_index].reshape(12, MODES, -1)
        adjoint_state = advance(
            adjoint_state,
            metric,
            base_now,
            edge_list[0],
            flips[0],
            deriv_table,
            span_basis,
            span_slope,
            forward,
            wave_local,
        )
    return adjoint_state


def shards(adjoint, metric, base_flow, edge_list, flips):
    if adjoint.shape[1:] == (MODES // 4, NODES, NODES, 32) and (
        edge_list.shape[1:] == (5, 24) and lax.axis_size("dom") % 4 == 0
    ):
        return packed_shards(adjoint, metric, base_flow, edge_list, flips)
    return plain_shards(adjoint, metric, base_flow, edge_list, flips)


def solution(mesh):
    placed = (
        P(None, "plane", None, None, "dom"),
        P(None, "dom"),
        P(None, None, ("dom", "plane")),
        P("dom", None, None),
        P("dom", None, None),
    )
    return jax.shard_map(
        shards,
        mesh=mesh,
        in_specs=placed,
        out_specs=P(None, "plane", None, None, "dom"),
        check_vma=False,
    )
```

```python
import functools

import jax
import jax.numpy as jnp
import numpy as np
from jax import lax
from jax.experimental import pallas as pl
from jax.experimental.pallas import tpu as pltpu
from jax.sharding import PartitionSpec as P

MODES = 64
STEPS = 2


step_size = 0.01
viscosity = 0.02


def passed_along(shard, axis, by):
    size = lax.axis_size(axis)
    return lax.ppermute(shard, axis, [(i, (i + by) % size) for i in range(size)])


def cheb_table(node_count):
    order = node_count - 1
    node_ids = jnp.arange(node_count, dtype=jnp.int32)
    node_coords = -jnp.cos(jnp.pi * node_ids.astype(jnp.float32) / order)
    weight = jnp.where((node_ids == 0) | (node_ids == order), 2.0, 1.0).astype(jnp.float32)
    parity = jnp.where((node_ids[:, None] + node_ids[None, :]) % 2 == 0, 1.0, -1.0).astype(
        jnp.float32
    )
    on_diag = node_ids[:, None] == node_ids[None, :]
    differ = jnp.where(on_diag, 1.0, node_coords[:, None] - node_coords[None, :])
    off_diag = jnp.where(on_diag, 0.0, weight[:, None] / weight[None, :] * parity / differ)
    return off_diag - jnp.diag(jnp.sum(off_diag, axis=1))


def span_tables(modes):
    mode_ids = jnp.arange(modes, dtype=jnp.int32)
    wavenumber = (mode_ids + 1) // 2
    is_cosine = (mode_ids % 2 == 1) | (mode_ids == 0)
    span_ids = jnp.arange(modes, dtype=jnp.int32)
    phase_num = span_ids[:, None] * wavenumber[None, :] % modes
    angles = 2.0 * jnp.pi * phase_num.astype(jnp.float32) / modes
    cosines = jnp.cos(angles)
    sines = jnp.sin(angles)
    wave_f = wavenumber.astype(jnp.float32)
    span_basis = jnp.where(is_cosine[None, :], cosines, sines)
    span_slope = jnp.where(is_cosine[None, :], -wave_f[None, :] * sines, wave_f[None, :] * cosines)
    scaling = jnp.where((mode_ids == 0) | (mode_ids == modes - 1), 1.0 / modes, 2.0 / modes).astype(
        jnp.float32
    )
    forward = span_basis.T * scaling[:, None]
    return (span_basis, span_slope, forward, wave_f * wave_f)


def directional(field_data, metric, deriv_table, xi_row, eta_row):
    along_xi = jnp.einsum(
        "ai,cmije->cmaje", deriv_table, field_data, precision=lax.Precision.HIGHEST
    )
    along_eta = jnp.einsum(
        "bj,cmije->cmibe", deriv_table, field_data, precision=lax.Precision.HIGHEST
    )
    return metric[xi_row] * along_xi + metric[eta_row] * along_eta


def advect(coeffs, base_now, span_basis, span_slope, forward):
    values = jnp.einsum("nm,fmq->fnq", span_basis, coeffs, precision=lax.Precision.HIGHEST)
    along_z = jnp.einsum("nm,cmq->cnq", span_slope, coeffs[0:3], precision=lax.Precision.HIGHEST)
    products = []
    for comp in range(3):
        term = (
            base_now[0] * values[3 + comp]
            + base_now[1] * values[6 + comp]
            + base_now[2] * along_z[comp]
        )
        term = term - (
            values[0] * base_now[3 + comp]
            + values[1] * base_now[6 + comp]
            + values[2] * base_now[9 + comp]
        )
        products.append(term)
    return jnp.einsum("mn,cnq->cmq", forward, jnp.stack(products), precision=lax.Precision.HIGHEST)


def accumulate(field_data, edge_sums, counts):
    node_count = field_data.shape[2]
    last = node_count - 1
    total = field_data
    total = total.at[:, :, :, 0, :].add(edge_sums[:, :, :, 0, :])
    total = total.at[:, :, last, :, :].add(edge_sums[:, :, :, 1, :])
    total = total.at[:, :, :, last, :].add(edge_sums[:, :, :, 2, :])
    total = total.at[:, :, 0, :, :].add(edge_sums[:, :, :, 3, :])
    weight = jnp.ones((node_count, node_count, field_data.shape[4]), jnp.float32)
    weight = weight.at[:, 0, :].add(counts[0][None, :])
    weight = weight.at[last, :, :].add(counts[1][None, :])
    weight = weight.at[:, last, :].add(counts[2][None, :])
    weight = weight.at[0, :, :].add(counts[3][None, :])
    return total / weight


def assemble(field_data, edge_slots, flip_flags):
    components, local_modes, node_count, _, elements = field_data.shape
    last = node_count - 1
    row_count = components * local_modes * node_count
    traces = jnp.stack(
        [
            field_data[:, :, :, 0, :],
            field_data[:, :, last, :, :],
            field_data[:, :, :, last, :],
            field_data[:, :, 0, :, :],
        ],
        axis=3,
    )
    edge_table = traces.reshape(row_count, 4 * elements)
    blocks, capacity = edge_slots.shape
    half_span = (blocks - 1) // 2
    slot_edges = edge_slots.reshape(-1)
    occupied = (slot_edges >= 0).astype(jnp.float32)
    outgoing = jnp.take(edge_table, jnp.maximum(slot_edges, 0), axis=1) * occupied[None, :]

    def block_of(block_id):
        return outgoing[:, block_id * capacity : (block_id + 1) * capacity]

    own_pairs = (
        block_of(half_span)
        .reshape(row_count, capacity // 2, 2)[:, :, ::-1]
        .reshape(row_count, capacity)
    )
    received = {half_span: own_pairs}
    for block_id in range(blocks):
        if block_id != half_span:
            received[block_id] = passed_along(
                block_of(blocks - 1 - block_id), "dom", half_span - block_id
            )
    partners = jnp.concatenate([received[block_id] for block_id in range(blocks)], axis=1)
    shaped = partners.reshape(components * local_modes, node_count, blocks * capacity)
    shaped = (
        jnp.where(flip_flags.reshape(-1)[None, None, :] == 1, shaped[:, ::-1, :], shaped)
        * occupied[None, None, :]
    )
    onehot = (slot_edges[:, None] == jnp.arange(4 * elements, dtype=jnp.int32)[None, :]).astype(
        jnp.float32
    )
    edge_sums = jnp.dot(
        shaped.reshape(row_count, blocks * capacity), onehot, precision=lax.Precision.HIGHEST
    )
    edge_sums = edge_sums.reshape(components, local_modes, node_count, 4, elements)
    counts = jnp.sum(onehot, axis=0).reshape(4, elements)
    return accumulate(field_data, edge_sums, counts)


def advance(
    adjoint_state,
    metric,
    base_now,
    edge_slots,
    flip_flags,
    deriv_table,
    span_basis,
    span_slope,
    forward,
    wave_local,
):
    components, local_modes, node_count, _, elements = adjoint_state.shape
    points = node_count * node_count * elements
    grad_x = directional(adjoint_state, metric, deriv_table, 0, 2)
    grad_y = directional(adjoint_state, metric, deriv_table, 1, 3)
    stacked = jnp.concatenate([adjoint_state, grad_x, grad_y], axis=0).reshape(
        9, local_modes, points
    )
    gathered = lax.all_to_all(stacked, "plane", split_axis=2, concat_axis=1, tiled=True)
    advective = advect(gathered, base_now, span_basis, span_slope, forward)
    returned = lax.all_to_all(advective, "plane", split_axis=1, concat_axis=2, tiled=True).reshape(
        adjoint_state.shape
    )
    laplacian = directional(grad_x, metric, deriv_table, 0, 2) + directional(
        grad_y, metric, deriv_table, 1, 3
    )
    updated = adjoint_state + step_size * (
        returned + viscosity * (laplacian - wave_local[None, :, None, None, None] * adjoint_state)
    )
    return assemble(updated, edge_slots, flip_flags)


NODES = 9
LANES = 128
SLAB_TILES = 3
STATE_TILES = 7
RING_TILES = 6
BASE_TILES = 11
SEND_TILES = 12
CHUNK_TILES = 6
BODY_TILES = 5
BACK_TILES = 31
GROUP = 8
PARTNERS = (0, 2, 1, 3)
FIELDS_ORDER = (0, 1, 2, 3)
STEP_VISC = step_size * viscosity


def cheb_numbers():
    order = NODES - 1
    coords = -np.cos(np.pi * np.arange(NODES) / order)
    weight = np.ones(NODES)
    weight[0] = weight[-1] = 2.0
    table = np.zeros((NODES, NODES))
    for a in range(NODES):
        for i in range(NODES):
            if a != i:
                table[a, i] = weight[a] / weight[i] * (-1.0) ** (a + i) / (coords[a] - coords[i])
    return table - np.diag(table.sum(axis=1))


DERIV = cheb_numbers()


def span_numbers():
    modes = np.arange(MODES)
    wave = (modes + 1) // 2
    is_cosine = (modes % 2 == 1) | (modes == 0)
    angles = 2.0 * np.pi * (np.arange(MODES)[:, None] * wave[None, :] % MODES) / MODES
    cosines, sines = np.cos(angles), np.sin(angles)
    basis = np.where(is_cosine, cosines, sines)
    slope = np.where(is_cosine, -wave * sines, wave * cosines)
    scaling = np.where((modes == 0) | (modes == MODES - 1), 1.0 / MODES, 2.0 / MODES)
    return basis, slope, basis.T * scaling[:, None]


def in_two(table):
    table = table.astype(np.float32)
    high = table.astype(jnp.bfloat16)
    low = (table - high.astype(np.float32)).astype(jnp.bfloat16)
    return high, low


def span_weights(planes):
    basis, slope, forward = span_numbers()
    local = MODES // planes
    to_span, to_span_last, to_modes = [], [], []
    for me in range(planes):
        came = np.concatenate([(me ^ step) * local + np.arange(local) for step in PARTNERS])
        high, low = in_two(np.concatenate([basis, slope])[:, came])
        early, last = slice(0, MODES - local), slice(MODES - local, MODES)
        for table, columns in ((to_span, early), (to_span_last, last)):
            table.append(np.concatenate([high[:, columns], high[:, columns], low[:, columns]], axis=1))
        high, low = in_two(forward[came])
        to_modes.append(np.concatenate([high, high, low], axis=1))
    return np.stack(to_span), np.stack(to_span_last), np.stack(to_modes)


def eta_bands(first_lane, lanes, count):
    bands = np.zeros((24, lanes), np.float32)
    for lane in range(count):
        j = (first_lane + lane) % 288 // 32
        for d in range(-8, 9):
            if 0 <= j + d < NODES:
                bands[d + 8, lane] = DERIV[j, j + d]
    return bands


def tile_plan(segments, tiles):
    plan = [[] for _ in range(tiles)]
    for source, src, dst, length in segments:
        done = 0
        while done < length:
            s, d = src + done, dst + done
            size = min(length - done, LANES - s % LANES, LANES - d % LANES)
            plan[d // LANES].append((source, s // LANES, (d - s) % LANES, d % LANES, size))
            done += size
    return plan


def end_part(chunk, points):
    part = points - 2 * NODES * 32
    if chunk == 0:
        return 2, 0, points - part, part, 3
    if chunk == 3:
        return 6, NODES * 32 - part, 0, part, -7
    return None


def send_segments(chunk, points):
    ring, slab = STATE_TILES * LANES, NODES * 32
    turned = (points - 2 * slab) * chunk
    part = end_part(chunk, points)
    segments = []

    def add(source, src, dst, length):
        split = RING_TILES * LANES
        if dst < split < dst + length:
            add(source, src, dst, split - dst)
            add(source, src + split - dst, split, length - split + dst)
        else:
            segments.append((source, src, dst + (BASE_TILES - RING_TILES) * LANES * (dst >= split), length))

    if part is None:
        for r in range(3):
            start = (r * slab - turned) % ring
            first = min(slab, ring - start)
            add(("state", 2 * chunk + r), 0, start, first)
            if first < slab:
                add(("state", 2 * chunk + r), first, 0, slab - first)
        gap = (3 * slab - turned) % ring
    else:
        for i in range(NODES):
            low, high = max(i * slab, points * chunk), min((i + 1) * slab, points * (chunk + 1))
            if low < high:
                add(("state", i), low - i * slab, low - points * chunk, high - low)
        i, src, lane, length, ahead = part
        start = (lane + 32 * ahead) % ring
        add(("eta", i), src, start, length)
        gap = start + length
    body = points // LANES * LANES
    for i in range(NODES):
        low, high = max(i * slab, points * chunk), min((i + 1) * slab, points * (chunk + 1))
        cut = points * chunk + body
        if low < min(high, cut):
            segments.append(
                (("xi", i), low - i * slab, RING_TILES * LANES + low - points * chunk, min(high, cut) - low)
            )
        if max(low, cut) < high:
            low = max(low, cut)
            add(("xi", i), low - i * slab, gap + low - cut, high - low)
    return segments, gap


def chunk_eta_bands(chunk, points):
    bands = eta_bands((points - 2 * NODES * 32) * chunk, CHUNK_TILES * LANES, points)
    part = end_part(chunk, points)
    if part is not None:
        _, _, lane, length, ahead = part
        bands[:, lane : lane + length] = 0.0
        bands[ahead + 8, lane : lane + length] = 1.0
    return bands


def return_segments(points):
    slab = NODES * 32
    body = points // LANES * LANES
    plans = []
    for i in range(NODES):
        segments = []
        for chunk in range(4):
            for name, start, stop in (("body", 0, body), ("tail", body, points)):
                low = max(i * slab, chunk * points + start)
                high = min((i + 1) * slab, chunk * points + stop)
                if low < high:
                    segments.append(((name, chunk), low - chunk * points - start, low - i * slab, high - low))
        plans.append(tile_plan(segments, SLAB_TILES))
    return plans


def lane_ids(rows):
    return lax.broadcasted_iota(jnp.int32, (rows, LANES), 1)


def turn(value, shift):
    return value if shift % LANES == 0 else pltpu.roll(value, shift % LANES, 1)


def turner(load):
    made = {}

    def turned(source, tile, shift):
        key = source, tile, shift
        if key not in made:
            made[key] = turn(load(source, tile), shift)
        return made[key]

    return turned


def pieced(pieces, turned, lanes):
    total = None
    for source, tile, shift, low, size in pieces:
        value = turned(source, tile, shift)
        if total is None:
            total = value
        elif low + size == LANES:
            total = jnp.where(lanes >= low, value, total)
        else:
            total = jnp.where((lanes >= low) & (lanes < low + size), value, total)
    return total


def aligned(index, unit):
    return index if isinstance(index, int) else pl.multiple_of(index, unit)


def group_rows(g):
    return pl.ds(aligned(g * GROUP, GROUP), GROUP)


def tile_at(ref, lead, rows, tile):
    return ref[(*lead, rows, pl.ds(tile * LANES, LANES))]


def along_i(tiles):
    return [
        sum(tiles[i] * float(DERIV[a, i]) for i in range(1, NODES)) + tiles[0] * float(DERIV[a, 0])
        for a in range(NODES)
    ]


def turned_tiles(tiles, lanes):
    out = [tiles]
    for s in range(1, 4):
        spun = [pltpu.roll(t, LANES - 32 * s, 1) for t in tiles]
        out.append(
            [
                jnp.where(lanes < LANES - 32 * s, spun[t], spun[(t + 1) % len(tiles)])
                for t in range(len(tiles))
            ]
        )
    return out


def along_j(turned, ring, tile, band, used):
    total = None
    for d in used:
        term = turned[d % 4][(tile + d // 4) % ring] * band(d)
        total = term if total is None else total + term
    return total


def make_xi(groups, state, xi):
    for g in groups:
        rows = group_rows(g)
        for t in range(SLAB_TILES):
            for a, value in enumerate(along_i([tile_at(state, (i,), rows, t) for i in range(NODES)])):
                xi[a, rows, pl.ds(t * LANES, LANES)] = value


def used_offsets(tile):
    nodes = range(4 * tile, min(4 * tile + 4, NODES))
    return [d for d in range(-8, 9) if any(0 <= j + d < NODES for j in nodes)]


def make_buffer(plan, groups, state, xi, bands, put):
    lanes = lane_ids(GROUP)
    for g in groups:
        rows = group_rows(g)

        def load(source, tile, rows=rows):
            name, i = source
            if name != "eta":
                return tile_at(state if name == "state" else xi, (i,), rows, tile)
            turned = turned_tiles([tile_at(state, (i,), rows, t) for t in range(SLAB_TILES)], lanes)
            return along_j(
                turned, SLAB_TILES, tile, lambda d: tile_at(bands, (), pl.ds(d + 8, 1), tile), used_offsets(tile)
            )

        turned = turner(load)
        for t, pieces in enumerate(plan):
            value = pieced(pieces, turned, lanes) if pieces else jnp.zeros((GROUP, LANES), jnp.float32)
            put(rows, t, value)


def make_first(plans, state, xi, bands, out):
    target = lax.axis_index("plane") ^ PARTNERS[1]

    def put(rows, t, value):
        out[rows, pl.ds(t * LANES, LANES)] = value

    for chunk, plan in enumerate(plans):
        groups = range(state.shape[1] // GROUP)
        pl.when(target == chunk)(
            functools.partial(make_buffer, plan[:BASE_TILES], groups, state, xi, bands, put)
        )


def rest_kernel(plans, state, xi, bands, out0, out2, out3, extra1, extra2, extra3, staged):
    me = lax.axis_index("plane")
    for chunk, plan in enumerate(plans):

        def put(rows, t, value, chunk=chunk):
            staged[chunk, rows, pl.ds(t * LANES, LANES)] = value

        make_buffer(plan, range(state.shape[1] // GROUP), state, xi, bands, put)
    base, last = pl.ds(0, BASE_TILES * LANES), pl.ds(BASE_TILES * LANES, LANES)
    out0[...] = staged[me ^ PARTNERS[0]]
    out2[...] = staged[me ^ PARTNERS[2], :, base]
    out3[...] = staged[me ^ PARTNERS[3], :, base]
    for k, extra in ((1, extra1), (2, extra2), (3, extra3)):
        extra[...] = staged[me ^ PARTNERS[k], :, last]


def first_kernel(plans, adjoint, far_bands, state, xi, out, taken, sems, bands):
    comps, local = taken.shape[0], taken.shape[3]

    def copies(c):
        for n in range(3):
            part = pl.ds(3 * n, 3)
            yield pltpu.make_async_copy(adjoint.at[c, part], taken.at[c, part], sems.at[3 * c + n])

    for c in range(comps):
        for copy in copies(c):
            copy.start()
    fetch = pltpu.make_async_copy(far_bands, bands, sems.at[3 * comps])
    fetch.start()

    for c in range(comps):
        for copy in copies(c):
            copy.wait()
        rows = pl.ds(c * local, local)
        for i in range(NODES):
            for t in range(SLAB_TILES):
                parts = [taken[c, i, j] for j in range(4 * t, min(4 * t + 4, NODES))]
                parts += [jnp.zeros_like(parts[0])] * (4 - len(parts))
                state[i, rows, pl.ds(t * LANES, LANES)] = jnp.concatenate(parts, axis=1)
        make_xi(range(c * local // GROUP, (c + 1) * local // GROUP), state, xi)
    fetch.wait()
    make_first(plans, state, xi, bands, out)


def metric_rows(metric):
    wide = jnp.concatenate([metric[...]] * (LANES // metric.shape[1]), axis=1)
    return jnp.concatenate([wide, wide], axis=0)


def flow_kernel(points, step_index, flow, metric, out, flat):
    me = lax.axis_index("plane")
    lanes, subs = lane_ids(8), lax.broadcasted_iota(jnp.int32, (8, LANES), 0)
    shift = lax.rem(LANES - lax.rem(me * points, LANES), LANES)
    turned = pltpu.roll(metric_rows(metric), shift, 1)
    ahead = pl.program_id(0) == 0
    first_first = jnp.where(ahead, turned[0:1], 1.0)
    first_second = jnp.where(ahead, turned[1:2], 0.0)
    second_first = jnp.where(ahead, turned[2:3], 0.0)
    second_second = jnp.where(ahead, turned[3:4], 1.0)
    per_sixteen = 16 * points // LANES
    last = CHUNK_TILES - 1

    for f in range(2):
        flat[f] = flow[f, step_index].reshape(flat.shape[1:])

    for half in range(2):
        moved = (lanes + 64 * half + 8 * subs) & (LANES - 1)
        kept = lanes < LANES - 64 * half - 8 * subs

        def some_rows(h, _, half=half, moved=moved, kept=kept):
            rows = pl.ds(pl.multiple_of(16 * h + 8 * half, 8), 8)

            def field(f):
                spun = []
                for k in range(CHUNK_TILES):
                    start = per_sixteen * h + 40 * half + k
                    spun.append(pick(flat[f, pl.ds(start, 8, stride=5), :], moved))
                return [jnp.where(kept, spun[k], spun[k + 1]) for k in range(last)] + [spun[last]]

            for t, (one, two) in enumerate(zip(field(0), field(1))):
                out[0, rows, pl.ds(t * LANES, LANES)] = one * first_first + two * first_second
                out[1, rows, pl.ds(t * LANES, LANES)] = one * second_first + two * second_second
            return 0

        lax.fori_loop(0, MODES // 16, some_rows, 0)


def tables_kernel(edges, flags, table, square):
    blocks, _, capacity = edges.shape
    lanes = lane_ids(capacity)
    slots = lax.broadcasted_iota(jnp.int32, (capacity, LANES), 0)
    here = slots == lax.rem(lanes, capacity)
    flag = jnp.zeros((1, LANES), jnp.int32)
    count = jnp.zeros((1, LANES), jnp.int32)
    table[...] = jnp.zeros(table.shape, jnp.int32)
    square[...] = jnp.zeros(square.shape, jnp.float32)
    for o in range(blocks):
        square[o : o + 1, 0:capacity] = edges[o].astype(jnp.float32)
        square[blocks + o : blocks + o + 1, 0:capacity] = flags[o].astype(jnp.float32)
    columns = square[...].T[0:capacity].astype(jnp.int32)
    for o in range(blocks):
        column = jnp.broadcast_to(columns[:, o : o + 1], (capacity, LANES))
        held = column == lanes

        def summed(mask, value):
            return jnp.sum(jnp.where(mask, value, 0), axis=0, keepdims=True)

        table[o : o + 1, :] = summed(here, jnp.maximum(column, 0))
        table[5 + o : 6 + o, :] = summed(held, slots)
        present = summed(held, jnp.ones_like(slots))
        table[10 + o : 11 + o, :] = present
        flag += summed(held, jnp.broadcast_to(columns[:, blocks + o : blocks + o + 1], (capacity, LANES)))
        count += present
        if o == blocks // 2:
            partner = slots + 1 - 2 * lax.rem(slots, 2)
            slot_of = jnp.broadcast_to(summed(held, partner), (capacity, LANES))
            partner_edge = summed(slots == slot_of, jnp.maximum(column, 0))
            table[16:17, :] = jnp.where(present > 0, partner_edge, 0)
    table[15:16, :] = flag
    table[17:18, :] = count


def diffuse_kernel(state, metric, bands, local_sum, first, second):
    me = lax.axis_index("plane")
    rows_total = state.shape[1]
    lanes = lane_ids(8)
    local = rows_total // 3
    wide = metric_rows(metric)
    xi_x, xi_y, eta_x, eta_y = (wide[r : r + 1] for r in range(4))
    g_ii = xi_x * xi_x + xi_y * xi_y
    g_ij = xi_x * eta_x + xi_y * eta_y
    g_jj = eta_x * eta_x + eta_y * eta_y
    def eta_of(tiles):
        turned = turned_tiles(tiles, lanes)
        return [
            along_j(turned, SLAB_TILES, t, lambda d, t=t: tile_at(bands, (), pl.ds(d + 8, 1), t), used_offsets(t))
            for t in range(SLAB_TILES)
        ]

    def some_rows(g, _):
        rows = pl.ds(pl.multiple_of(g * 8, 8), 8)
        first_mode = me * local + lax.rem(g * 8, local)
        wave = ((first_mode + lax.broadcasted_iota(jnp.int32, (8, LANES), 0) + 1) // 2).astype(jnp.float32)
        wave_sq = wave * wave
        for t in range(SLAB_TILES):
            for a, value in enumerate(along_i([tile_at(state, (i,), rows, t) for i in range(NODES)])):
                first[a, :, pl.ds(t * LANES, LANES)] = value
        for i in range(NODES):
            eta = eta_of([tile_at(state, (i,), rows, t) for t in range(SLAB_TILES)])
            mixed = []
            for t in range(SLAB_TILES):
                xi = first[i, :, pl.ds(t * LANES, LANES)]
                first[i, :, pl.ds(t * LANES, LANES)] = g_ii * xi + g_ij * eta[t]
                mixed.append(g_ij * xi + g_jj * eta[t])
            for t, value in enumerate(eta_of(mixed)):
                second[i, :, pl.ds(t * LANES, LANES)] = value
        for t in range(SLAB_TILES):
            tiles = [first[i, :, pl.ds(t * LANES, LANES)] for i in range(NODES)]
            for a, value in enumerate(along_i(tiles)):
                now = tile_at(state, (a,), rows, t)
                laplacian = value + second[a, :, pl.ds(t * LANES, LANES)]
                local_sum[a, rows, pl.ds(t * LANES, LANES)] = now + STEP_VISC * (laplacian - wave_sq * now)
        return 0

    lax.fori_loop(0, rows_total // 8, some_rows, 0)


def halves(value):
    high = value.astype(jnp.bfloat16)
    return high, (value - high.astype(jnp.float32)).astype(jnp.bfloat16)


def fields_kernel(gaps, split, source, *refs):
    extra, bands = (refs[0], refs[1]) if split else (None, refs[0])
    fields = refs[-1]
    me = lax.axis_index("plane")
    rows_total = source.shape[0]
    local = fields.shape[2]
    lanes = lane_ids(GROUP)
    gap = sum(jnp.where(me == b, g, 0) for b, g in enumerate(gaps))
    gap_late, gap_shift = gap >= RING_TILES * LANES, lax.rem(LANES - lax.rem(gap, LANES), LANES)

    for g in range(rows_total // GROUP):
        rows = group_rows(g)
        c = g * GROUP // local
        target = pl.ds(g * GROUP % local, GROUP)
        tiles = [tile_at(source, (), rows, t) for t in range(RING_TILES)]
        tiles.append(extra[rows, :] if split else tile_at(source, (), rows, BASE_TILES))
        turned = turned_tiles(tiles, lanes)
        for t in range(CHUNK_TILES):
            at = pl.ds(t * LANES, LANES)
            fields[0, c, target, at] = tiles[t]
            fields[2, c, target, at] = along_j(
                turned, STATE_TILES, t, lambda d, at=at: bands[me, pl.ds(d + 8, 1), at], range(-8, 9)
            )
        for t in range(BODY_TILES):
            fields[1, c, target, pl.ds(t * LANES, LANES)] = tile_at(source, (), rows, RING_TILES + t)
        tail = jnp.where(gap_late, tiles[RING_TILES], tiles[RING_TILES - 1])
        fields[1, c, target, pl.ds(BODY_TILES * LANES, LANES)] = pltpu.roll(tail, gap_shift, 1)


def span_dot(a, value):
    high, low = halves(value)
    stacked = jnp.concatenate([high, low, high], axis=0)
    return jnp.dot(a, stacked, preferred_element_type=jnp.float32)


LANE_PARTS = [pl.ds(first, 2 * LANES) for first in range(0, CHUNK_TILES * LANES, 2 * LANES)]


def products(sources, flow, both, part):
    def field(kind, c):
        return jnp.concatenate([fields[kind, c, :, part] for fields in sources], axis=0)

    comps, basis = sources[0].shape[1], both[:MODES]
    values, sums = [], []
    for c in range(comps):
        out = span_dot(both, field(0, c))
        values.append(out[:MODES])
        along_x = flow[0, :, part] * span_dot(basis, field(1, c))
        along_y = flow[1, :, part] * span_dot(basis, field(2, c))
        sums.append(along_x + along_y + flow[2, :, part] * out[MODES:])
    for c in range(comps):
        taken = values[0] * flow[3 + c, :, part]
        taken += values[1] * flow[6 + c, :, part]
        taken += values[2] * flow[9 + c, :, part]
        yield c, sums[c] - taken


def early_kernel(fields0, fields1, fields2, flow, to_span, early):
    both = to_span[lax.axis_index("plane")]
    for part in LANE_PARTS:
        for c, product in products((fields0, fields1, fields2), flow, both, part):
            early[c, :, part] = product


def advect_kernel(fields3, early, flow, to_span, to_modes, *refs):
    *outs, stacked = refs
    me = lax.axis_index("plane")
    both, back = to_span[me], to_modes[me]
    lanes = lane_ids(GROUP)
    local = MODES // len(outs)
    for part in LANE_PARTS:
        for c, product in products((fields3,), flow, both, part):
            high, low = halves(product + early[c, :, part])
            stacked[c, :, part] = jnp.concatenate([high, low, high], axis=0)
    tails = [None] * len(outs)
    for c in range(stacked.shape[0]):
        for n, part in enumerate(LANE_PARTS):
            result = jnp.dot(back, stacked[c, :, part], preferred_element_type=jnp.float32)
            for k, out in enumerate(outs):
                for half in range(local // GROUP):
                    g = c * (local // GROUP) + half
                    piece = result[k * local + half * GROUP : k * local + (half + 1) * GROUP]
                    first = (BODY_TILES * g + 2 * n) * LANES
                    if n < len(LANE_PARTS) - 1:
                        out[:, pl.ds(first, 2 * LANES)] = piece
                        continue
                    out[:, pl.ds(first, LANES)] = piece[:, :LANES]
                    tail = turn(piece[:, LANES:], 8 * g)
                    tails[k] = tail if g == 0 else jnp.where(lanes >= 8 * g, tail, tails[k])
    for out, tail in zip(outs, tails):
        out[:, pl.ds((BACK_TILES - 1) * LANES, LANES)] = tail


def trace_blocks(me):
    odd, late = lax.rem(me, 2), lax.rem(me, 4) // 2
    return 4 * late, 1 + 2 * odd, 4 - 4 * late, 3 - 2 * odd


def trace_partner(me, matching, size):
    step, start = ((2, 2), (1, 1), (2, 0), (1, 0))[matching]
    return (((me + start) ^ step) - start) % size


def update_kernel(plans, in0, in1, in2, in3, local_sum, table, updated, traces, out0, out1, out2, out3, chunks):
    me = lax.axis_index("plane")
    rows_total = local_sum.shape[1]
    last = NODES - 1
    lanes = lane_ids(8)
    for step, source in zip(PARTNERS, (in0, in1, in2, in3)):
        chunks[me ^ step] = source[...]

    trace_plans = [
        tile_plan([(k, 0, 0, 32), (last, 32 * k, 32, 32), (k, 256, 64, 32), (0, 32 * k, 96, 32)], 1)[0]
        for k in range(NODES)
    ]

    blocks = trace_blocks(lax.axis_index("dom"))

    def wide(row):
        return jnp.broadcast_to(table[pl.ds(row, 1), :], (8, LANES))

    turned_round = wide(15) == 1
    slot_edges = [wide(o) for o in blocks]
    groups = range(rows_total // GROUP)
    for g in groups:
        rows = group_rows(g)

        def load(source, tile, g=g):
            if source[0] == "tail":
                return turn(tile_at(chunks, (source[1],), slice(None), BACK_TILES - 1), -8 * g)
            return tile_at(chunks, (source[1],), slice(None), BODY_TILES * g + tile)

        turned = turner(load)
        for i in range(NODES):
            for t in range(SLAB_TILES):
                value = pieced(plans[i][t], turned, lanes)
                updated[i, rows, pl.ds(t * LANES, LANES)] = (
                    tile_at(local_sum, (i,), rows, t) + step_size * value
                )
    for g in groups:
        rows = group_rows(g)
        edges = turner(lambda i, tile, rows=rows: tile_at(updated, (i,), rows, tile))
        raw = [pieced(plan, edges, lanes) for plan in trace_plans]
        for k in range(NODES):
            traces[k, rows, :] = jnp.where(turned_round, raw[last - k], raw[k])
    for g in groups:
        rows = group_rows(g)
        for slot_edge, out in zip(slot_edges, (out0, out1, out2, out3)):
            for t in range(2):
                total = None
                for k in range(5 * t, min(5 * t + 5, NODES)):
                    value = pick(traces[k, rows, :], slot_edge)
                    total = value if total is None else jnp.where(lanes >= 24 * (k - 5 * t), value, total)
                out[rows, pl.ds(t * LANES, LANES)] = total


def own_kernel(table, traces, own):
    partner = jnp.broadcast_to(table[16:17, :], (GROUP, LANES))
    present = jnp.broadcast_to(table[12:13, :], (GROUP, LANES)) > 0
    for g in range(traces.shape[1] // GROUP):
        rows = group_rows(g)
        for k in range(NODES):
            own[k, rows, :] = jnp.where(present, pick(traces[k, rows, :], partner), 0.0)


def pick(value, index):
    return jnp.take_along_axis(value, index, axis=1, mode="promise_in_bounds")


def join_edges(table, updated, own, came, sums, put):
    rows_total = updated.shape[1]
    last = NODES - 1
    lanes = lane_ids(8)
    blocks = trace_blocks(lax.axis_index("dom"))

    def wide(row):
        return jnp.broadcast_to(table[pl.ds(row, 1), :], (8, LANES))

    share = wide(17).astype(jnp.float32)
    quarter = lanes // 32
    has = [wide(10 + o) > 0 for o in blocks]
    slots = [wide(5 + o) for o in blocks]

    def spread(values, at, t):
        value = None
        for k in range(4 * t, min(4 * t + 4, NODES)):
            moved = turn(values[k], 32 * (k - 4 * t - at))
            value = jnp.where(quarter == k - 4 * t, moved, 0.0 if value is None else value)
        return value

    def edge_parts(values, i, t):
        parts = []
        if t == 0:
            parts.append(jnp.where(quarter == 0, values[i], 0.0))
        if i == last:
            parts.append(spread(values, 1, t))
        if t == 2:
            parts.append(jnp.where(quarter == 0, turn(values[i], -64), 0.0))
        if i == 0:
            parts.append(spread(values, 3, t))
        return parts

    shares, scale = [share] * NODES, {}
    for i in (0, 1, last):
        for t in range(SLAB_TILES):
            parts = edge_parts(shares, i, t)
            if parts:
                scale[i, t] = 1.0 / (1.0 + sum(parts[1:], parts[0]))

    groups = range(rows_total // GROUP)
    for g in groups:
        rows = group_rows(g)
        for k in range(NODES):
            total = own[k, rows, :]
            for slot, there, source in zip(slots, has, came):
                value = pick(tile_at(source, (), rows, k // 5), slot + 24 * (k % 5))
                total = jnp.where(there, value, total)
            sums[k, rows, :] = total
    for g in groups:
        rows = group_rows(g)
        values = [sums[k, rows, :] for k in range(NODES)]
        for i in range(NODES):
            for t in range(SLAB_TILES):
                parts = edge_parts(values, i, t)
                if parts:
                    total = tile_at(updated, (i,), rows, t)
                    for part in parts:
                        total += part
                    put(g, i, t, total * scale[i if i in (0, last) else 1, t])


def next_kernel(plans, table, updated, own, r0, r1, r2, r3, bands, state, xi, out, sums):
    def put(g, i, t, value):
        state[i, group_rows(g), pl.ds(t * LANES, LANES)] = value

    for i in range(1, NODES - 1):
        state[i, :, pl.ds(LANES, LANES)] = updated[i, :, pl.ds(LANES, LANES)]
    join_edges(table, updated, own, (r0, r1, r2, r3), sums, put)
    make_xi(range(updated.shape[1] // GROUP), state, xi)
    make_first(plans, state, xi, bands, out)


def last_kernel(table, updated, own, r0, r1, r2, r3, out, state, sums, given, sems):
    comps, local, elements = given.shape[0], given.shape[3], given.shape[4]

    def put(g, i, t, value):
        state[i, group_rows(g), pl.ds(t * LANES, LANES)] = value

    join_edges(table, updated, own, (r0, r1, r2, r3), sums, put)
    copies = []
    for i in range(NODES):
        for c in range(comps):
            rows = pl.ds(c * local, local)
            for t in range(SLAB_TILES):
                joined = t != 1 or i in (0, NODES - 1)
                tile = tile_at(state if joined else updated, (i,), rows, t)
                for q in range(min(4, NODES - 4 * t)):
                    given[c, i, 4 * t + q] = turn(tile, -32 * q)[:, :elements]
        copies.append(pltpu.make_async_copy(given.at[:, i], out.at[:, i], sems.at[i]))
        copies[-1].start()
    for copy in copies:
        copy.wait()


def f32(*shape):
    return jax.ShapeDtypeStruct(shape, jnp.float32)


def kernel_call(body, outs, scratch, flops, moved, **more):
    return pl.pallas_call(
        body,
        out_shape=outs,
        scratch_shapes=scratch,
        compiler_params=pltpu.CompilerParams(vmem_limit_bytes=16 * 1024 * 1024),
        cost_estimate=pl.CostEstimate(flops=flops, bytes_accessed=moved, transcendentals=0),
        **more,
    )


def swapped(buffers):
    return [buffers[0]] + [swap(buffer, step) for buffer, step in zip(buffers[1:], PARTNERS[1:])]


def swap(buffer, step, wanted=range(4)):
    return lax.ppermute(buffer, "plane", sorted((i ^ step, i) for i in wanted))


def packed_shards(adjoint, metric, base_flow, edge_list, flips):
    comps, local, nodes, _, elements = adjoint.shape
    planes = MODES // local
    points = nodes * nodes * elements // planes
    rows_total = comps * local
    partitions = lax.axis_size("dom")
    state_shape = (nodes, rows_total, SLAB_TILES * LANES)

    layouts = [send_segments(chunk, points) for chunk in range(planes)]
    plans = [tile_plan(segments, SEND_TILES) for segments, _ in layouts]
    gaps = [gap for _, gap in layouts]
    back_plans = return_segments(points)
    to_span, to_span_last, to_modes = span_weights(planes)
    slab_bands = eta_bands(0, SLAB_TILES * LANES, nodes * elements)
    middle = [chunk for chunk, plan in enumerate(plans) if plan[-1]]
    chunk_bands = np.stack([chunk_eta_bands(b, points) for b in range(planes)])

    in_hbm, vmem = (pl.BlockSpec(memory_space=space) for space in (pltpu.HBM, pltpu.VMEM))
    buffer, base, extra = (f32(rows_total, tiles * LANES) for tiles in (SEND_TILES, BASE_TILES, 1))
    row_copies = [
        pltpu.VMEM((comps, nodes, nodes, local, elements), jnp.float32),
        pltpu.SemaphoreType.DMA((nodes + 1,)),
    ]
    edge_scratch = pltpu.VMEM((nodes, rows_total, LANES), jnp.float32)

    def forward(state, xi, first):
        own, second, third, *extras = kernel_call(
            functools.partial(rest_kernel, plans),
            [buffer, base, base, extra, extra, extra],
            [pltpu.VMEM((planes, *buffer.shape), jnp.float32)],
            10**6,
            2 * 10**6,
        )(state, xi, slab_bands)
        came = swapped([own, first, second, third])
        late = [swap(part, step, middle) for part, step in zip(extras, PARTNERS[1:])]
        return [(own,), *zip(came[1:], late)]

    in_rows = pltpu.with_memory_space_constraint(adjoint.transpose(0, 2, 3, 1, 4), pltpu.HBM)
    state, *prepared = kernel_call(
        functools.partial(first_kernel, plans),
        [f32(*state_shape), f32(*state_shape), base],
        row_copies + [pltpu.VMEM(slab_bands.shape, jnp.float32)],
        4 * 10**6,
        4 * 10**6,
        in_specs=[in_hbm, in_hbm],
    )(in_rows, pltpu.with_memory_space_constraint(jnp.asarray(slab_bands), pltpu.HBM))
    incoming = forward(state, *prepared)
    whole, two_fields = (12, MODES, CHUNK_TILES * LANES), (2, MODES, CHUNK_TILES * LANES)
    lay = base_flow.transpose(1, 0, 2)
    table = kernel_call(
        tables_kernel,
        jax.ShapeDtypeStruct((24, LANES), jnp.int32),
        [pltpu.VMEM((LANES, LANES), jnp.float32)],
        10**5,
        10**5,
    )(edge_list.transpose(1, 0, 2), flips.transpose(1, 0, 2))

    for step_index in range(STEPS):
        flow = kernel_call(
            functools.partial(flow_kernel, points, step_index),
            f32(*whole),
            [pltpu.VMEM((2, lay.shape[2] // LANES, LANES), jnp.float32)],
            2 * 10**6,
            7 * 10**6,
            grid=(6,),
            in_specs=[
                pl.BlockSpec((2, *lay.shape[1:]), lambda pair: (pair, 0, 0)),
                pl.BlockSpec(metric.shape, lambda pair: (0, 0)),
            ],
            out_specs=pl.BlockSpec(two_fields, lambda pair: (pair, 0, 0)),
        )(lay, metric)
        fields = [None] * planes
        before = []
        for k in FIELDS_ORDER:
            parts = incoming[k]
            fields[k] = kernel_call(
                functools.partial(fields_kernel, gaps, len(parts) > 1),
                f32(3, comps, local, CHUNK_TILES * LANES),
                [],
                2 * 10**6,
                10**6,
                in_specs=[vmem] * (len(parts) + 1) + [pl.BlockSpec(memory_space=pl.ANY)] * len(before),
            )(*parts, chunk_bands, *before)
            before = [fields[k]] if k > 0 else []
        early = kernel_call(
            early_kernel, f32(comps, MODES, CHUNK_TILES * LANES), [], 50 * 10**6, 5 * 10**6
        )(*fields[:-1], flow, to_span)
        returning = kernel_call(
            advect_kernel,
            [f32(GROUP, BACK_TILES * LANES)] * planes,
            [pltpu.VMEM((comps, 3 * MODES, CHUNK_TILES * LANES), jnp.bfloat16)],
            30 * 10**6,
            5 * 10**6,
        )(fields[-1], early, flow, to_span_last, to_modes)
        local_sum = kernel_call(
            diffuse_kernel,
            f32(*state_shape),
            [pltpu.VMEM((nodes, GROUP, SLAB_TILES * LANES), jnp.float32)] * 2,
            12 * 10**6,
            2 * 10**6,
        )(state, metric, slab_bands)
        updated, seen, *leaving = kernel_call(
            functools.partial(update_kernel, back_plans),
            [f32(*state_shape), f32(nodes, rows_total, LANES)] + [f32(rows_total, 2 * LANES)] * 4,
            [pltpu.VMEM((planes, GROUP, BACK_TILES * LANES), jnp.float32)],
            2 * 10**6,
            3 * 10**6,
        )(*swapped(returning), local_sum, table)
        traces = [
            lax.ppermute(
                buffer, "dom", [(i, trace_partner(i, matching, partitions)) for i in range(partitions)]
            )
            for matching, buffer in enumerate(leaving)
        ]
        own = kernel_call(own_kernel, f32(nodes, rows_total, LANES), [], 10**5, 10**6)(table, seen)
        if step_index + 1 < STEPS:
            state, *prepared = kernel_call(
                functools.partial(next_kernel, plans),
                [f32(*state_shape), f32(*state_shape), base],
                [edge_scratch],
                6 * 10**6,
                4 * 10**6,
            )(table, updated, own, *traces, slab_bands)
            incoming = forward(state, *prepared)
        else:
            result = kernel_call(
                last_kernel,
                f32(comps, nodes, nodes, local, elements),
                [pltpu.VMEM(state_shape, jnp.float32), edge_scratch, *row_copies],
                2 * 10**6,
                3 * 10**6,
                out_specs=in_hbm,
            )(table, updated, own, *traces)
    return result.transpose(0, 3, 1, 2, 4)


def plain_shards(adjoint, metric, base_flow, edge_list, flips):
    local_modes = adjoint.shape[1]
    deriv_table = cheb_table(adjoint.shape[2])
    span_basis, span_slope, forward, wave_sq = span_tables(MODES)
    wave_local = lax.dynamic_slice_in_dim(
        wave_sq, lax.axis_index("plane") * local_modes, local_modes, 0
    )
    adjoint_state = adjoint
    for step_index in range(STEPS):
        base_now = base_flow[step_index].reshape(12, MODES, -1)
        adjoint_state = advance(
            adjoint_state,
            metric,
            base_now,
            edge_list[0],
            flips[0],
            deriv_table,
            span_basis,
            span_slope,
            forward,
            wave_local,
        )
    return adjoint_state


def shards(adjoint, metric, base_flow, edge_list, flips):
    if adjoint.shape[1:] == (MODES // 4, NODES, NODES, 32) and (
        edge_list.shape[1:] == (5, 24) and lax.axis_size("dom") % 4 == 0
    ):
        return packed_shards(adjoint, metric, base_flow, edge_list, flips)
    return plain_shards(adjoint, metric, base_flow, edge_list, flips)


def solution(mesh):
    placed = (
        P(None, "plane", None, None, "dom"),
        P(None, "dom"),
        P(None, None, ("dom", "plane")),
        P("dom", None, None),
        P("dom", None, None),
    )
    return jax.shard_map(
        shards,
        mesh=mesh,
        in_specs=placed,
        out_specs=P(None, "plane", None, None, "dom"),
        check_vma=False,
    )
```

```python
import functools

import jax
import jax.numpy as jnp
import numpy as np
from jax import lax
from jax.experimental import pallas as pl
from jax.experimental.pallas import tpu as pltpu
from jax.sharding import PartitionSpec as P

MODES = 64
STEPS = 2


step_size = 0.01
viscosity = 0.02


def passed_along(shard, axis, by):
    size = lax.axis_size(axis)
    return lax.ppermute(shard, axis, [(i, (i + by) % size) for i in range(size)])


def cheb_table(node_count):
    order = node_count - 1
    node_ids = jnp.arange(node_count, dtype=jnp.int32)
    node_coords = -jnp.cos(jnp.pi * node_ids.astype(jnp.float32) / order)
    weight = jnp.where((node_ids == 0) | (node_ids == order), 2.0, 1.0).astype(jnp.float32)
    parity = jnp.where((node_ids[:, None] + node_ids[None, :]) % 2 == 0, 1.0, -1.0).astype(
        jnp.float32
    )
    on_diag = node_ids[:, None] == node_ids[None, :]
    differ = jnp.where(on_diag, 1.0, node_coords[:, None] - node_coords[None, :])
    off_diag = jnp.where(on_diag, 0.0, weight[:, None] / weight[None, :] * parity / differ)
    return off_diag - jnp.diag(jnp.sum(off_diag, axis=1))


def span_tables(modes):
    mode_ids = jnp.arange(modes, dtype=jnp.int32)
    wavenumber = (mode_ids + 1) // 2
    is_cosine = (mode_ids % 2 == 1) | (mode_ids == 0)
    span_ids = jnp.arange(modes, dtype=jnp.int32)
    phase_num = span_ids[:, None] * wavenumber[None, :] % modes
    angles = 2.0 * jnp.pi * phase_num.astype(jnp.float32) / modes
    cosines = jnp.cos(angles)
    sines = jnp.sin(angles)
    wave_f = wavenumber.astype(jnp.float32)
    span_basis = jnp.where(is_cosine[None, :], cosines, sines)
    span_slope = jnp.where(is_cosine[None, :], -wave_f[None, :] * sines, wave_f[None, :] * cosines)
    scaling = jnp.where((mode_ids == 0) | (mode_ids == modes - 1), 1.0 / modes, 2.0 / modes).astype(
        jnp.float32
    )
    forward = span_basis.T * scaling[:, None]
    return (span_basis, span_slope, forward, wave_f * wave_f)


def directional(field_data, metric, deriv_table, xi_row, eta_row):
    along_xi = jnp.einsum(
        "ai,cmije->cmaje", deriv_table, field_data, precision=lax.Precision.HIGHEST
    )
    along_eta = jnp.einsum(
        "bj,cmije->cmibe", deriv_table, field_data, precision=lax.Precision.HIGHEST
    )
    return metric[xi_row] * along_xi + metric[eta_row] * along_eta


def advect(coeffs, base_now, span_basis, span_slope, forward):
    values = jnp.einsum("nm,fmq->fnq", span_basis, coeffs, precision=lax.Precision.HIGHEST)
    along_z = jnp.einsum("nm,cmq->cnq", span_slope, coeffs[0:3], precision=lax.Precision.HIGHEST)
    products = []
    for comp in range(3):
        term = (
            base_now[0] * values[3 + comp]
            + base_now[1] * values[6 + comp]
            + base_now[2] * along_z[comp]
        )
        term = term - (
            values[0] * base_now[3 + comp]
            + values[1] * base_now[6 + comp]
            + values[2] * base_now[9 + comp]
        )
        products.append(term)
    return jnp.einsum("mn,cnq->cmq", forward, jnp.stack(products), precision=lax.Precision.HIGHEST)


def accumulate(field_data, edge_sums, counts):
    node_count = field_data.shape[2]
    last = node_count - 1
    total = field_data
    total = total.at[:, :, :, 0, :].add(edge_sums[:, :, :, 0, :])
    total = total.at[:, :, last, :, :].add(edge_sums[:, :, :, 1, :])
    total = total.at[:, :, :, last, :].add(edge_sums[:, :, :, 2, :])
    total = total.at[:, :, 0, :, :].add(edge_sums[:, :, :, 3, :])
    weight = jnp.ones((node_count, node_count, field_data.shape[4]), jnp.float32)
    weight = weight.at[:, 0, :].add(counts[0][None, :])
    weight = weight.at[last, :, :].add(counts[1][None, :])
    weight = weight.at[:, last, :].add(counts[2][None, :])
    weight = weight.at[0, :, :].add(counts[3][None, :])
    return total / weight


def assemble(field_data, edge_slots, flip_flags):
    components, local_modes, node_count, _, elements = field_data.shape
    last = node_count - 1
    row_count = components * local_modes * node_count
    traces = jnp.stack(
        [
            field_data[:, :, :, 0, :],
            field_data[:, :, last, :, :],
            field_data[:, :, :, last, :],
            field_data[:, :, 0, :, :],
        ],
        axis=3,
    )
    edge_table = traces.reshape(row_count, 4 * elements)
    blocks, capacity = edge_slots.shape
    half_span = (blocks - 1) // 2
    slot_edges = edge_slots.reshape(-1)
    occupied = (slot_edges >= 0).astype(jnp.float32)
    outgoing = jnp.take(edge_table, jnp.maximum(slot_edges, 0), axis=1) * occupied[None, :]

    def block_of(block_id):
        return outgoing[:, block_id * capacity : (block_id + 1) * capacity]

    own_pairs = (
        block_of(half_span)
        .reshape(row_count, capacity // 2, 2)[:, :, ::-1]
        .reshape(row_count, capacity)
    )
    received = {half_span: own_pairs}
    for block_id in range(blocks):
        if block_id != half_span:
            received[block_id] = passed_along(
                block_of(blocks - 1 - block_id), "dom", half_span - block_id
            )
    partners = jnp.concatenate([received[block_id] for block_id in range(blocks)], axis=1)
    shaped = partners.reshape(components * local_modes, node_count, blocks * capacity)
    shaped = (
        jnp.where(flip_flags.reshape(-1)[None, None, :] == 1, shaped[:, ::-1, :], shaped)
        * occupied[None, None, :]
    )
    onehot = (slot_edges[:, None] == jnp.arange(4 * elements, dtype=jnp.int32)[None, :]).astype(
        jnp.float32
    )
    edge_sums = jnp.dot(
        shaped.reshape(row_count, blocks * capacity), onehot, precision=lax.Precision.HIGHEST
    )
    edge_sums = edge_sums.reshape(components, local_modes, node_count, 4, elements)
    counts = jnp.sum(onehot, axis=0).reshape(4, elements)
    return accumulate(field_data, edge_sums, counts)


def advance(
    adjoint_state,
    metric,
    base_now,
    edge_slots,
    flip_flags,
    deriv_table,
    span_basis,
    span_slope,
    forward,
    wave_local,
):
    components, local_modes, node_count, _, elements = adjoint_state.shape
    points = node_count * node_count * elements
    grad_x = directional(adjoint_state, metric, deriv_table, 0, 2)
    grad_y = directional(adjoint_state, metric, deriv_table, 1, 3)
    stacked = jnp.concatenate([adjoint_state, grad_x, grad_y], axis=0).reshape(
        9, local_modes, points
    )
    gathered = lax.all_to_all(stacked, "plane", split_axis=2, concat_axis=1, tiled=True)
    advective = advect(gathered, base_now, span_basis, span_slope, forward)
    returned = lax.all_to_all(advective, "plane", split_axis=1, concat_axis=2, tiled=True).reshape(
        adjoint_state.shape
    )
    laplacian = directional(grad_x, metric, deriv_table, 0, 2) + directional(
        grad_y, metric, deriv_table, 1, 3
    )
    updated = adjoint_state + step_size * (
        returned + viscosity * (laplacian - wave_local[None, :, None, None, None] * adjoint_state)
    )
    return assemble(updated, edge_slots, flip_flags)


NODES = 9
LANES = 128
SLAB_TILES = 3
STATE_TILES = 7
RING_TILES = 6
BASE_TILES = 11
SEND_TILES = 12
CHUNK_TILES = 6
BODY_TILES = 5
BACK_TILES = 31
GROUP = 8
PARTNERS = (0, 2, 1, 3)
FIELDS_ORDER = (0, 1, 2, 3)
STEP_VISC = step_size * viscosity


def cheb_numbers():
    order = NODES - 1
    coords = -np.cos(np.pi * np.arange(NODES) / order)
    weight = np.ones(NODES)
    weight[0] = weight[-1] = 2.0
    table = np.zeros((NODES, NODES))
    for a in range(NODES):
        for i in range(NODES):
            if a != i:
                table[a, i] = weight[a] / weight[i] * (-1.0) ** (a + i) / (coords[a] - coords[i])
    return table - np.diag(table.sum(axis=1))


DERIV = cheb_numbers()


def span_numbers():
    modes = np.arange(MODES)
    wave = (modes + 1) // 2
    is_cosine = (modes % 2 == 1) | (modes == 0)
    angles = 2.0 * np.pi * (np.arange(MODES)[:, None] * wave[None, :] % MODES) / MODES
    cosines, sines = np.cos(angles), np.sin(angles)
    basis = np.where(is_cosine, cosines, sines)
    slope = np.where(is_cosine, -wave * sines, wave * cosines)
    scaling = np.where((modes == 0) | (modes == MODES - 1), 1.0 / MODES, 2.0 / MODES)
    return basis, slope, basis.T * scaling[:, None]


def in_two(table):
    table = table.astype(np.float32)
    high = table.astype(jnp.bfloat16)
    low = (table - high.astype(np.float32)).astype(jnp.bfloat16)
    return high, low


def span_weights(planes):
    basis, slope, forward = span_numbers()
    local = MODES // planes
    to_span, to_span_last, to_modes = [], [], []
    for me in range(planes):
        came = np.concatenate([(me ^ step) * local + np.arange(local) for step in PARTNERS])
        high, low = in_two(np.concatenate([basis, slope])[:, came])
        early, last = slice(0, MODES - local), slice(MODES - local, MODES)
        for table, columns in ((to_span, early), (to_span_last, last)):
            table.append(np.concatenate([high[:, columns], high[:, columns], low[:, columns]], axis=1))
        high, low = in_two(forward[came])
        to_modes.append(np.concatenate([high, high, low], axis=1))
    return np.stack(to_span), np.stack(to_span_last), np.stack(to_modes)


def eta_bands(first_lane, lanes, count):
    bands = np.zeros((24, lanes), np.float32)
    for lane in range(count):
        j = (first_lane + lane) % 288 // 32
        for d in range(-8, 9):
            if 0 <= j + d < NODES:
                bands[d + 8, lane] = DERIV[j, j + d]
    return bands


def tile_plan(segments, tiles):
    plan = [[] for _ in range(tiles)]
    for source, src, dst, length in segments:
        done = 0
        while done < length:
            s, d = src + done, dst + done
            size = min(length - done, LANES - s % LANES, LANES - d % LANES)
            plan[d // LANES].append((source, s // LANES, (d - s) % LANES, d % LANES, size))
            done += size
    return plan


def end_part(chunk, points):
    part = points - 2 * NODES * 32
    if chunk == 0:
        return 2, 0, points - part, part, 3
    if chunk == 3:
        return 6, NODES * 32 - part, 0, part, -7
    return None


def send_segments(chunk, points):
    ring, slab = STATE_TILES * LANES, NODES * 32
    turned = (points - 2 * slab) * chunk
    part = end_part(chunk, points)
    segments = []

    def add(source, src, dst, length):
        split = RING_TILES * LANES
        if dst < split < dst + length:
            add(source, src, dst, split - dst)
            add(source, src + split - dst, split, length - split + dst)
        else:
            segments.append((source, src, dst + (BASE_TILES - RING_TILES) * LANES * (dst >= split), length))

    if part is None:
        for r in range(3):
            start = (r * slab - turned) % ring
            first = min(slab, ring - start)
            add(("state", 2 * chunk + r), 0, start, first)
            if first < slab:
                add(("state", 2 * chunk + r), first, 0, slab - first)
        gap = (3 * slab - turned) % ring
    else:
        for i in range(NODES):
            low, high = max(i * slab, points * chunk), min((i + 1) * slab, points * (chunk + 1))
            if low < high:
                add(("state", i), low - i * slab, low - points * chunk, high - low)
        i, src, lane, length, ahead = part
        start = (lane + 32 * ahead) % ring
        add(("eta", i), src, start, length)
        gap = start + length
    body = points // LANES * LANES
    for i in range(NODES):
        low, high = max(i * slab, points * chunk), min((i + 1) * slab, points * (chunk + 1))
        cut = points * chunk + body
        if low < min(high, cut):
            segments.append(
                (("xi", i), low - i * slab, RING_TILES * LANES + low - points * chunk, min(high, cut) - low)
            )
        if max(low, cut) < high:
            low = max(low, cut)
            add(("xi", i), low - i * slab, gap + low - cut, high - low)
    return segments, gap


def chunk_eta_bands(chunk, points):
    bands = eta_bands((points - 2 * NODES * 32) * chunk, CHUNK_TILES * LANES, points)
    part = end_part(chunk, points)
    if part is not None:
        _, _, lane, length, ahead = part
        bands[:, lane : lane + length] = 0.0
        bands[ahead + 8, lane : lane + length] = 1.0
    return bands


def return_segments(points):
    slab = NODES * 32
    body = points // LANES * LANES
    plans = []
    for i in range(NODES):
        segments = []
        for chunk in range(4):
            for name, start, stop in (("body", 0, body), ("tail", body, points)):
                low = max(i * slab, chunk * points + start)
                high = min((i + 1) * slab, chunk * points + stop)
                if low < high:
                    segments.append(((name, chunk), low - chunk * points - start, low - i * slab, high - low))
        plans.append(tile_plan(segments, SLAB_TILES))
    return plans


def lane_ids(rows):
    return lax.broadcasted_iota(jnp.int32, (rows, LANES), 1)


def turn(value, shift):
    return value if shift % LANES == 0 else pltpu.roll(value, shift % LANES, 1)


def turner(load):
    made = {}

    def turned(source, tile, shift):
        key = source, tile, shift
        if key not in made:
            made[key] = turn(load(source, tile), shift)
        return made[key]

    return turned


def pieced(pieces, turned, lanes):
    total = None
    for source, tile, shift, low, size in pieces:
        value = turned(source, tile, shift)
        if total is None:
            total = value
        elif low + size == LANES:
            total = jnp.where(lanes >= low, value, total)
        else:
            total = jnp.where((lanes >= low) & (lanes < low + size), value, total)
    return total


def aligned(index, unit):
    return index if isinstance(index, int) else pl.multiple_of(index, unit)


def group_rows(g):
    return pl.ds(aligned(g * GROUP, GROUP), GROUP)


def tile_at(ref, lead, rows, tile):
    return ref[(*lead, rows, pl.ds(tile * LANES, LANES))]


def along_i(tiles):
    return [
        sum(tiles[i] * float(DERIV[a, i]) for i in range(1, NODES)) + tiles[0] * float(DERIV[a, 0])
        for a in range(NODES)
    ]


def turned_tiles(tiles, lanes):
    out = [tiles]
    for s in range(1, 4):
        spun = [pltpu.roll(t, LANES - 32 * s, 1) for t in tiles]
        out.append(
            [
                jnp.where(lanes < LANES - 32 * s, spun[t], spun[(t + 1) % len(tiles)])
                for t in range(len(tiles))
            ]
        )
    return out


def along_j(turned, ring, tile, band, used):
    total = None
    for d in used:
        term = turned[d % 4][(tile + d // 4) % ring] * band(d)
        total = term if total is None else total + term
    return total


def make_xi(groups, state, xi):
    for g in groups:
        rows = group_rows(g)
        for t in range(SLAB_TILES):
            for a, value in enumerate(along_i([tile_at(state, (i,), rows, t) for i in range(NODES)])):
                xi[a, rows, pl.ds(t * LANES, LANES)] = value


def used_offsets(tile):
    nodes = range(4 * tile, min(4 * tile + 4, NODES))
    return [d for d in range(-8, 9) if any(0 <= j + d < NODES for j in nodes)]


def make_buffer(plan, groups, state, xi, bands, put):
    lanes = lane_ids(GROUP)
    for g in groups:
        rows = group_rows(g)

        def load(source, tile, rows=rows):
            name, i = source
            if name != "eta":
                return tile_at(state if name == "state" else xi, (i,), rows, tile)
            turned = turned_tiles([tile_at(state, (i,), rows, t) for t in range(SLAB_TILES)], lanes)
            return along_j(
                turned, SLAB_TILES, tile, lambda d: tile_at(bands, (), pl.ds(d + 8, 1), tile), used_offsets(tile)
            )

        turned = turner(load)
        for t, pieces in enumerate(plan):
            value = pieced(pieces, turned, lanes) if pieces else jnp.zeros((GROUP, LANES), jnp.float32)
            put(rows, t, value)


def make_first(plans, state, xi, bands, out):
    target = lax.axis_index("plane") ^ PARTNERS[1]

    def put(rows, t, value):
        out[rows, pl.ds(t * LANES, LANES)] = value

    for chunk, plan in enumerate(plans):
        groups = range(state.shape[1] // GROUP)
        pl.when(target == chunk)(functools.partial(make_buffer, plan, groups, state, xi, bands, put))


def rest_kernel(plans, state, xi, bands, out0, out2, out3, extra3, staged):
    me = lax.axis_index("plane")
    for chunk, plan in enumerate(plans):

        def put(rows, t, value, chunk=chunk):
            staged[chunk, rows, pl.ds(t * LANES, LANES)] = value

        make_buffer(plan, range(state.shape[1] // GROUP), state, xi, bands, put)
    base, last = pl.ds(0, BASE_TILES * LANES), pl.ds(BASE_TILES * LANES, LANES)
    out0[...] = staged[me ^ PARTNERS[0]]
    out2[...] = staged[me ^ PARTNERS[2]]
    out3[...] = staged[me ^ PARTNERS[3], :, base]
    extra3[...] = staged[me ^ PARTNERS[3], :, last]


def first_kernel(plans, adjoint, far_bands, state, xi, out, taken, sems, bands):
    comps, local = taken.shape[0], taken.shape[3]

    def copy(c):
        return pltpu.make_async_copy(adjoint.at[c], taken.at[c], sems.at[c])

    for c in range(comps):
        copy(c).start()
    fetch = pltpu.make_async_copy(far_bands, bands, sems.at[comps])
    fetch.start()

    for c in range(comps):
        copy(c).wait()
        rows = pl.ds(c * local, local)
        for i in range(NODES):
            for t in range(SLAB_TILES):
                parts = [taken[c, i, j] for j in range(4 * t, min(4 * t + 4, NODES))]
                parts += [jnp.zeros_like(parts[0])] * (4 - len(parts))
                state[i, rows, pl.ds(t * LANES, LANES)] = jnp.concatenate(parts, axis=1)
        make_xi(range(c * local // GROUP, (c + 1) * local // GROUP), state, xi)
    fetch.wait()
    make_first(plans, state, xi, bands, out)


def metric_rows(metric):
    wide = jnp.concatenate([metric[...]] * (LANES // metric.shape[1]), axis=1)
    return jnp.concatenate([wide, wide], axis=0)


def flow_kernel(points, flow, metric, out0, out1, flat):
    me = lax.axis_index("plane")
    lanes, subs = lane_ids(8), lax.broadcasted_iota(jnp.int32, (8, LANES), 0)
    shift = lax.rem(LANES - lax.rem(me * points, LANES), LANES)
    turned = pltpu.roll(metric_rows(metric), shift, 1)
    ahead = pl.program_id(0) == 0
    first_first = jnp.where(ahead, turned[0:1], 1.0)
    first_second = jnp.where(ahead, turned[1:2], 0.0)
    second_first = jnp.where(ahead, turned[2:3], 0.0)
    second_second = jnp.where(ahead, turned[3:4], 1.0)
    per_sixteen = 16 * points // LANES
    last = CHUNK_TILES - 1

    for f in range(2):
        for s in range(STEPS):
            flat[f, s] = flow[f, s].reshape(flat.shape[2:])

    for s, out in enumerate((out0, out1)):
        for half in range(2):
            moved = (lanes + 64 * half + 8 * subs) & (LANES - 1)
            kept = lanes < LANES - 64 * half - 8 * subs

            def some_rows(h, _, s=s, half=half, out=out, moved=moved, kept=kept):
                rows = pl.ds(pl.multiple_of(16 * h + 8 * half, 8), 8)

                def field(f):
                    spun = []
                    for k in range(CHUNK_TILES):
                        start = per_sixteen * h + 40 * half + k
                        spun.append(pick(flat[f, s, pl.ds(start, 8, stride=5), :], moved))
                    return [jnp.where(kept, spun[k], spun[k + 1]) for k in range(last)] + [spun[last]]

                for t, (one, two) in enumerate(zip(field(0), field(1))):
                    out[0, rows, pl.ds(t * LANES, LANES)] = one * first_first + two * first_second
                    out[1, rows, pl.ds(t * LANES, LANES)] = one * second_first + two * second_second
                return 0

            lax.fori_loop(0, MODES // 16, some_rows, 0)


def tables_kernel(edges, flags, table, square):
    blocks, _, capacity = edges.shape
    lanes = lane_ids(capacity)
    slots = lax.broadcasted_iota(jnp.int32, (capacity, LANES), 0)
    here = slots == lax.rem(lanes, capacity)
    flag = jnp.zeros((1, LANES), jnp.int32)
    count = jnp.zeros((1, LANES), jnp.int32)
    table[...] = jnp.zeros(table.shape, jnp.int32)
    square[...] = jnp.zeros(square.shape, jnp.float32)
    for o in range(blocks):
        square[o : o + 1, 0:capacity] = edges[o].astype(jnp.float32)
        square[blocks + o : blocks + o + 1, 0:capacity] = flags[o].astype(jnp.float32)
    columns = square[...].T[0:capacity].astype(jnp.int32)
    for o in range(blocks):
        column = jnp.broadcast_to(columns[:, o : o + 1], (capacity, LANES))
        held = column == lanes

        def summed(mask, value):
            return jnp.sum(jnp.where(mask, value, 0), axis=0, keepdims=True)

        table[o : o + 1, :] = summed(here, jnp.maximum(column, 0))
        table[5 + o : 6 + o, :] = summed(held, slots)
        present = summed(held, jnp.ones_like(slots))
        table[10 + o : 11 + o, :] = present
        flag += summed(held, jnp.broadcast_to(columns[:, blocks + o : blocks + o + 1], (capacity, LANES)))
        count += present
        if o == blocks // 2:
            partner = slots + 1 - 2 * lax.rem(slots, 2)
            slot_of = jnp.broadcast_to(summed(held, partner), (capacity, LANES))
            partner_edge = summed(slots == slot_of, jnp.maximum(column, 0))
            table[16:17, :] = jnp.where(present > 0, partner_edge, 0)
    table[15:16, :] = flag
    table[17:18, :] = count


def diffuse_kernel(state, metric, bands, local_sum, first, second):
    me = lax.axis_index("plane")
    rows_total = state.shape[1]
    lanes = lane_ids(8)
    local = rows_total // 3
    wide = metric_rows(metric)
    xi_x, xi_y, eta_x, eta_y = (wide[r : r + 1] for r in range(4))
    g_ii = xi_x * xi_x + xi_y * xi_y
    g_ij = xi_x * eta_x + xi_y * eta_y
    g_jj = eta_x * eta_x + eta_y * eta_y
    def eta_of(tiles):
        turned = turned_tiles(tiles, lanes)
        return [
            along_j(turned, SLAB_TILES, t, lambda d, t=t: tile_at(bands, (), pl.ds(d + 8, 1), t), used_offsets(t))
            for t in range(SLAB_TILES)
        ]

    def some_rows(g, _):
        rows = pl.ds(pl.multiple_of(g * 8, 8), 8)
        first_mode = me * local + lax.rem(g * 8, local)
        wave = ((first_mode + lax.broadcasted_iota(jnp.int32, (8, LANES), 0) + 1) // 2).astype(jnp.float32)
        wave_sq = wave * wave
        for t in range(SLAB_TILES):
            for a, value in enumerate(along_i([tile_at(state, (i,), rows, t) for i in range(NODES)])):
                first[a, :, pl.ds(t * LANES, LANES)] = value
        for i in range(NODES):
            eta = eta_of([tile_at(state, (i,), rows, t) for t in range(SLAB_TILES)])
            mixed = []
            for t in range(SLAB_TILES):
                xi = first[i, :, pl.ds(t * LANES, LANES)]
                first[i, :, pl.ds(t * LANES, LANES)] = g_ii * xi + g_ij * eta[t]
                mixed.append(g_ij * xi + g_jj * eta[t])
            for t, value in enumerate(eta_of(mixed)):
                second[i, :, pl.ds(t * LANES, LANES)] = value
        for t in range(SLAB_TILES):
            tiles = [first[i, :, pl.ds(t * LANES, LANES)] for i in range(NODES)]
            for a, value in enumerate(along_i(tiles)):
                now = tile_at(state, (a,), rows, t)
                laplacian = value + second[a, :, pl.ds(t * LANES, LANES)]
                local_sum[a, rows, pl.ds(t * LANES, LANES)] = now + STEP_VISC * (laplacian - wave_sq * now)
        return 0

    lax.fori_loop(0, rows_total // 8, some_rows, 0)


def halves(value):
    high = value.astype(jnp.bfloat16)
    return high, (value - high.astype(jnp.float32)).astype(jnp.bfloat16)


def fields_kernel(gaps, split, source, *refs):
    extra, bands = (refs[0], refs[1]) if split else (None, refs[0])
    fields = refs[-1]
    me = lax.axis_index("plane")
    rows_total = source.shape[0]
    local = fields.shape[2]
    lanes = lane_ids(GROUP)
    gap = sum(jnp.where(me == b, g, 0) for b, g in enumerate(gaps))
    gap_late, gap_shift = gap >= RING_TILES * LANES, lax.rem(LANES - lax.rem(gap, LANES), LANES)

    for g in range(rows_total // GROUP):
        rows = group_rows(g)
        c = g * GROUP // local
        target = pl.ds(g * GROUP % local, GROUP)
        tiles = [tile_at(source, (), rows, t) for t in range(RING_TILES)]
        tiles.append(extra[rows, :] if split else tile_at(source, (), rows, BASE_TILES))
        turned = turned_tiles(tiles, lanes)
        for t in range(CHUNK_TILES):
            at = pl.ds(t * LANES, LANES)
            fields[0, c, target, at] = tiles[t]
            fields[2, c, target, at] = along_j(
                turned, STATE_TILES, t, lambda d, at=at: bands[me, pl.ds(d + 8, 1), at], range(-8, 9)
            )
        for t in range(BODY_TILES):
            fields[1, c, target, pl.ds(t * LANES, LANES)] = tile_at(source, (), rows, RING_TILES + t)
        tail = jnp.where(gap_late, tiles[RING_TILES], tiles[RING_TILES - 1])
        fields[1, c, target, pl.ds(BODY_TILES * LANES, LANES)] = pltpu.roll(tail, gap_shift, 1)


def span_dot(a, value):
    high, low = halves(value)
    stacked = jnp.concatenate([high, low, high], axis=0)
    return jnp.dot(a, stacked, preferred_element_type=jnp.float32)


LANE_PARTS = [pl.ds(first, 2 * LANES) for first in range(0, CHUNK_TILES * LANES, 2 * LANES)]


def products(sources, flow, both, part):
    def field(kind, c):
        return jnp.concatenate([fields[kind, c, :, part] for fields in sources], axis=0)

    comps, basis = sources[0].shape[1], both[:MODES]
    values, sums = [], []
    for c in range(comps):
        out = span_dot(both, field(0, c))
        values.append(out[:MODES])
        along_x = flow[0, :, part] * span_dot(basis, field(1, c))
        along_y = flow[1, :, part] * span_dot(basis, field(2, c))
        sums.append(along_x + along_y + flow[2, :, part] * out[MODES:])
    for c in range(comps):
        taken = values[0] * flow[3 + c, :, part]
        taken += values[1] * flow[6 + c, :, part]
        taken += values[2] * flow[9 + c, :, part]
        yield c, sums[c] - taken


def early_kernel(fields0, fields1, fields2, flow, to_span, early):
    both = to_span[lax.axis_index("plane")]
    for part in LANE_PARTS:
        for c, product in products((fields0, fields1, fields2), flow, both, part):
            early[c, :, part] = product


def advect_kernel(fields3, early, flow, to_span, to_modes, *refs):
    *outs, stacked = refs
    me = lax.axis_index("plane")
    both, back = to_span[me], to_modes[me]
    lanes = lane_ids(GROUP)
    local = MODES // len(outs)
    for part in LANE_PARTS:
        for c, product in products((fields3,), flow, both, part):
            high, low = halves(product + early[c, :, part])
            stacked[c, :, part] = jnp.concatenate([high, low, high], axis=0)
    tails = [None] * len(outs)
    for c in range(stacked.shape[0]):
        for n, part in enumerate(LANE_PARTS):
            result = jnp.dot(back, stacked[c, :, part], preferred_element_type=jnp.float32)
            for k, out in enumerate(outs):
                for half in range(local // GROUP):
                    g = c * (local // GROUP) + half
                    piece = result[k * local + half * GROUP : k * local + (half + 1) * GROUP]
                    first = (BODY_TILES * g + 2 * n) * LANES
                    if n < len(LANE_PARTS) - 1:
                        out[:, pl.ds(first, 2 * LANES)] = piece
                        continue
                    out[:, pl.ds(first, LANES)] = piece[:, :LANES]
                    tail = turn(piece[:, LANES:], 8 * g)
                    tails[k] = tail if g == 0 else jnp.where(lanes >= 8 * g, tail, tails[k])
    for out, tail in zip(outs, tails):
        out[:, pl.ds((BACK_TILES - 1) * LANES, LANES)] = tail


def trace_blocks(me):
    odd, late = lax.rem(me, 2), lax.rem(me, 4) // 2
    return 4 * late, 1 + 2 * odd, 4 - 4 * late, 3 - 2 * odd


def trace_partner(me, matching, size):
    step, start = ((2, 2), (1, 1), (2, 0), (1, 0))[matching]
    return (((me + start) ^ step) - start) % size


def update_kernel(plans, in0, in1, in2, in3, local_sum, table, updated, traces, out0, out1, out2, out3, chunks):
    me = lax.axis_index("plane")
    rows_total = local_sum.shape[1]
    last = NODES - 1
    lanes = lane_ids(8)
    for step, source in zip(PARTNERS, (in0, in1, in2, in3)):
        chunks[me ^ step] = source[...]

    trace_plans = [
        tile_plan([(k, 0, 0, 32), (last, 32 * k, 32, 32), (k, 256, 64, 32), (0, 32 * k, 96, 32)], 1)[0]
        for k in range(NODES)
    ]

    blocks = trace_blocks(lax.axis_index("dom"))

    def wide(row):
        return jnp.broadcast_to(table[pl.ds(row, 1), :], (8, LANES))

    turned_round = wide(15) == 1
    slot_edges = [wide(o) for o in blocks]
    groups = range(rows_total // GROUP)
    for g in groups:
        rows = group_rows(g)

        def load(source, tile, g=g):
            if source[0] == "tail":
                return turn(tile_at(chunks, (source[1],), slice(None), BACK_TILES - 1), -8 * g)
            return tile_at(chunks, (source[1],), slice(None), BODY_TILES * g + tile)

        turned = turner(load)
        for i in range(NODES):
            for t in range(SLAB_TILES):
                value = pieced(plans[i][t], turned, lanes)
                updated[i, rows, pl.ds(t * LANES, LANES)] = (
                    tile_at(local_sum, (i,), rows, t) + step_size * value
                )
    for g in groups:
        rows = group_rows(g)
        edges = turner(lambda i, tile, rows=rows: tile_at(updated, (i,), rows, tile))
        raw = [pieced(plan, edges, lanes) for plan in trace_plans]
        for k in range(NODES):
            traces[k, rows, :] = jnp.where(turned_round, raw[last - k], raw[k])
    for g in groups:
        rows = group_rows(g)
        for slot_edge, out in zip(slot_edges, (out0, out1, out2, out3)):
            for t in range(2):
                total = None
                for k in range(5 * t, min(5 * t + 5, NODES)):
                    value = pick(traces[k, rows, :], slot_edge)
                    total = value if total is None else jnp.where(lanes >= 24 * (k - 5 * t), value, total)
                out[rows, pl.ds(t * LANES, LANES)] = total


def own_kernel(table, traces, own):
    partner = jnp.broadcast_to(table[16:17, :], (GROUP, LANES))
    present = jnp.broadcast_to(table[12:13, :], (GROUP, LANES)) > 0
    for g in range(traces.shape[1] // GROUP):
        rows = group_rows(g)
        for k in range(NODES):
            own[k, rows, :] = jnp.where(present, pick(traces[k, rows, :], partner), 0.0)


def pick(value, index):
    return jnp.take_along_axis(value, index, axis=1, mode="promise_in_bounds")


def join_edges(table, updated, own, came, sums, put):
    rows_total = updated.shape[1]
    last = NODES - 1
    lanes = lane_ids(8)
    blocks = trace_blocks(lax.axis_index("dom"))

    def wide(row):
        return jnp.broadcast_to(table[pl.ds(row, 1), :], (8, LANES))

    share = wide(17).astype(jnp.float32)
    quarter = lanes // 32
    has = [wide(10 + o) > 0 for o in blocks]
    slots = [wide(5 + o) for o in blocks]

    def spread(values, at, t):
        value = None
        for k in range(4 * t, min(4 * t + 4, NODES)):
            moved = turn(values[k], 32 * (k - 4 * t - at))
            value = jnp.where(quarter == k - 4 * t, moved, 0.0 if value is None else value)
        return value

    def edge_parts(values, i, t):
        parts = []
        if t == 0:
            parts.append(jnp.where(quarter == 0, values[i], 0.0))
        if i == last:
            parts.append(spread(values, 1, t))
        if t == 2:
            parts.append(jnp.where(quarter == 0, turn(values[i], -64), 0.0))
        if i == 0:
            parts.append(spread(values, 3, t))
        return parts

    shares, scale = [share] * NODES, {}
    for i in (0, 1, last):
        for t in range(SLAB_TILES):
            parts = edge_parts(shares, i, t)
            if parts:
                scale[i, t] = 1.0 / (1.0 + sum(parts[1:], parts[0]))

    groups = range(rows_total // GROUP)
    for g in groups:
        rows = group_rows(g)
        for k in range(NODES):
            total = own[k, rows, :]
            for slot, there, source in zip(slots, has, came):
                value = pick(tile_at(source, (), rows, k // 5), slot + 24 * (k % 5))
                total = jnp.where(there, value, total)
            sums[k, rows, :] = total
    for g in groups:
        rows = group_rows(g)
        values = [sums[k, rows, :] for k in range(NODES)]
        for i in range(NODES):
            for t in range(SLAB_TILES):
                parts = edge_parts(values, i, t)
                if parts:
                    total = tile_at(updated, (i,), rows, t)
                    for part in parts:
                        total += part
                    put(g, i, t, total * scale[i if i in (0, last) else 1, t])


def next_kernel(plans, table, updated, own, r0, r1, r2, r3, bands, state, xi, out, sums):
    def put(g, i, t, value):
        state[i, group_rows(g), pl.ds(t * LANES, LANES)] = value

    for i in range(1, NODES - 1):
        state[i, :, pl.ds(LANES, LANES)] = updated[i, :, pl.ds(LANES, LANES)]
    join_edges(table, updated, own, (r0, r1, r2, r3), sums, put)
    make_xi(range(updated.shape[1] // GROUP), state, xi)
    make_first(plans, state, xi, bands, out)


def last_kernel(table, updated, own, r0, r1, r2, r3, out, state, sums, given, sems):
    comps, local, elements = given.shape[0], given.shape[3], given.shape[4]

    def put(g, i, t, value):
        state[i, group_rows(g), pl.ds(t * LANES, LANES)] = value

    join_edges(table, updated, own, (r0, r1, r2, r3), sums, put)
    copies = []
    for i in range(NODES):
        for c in range(comps):
            rows = pl.ds(c * local, local)
            for t in range(SLAB_TILES):
                joined = t != 1 or i in (0, NODES - 1)
                tile = tile_at(state if joined else updated, (i,), rows, t)
                for q in range(min(4, NODES - 4 * t)):
                    given[c, i, 4 * t + q] = turn(tile, -32 * q)[:, :elements]
        copies.append(pltpu.make_async_copy(given.at[:, i], out.at[:, i], sems.at[i]))
        copies[-1].start()
    for copy in copies:
        copy.wait()


def f32(*shape):
    return jax.ShapeDtypeStruct(shape, jnp.float32)


def kernel_call(body, outs, scratch, flops, moved, **more):
    return pl.pallas_call(
        body,
        out_shape=outs,
        scratch_shapes=scratch,
        compiler_params=pltpu.CompilerParams(vmem_limit_bytes=16 * 1024 * 1024),
        cost_estimate=pl.CostEstimate(flops=flops, bytes_accessed=moved, transcendentals=0),
        **more,
    )


def swapped(buffers):
    return [buffers[0]] + [swap(buffer, step) for buffer, step in zip(buffers[1:], PARTNERS[1:])]


def swap(buffer, step, wanted=range(4)):
    return lax.ppermute(buffer, "plane", sorted((i ^ step, i) for i in wanted))


def packed_shards(adjoint, metric, base_flow, edge_list, flips):
    comps, local, nodes, _, elements = adjoint.shape
    planes = MODES // local
    points = nodes * nodes * elements // planes
    rows_total = comps * local
    partitions = lax.axis_size("dom")
    state_shape = (nodes, rows_total, SLAB_TILES * LANES)

    layouts = [send_segments(chunk, points) for chunk in range(planes)]
    plans = [tile_plan(segments, SEND_TILES) for segments, _ in layouts]
    gaps = [gap for _, gap in layouts]
    back_plans = return_segments(points)
    to_span, to_span_last, to_modes = span_weights(planes)
    slab_bands = eta_bands(0, SLAB_TILES * LANES, nodes * elements)
    middle = [chunk for chunk, plan in enumerate(plans) if plan[-1]]
    chunk_bands = np.stack([chunk_eta_bands(b, points) for b in range(planes)])

    in_hbm, vmem = (pl.BlockSpec(memory_space=space) for space in (pltpu.HBM, pltpu.VMEM))
    buffer, base, extra = (f32(rows_total, tiles * LANES) for tiles in (SEND_TILES, BASE_TILES, 1))
    row_copies = [
        pltpu.VMEM((comps, nodes, nodes, local, elements), jnp.float32),
        pltpu.SemaphoreType.DMA((nodes,)),
    ]
    edge_scratch = pltpu.VMEM((nodes, rows_total, LANES), jnp.float32)

    def forward(state, xi, first):
        own, second, third, last_tile = kernel_call(
            functools.partial(rest_kernel, plans),
            [buffer, buffer, base, extra],
            [pltpu.VMEM((planes, *buffer.shape), jnp.float32)],
            10**6,
            2 * 10**6,
        )(state, xi, slab_bands)
        came = swapped([own, first, second, third])
        return [(part,) for part in came[:-1]] + [(came[-1], swap(last_tile, PARTNERS[-1], middle))]

    in_rows = pltpu.with_memory_space_constraint(adjoint.transpose(0, 2, 3, 1, 4), pltpu.HBM)
    state, *prepared = kernel_call(
        functools.partial(first_kernel, plans),
        [f32(*state_shape), f32(*state_shape), buffer],
        row_copies + [pltpu.VMEM(slab_bands.shape, jnp.float32)],
        4 * 10**6,
        4 * 10**6,
        in_specs=[in_hbm, in_hbm],
    )(in_rows, pltpu.with_memory_space_constraint(jnp.asarray(slab_bands), pltpu.HBM))
    incoming = forward(state, *prepared)
    whole, two_fields = (12, MODES, CHUNK_TILES * LANES), (2, MODES, CHUNK_TILES * LANES)
    lay = base_flow.transpose(1, 0, 2)
    flows = kernel_call(
        functools.partial(flow_kernel, points),
        [f32(*whole)] * STEPS,
        [pltpu.VMEM((2, STEPS, lay.shape[2] // LANES, LANES), jnp.float32)],
        4 * 10**6,
        9 * 10**6,
        grid=(6,),
        in_specs=[
            pl.BlockSpec((2, *lay.shape[1:]), lambda pair: (pair, 0, 0)),
            pl.BlockSpec(metric.shape, lambda pair: (0, 0)),
        ],
        out_specs=[pl.BlockSpec(two_fields, lambda pair: (pair, 0, 0))] * STEPS,
    )(lay, metric)
    table = kernel_call(
        tables_kernel,
        jax.ShapeDtypeStruct((24, LANES), jnp.int32),
        [pltpu.VMEM((LANES, LANES), jnp.float32)],
        10**5,
        10**5,
    )(edge_list.transpose(1, 0, 2), flips.transpose(1, 0, 2))

    for step_index in range(STEPS):
        fields = [None] * planes
        before = []
        for k in FIELDS_ORDER:
            parts = incoming[k]
            fields[k] = kernel_call(
                functools.partial(fields_kernel, gaps, len(parts) > 1),
                f32(3, comps, local, CHUNK_TILES * LANES),
                [],
                2 * 10**6,
                10**6,
                in_specs=[vmem] * (len(parts) + 1) + [pl.BlockSpec(memory_space=pl.ANY)] * len(before),
            )(*parts, chunk_bands, *before)
            before = [fields[k]] if k > 0 else []
        early = kernel_call(
            early_kernel, f32(comps, MODES, CHUNK_TILES * LANES), [], 50 * 10**6, 5 * 10**6
        )(*fields[:-1], flows[step_index], to_span)
        returning = kernel_call(
            advect_kernel,
            [f32(GROUP, BACK_TILES * LANES)] * planes,
            [pltpu.VMEM((comps, 3 * MODES, CHUNK_TILES * LANES), jnp.bfloat16)],
            30 * 10**6,
            5 * 10**6,
        )(fields[-1], early, flows[step_index], to_span_last, to_modes)
        local_sum = kernel_call(
            diffuse_kernel,
            f32(*state_shape),
            [pltpu.VMEM((nodes, GROUP, SLAB_TILES * LANES), jnp.float32)] * 2,
            12 * 10**6,
            2 * 10**6,
        )(state, metric, slab_bands)
        updated, seen, *leaving = kernel_call(
            functools.partial(update_kernel, back_plans),
            [f32(*state_shape), f32(nodes, rows_total, LANES)] + [f32(rows_total, 2 * LANES)] * 4,
            [pltpu.VMEM((planes, GROUP, BACK_TILES * LANES), jnp.float32)],
            2 * 10**6,
            3 * 10**6,
        )(*swapped(returning), local_sum, table)
        traces = [
            lax.ppermute(
                buffer, "dom", [(i, trace_partner(i, matching, partitions)) for i in range(partitions)]
            )
            for matching, buffer in enumerate(leaving)
        ]
        own = kernel_call(own_kernel, f32(nodes, rows_total, LANES), [], 10**5, 10**6)(table, seen)
        if step_index + 1 < STEPS:
            state, *prepared = kernel_call(
                functools.partial(next_kernel, plans),
                [f32(*state_shape), f32(*state_shape), buffer],
                [edge_scratch],
                6 * 10**6,
                4 * 10**6,
            )(table, updated, own, *traces, slab_bands)
            incoming = forward(state, *prepared)
        else:
            result = kernel_call(
                last_kernel,
                f32(comps, nodes, nodes, local, elements),
                [pltpu.VMEM(state_shape, jnp.float32), edge_scratch, *row_copies],
                2 * 10**6,
                3 * 10**6,
                out_specs=in_hbm,
            )(table, updated, own, *traces)
    return result.transpose(0, 3, 1, 2, 4)


def plain_shards(adjoint, metric, base_flow, edge_list, flips):
    local_modes = adjoint.shape[1]
    deriv_table = cheb_table(adjoint.shape[2])
    span_basis, span_slope, forward, wave_sq = span_tables(MODES)
    wave_local = lax.dynamic_slice_in_dim(
        wave_sq, lax.axis_index("plane") * local_modes, local_modes, 0
    )
    adjoint_state = adjoint
    for step_index in range(STEPS):
        base_now = base_flow[step_index].reshape(12, MODES, -1)
        adjoint_state = advance(
            adjoint_state,
            metric,
            base_now,
            edge_list[0],
            flips[0],
            deriv_table,
            span_basis,
            span_slope,
            forward,
            wave_local,
        )
    return adjoint_state


def shards(adjoint, metric, base_flow, edge_list, flips):
    if adjoint.shape[1:] == (MODES // 4, NODES, NODES, 32) and (
        edge_list.shape[1:] == (5, 24) and lax.axis_size("dom") % 4 == 0
    ):
        return packed_shards(adjoint, metric, base_flow, edge_list, flips)
    return plain_shards(adjoint, metric, base_flow, edge_list, flips)


def solution(mesh):
    placed = (
        P(None, "plane", None, None, "dom"),
        P(None, "dom"),
        P(None, None, ("dom", "plane")),
        P("dom", None, None),
        P("dom", None, None),
    )
    return jax.shard_map(
        shards,
        mesh=mesh,
        in_specs=placed,
        out_specs=P(None, "plane", None, None, "dom"),
        check_vma=False,
    )
```

```python
import functools

import jax
import jax.numpy as jnp
import numpy as np
from jax import lax
from jax.experimental import pallas as pl
from jax.experimental.pallas import tpu as pltpu
from jax.sharding import PartitionSpec as P

MODES = 64
STEPS = 2


step_size = 0.01
viscosity = 0.02


def passed_along(shard, axis, by):
    size = lax.axis_size(axis)
    return lax.ppermute(shard, axis, [(i, (i + by) % size) for i in range(size)])


def cheb_table(node_count):
    order = node_count - 1
    node_ids = jnp.arange(node_count, dtype=jnp.int32)
    node_coords = -jnp.cos(jnp.pi * node_ids.astype(jnp.float32) / order)
    weight = jnp.where((node_ids == 0) | (node_ids == order), 2.0, 1.0).astype(jnp.float32)
    parity = jnp.where((node_ids[:, None] + node_ids[None, :]) % 2 == 0, 1.0, -1.0).astype(
        jnp.float32
    )
    on_diag = node_ids[:, None] == node_ids[None, :]
    differ = jnp.where(on_diag, 1.0, node_coords[:, None] - node_coords[None, :])
    off_diag = jnp.where(on_diag, 0.0, weight[:, None] / weight[None, :] * parity / differ)
    return off_diag - jnp.diag(jnp.sum(off_diag, axis=1))


def span_tables(modes):
    mode_ids = jnp.arange(modes, dtype=jnp.int32)
    wavenumber = (mode_ids + 1) // 2
    is_cosine = (mode_ids % 2 == 1) | (mode_ids == 0)
    span_ids = jnp.arange(modes, dtype=jnp.int32)
    phase_num = span_ids[:, None] * wavenumber[None, :] % modes
    angles = 2.0 * jnp.pi * phase_num.astype(jnp.float32) / modes
    cosines = jnp.cos(angles)
    sines = jnp.sin(angles)
    wave_f = wavenumber.astype(jnp.float32)
    span_basis = jnp.where(is_cosine[None, :], cosines, sines)
    span_slope = jnp.where(is_cosine[None, :], -wave_f[None, :] * sines, wave_f[None, :] * cosines)
    scaling = jnp.where((mode_ids == 0) | (mode_ids == modes - 1), 1.0 / modes, 2.0 / modes).astype(
        jnp.float32
    )
    forward = span_basis.T * scaling[:, None]
    return (span_basis, span_slope, forward, wave_f * wave_f)


def directional(field_data, metric, deriv_table, xi_row, eta_row):
    along_xi = jnp.einsum(
        "ai,cmije->cmaje", deriv_table, field_data, precision=lax.Precision.HIGHEST
    )
    along_eta = jnp.einsum(
        "bj,cmije->cmibe", deriv_table, field_data, precision=lax.Precision.HIGHEST
    )
    return metric[xi_row] * along_xi + metric[eta_row] * along_eta


def advect(coeffs, base_now, span_basis, span_slope, forward):
    values = jnp.einsum("nm,fmq->fnq", span_basis, coeffs, precision=lax.Precision.HIGHEST)
    along_z = jnp.einsum("nm,cmq->cnq", span_slope, coeffs[0:3], precision=lax.Precision.HIGHEST)
    products = []
    for comp in range(3):
        term = (
            base_now[0] * values[3 + comp]
            + base_now[1] * values[6 + comp]
            + base_now[2] * along_z[comp]
        )
        term = term - (
            values[0] * base_now[3 + comp]
            + values[1] * base_now[6 + comp]
            + values[2] * base_now[9 + comp]
        )
        products.append(term)
    return jnp.einsum("mn,cnq->cmq", forward, jnp.stack(products), precision=lax.Precision.HIGHEST)


def accumulate(field_data, edge_sums, counts):
    node_count = field_data.shape[2]
    last = node_count - 1
    total = field_data
    total = total.at[:, :, :, 0, :].add(edge_sums[:, :, :, 0, :])
    total = total.at[:, :, last, :, :].add(edge_sums[:, :, :, 1, :])
    total = total.at[:, :, :, last, :].add(edge_sums[:, :, :, 2, :])
    total = total.at[:, :, 0, :, :].add(edge_sums[:, :, :, 3, :])
    weight = jnp.ones((node_count, node_count, field_data.shape[4]), jnp.float32)
    weight = weight.at[:, 0, :].add(counts[0][None, :])
    weight = weight.at[last, :, :].add(counts[1][None, :])
    weight = weight.at[:, last, :].add(counts[2][None, :])
    weight = weight.at[0, :, :].add(counts[3][None, :])
    return total / weight


def assemble(field_data, edge_slots, flip_flags):
    components, local_modes, node_count, _, elements = field_data.shape
    last = node_count - 1
    row_count = components * local_modes * node_count
    traces = jnp.stack(
        [
            field_data[:, :, :, 0, :],
            field_data[:, :, last, :, :],
            field_data[:, :, :, last, :],
            field_data[:, :, 0, :, :],
        ],
        axis=3,
    )
    edge_table = traces.reshape(row_count, 4 * elements)
    blocks, capacity = edge_slots.shape
    half_span = (blocks - 1) // 2
    slot_edges = edge_slots.reshape(-1)
    occupied = (slot_edges >= 0).astype(jnp.float32)
    outgoing = jnp.take(edge_table, jnp.maximum(slot_edges, 0), axis=1) * occupied[None, :]

    def block_of(block_id):
        return outgoing[:, block_id * capacity : (block_id + 1) * capacity]

    own_pairs = (
        block_of(half_span)
        .reshape(row_count, capacity // 2, 2)[:, :, ::-1]
        .reshape(row_count, capacity)
    )
    received = {half_span: own_pairs}
    for block_id in range(blocks):
        if block_id != half_span:
            received[block_id] = passed_along(
                block_of(blocks - 1 - block_id), "dom", half_span - block_id
            )
    partners = jnp.concatenate([received[block_id] for block_id in range(blocks)], axis=1)
    shaped = partners.reshape(components * local_modes, node_count, blocks * capacity)
    shaped = (
        jnp.where(flip_flags.reshape(-1)[None, None, :] == 1, shaped[:, ::-1, :], shaped)
        * occupied[None, None, :]
    )
    onehot = (slot_edges[:, None] == jnp.arange(4 * elements, dtype=jnp.int32)[None, :]).astype(
        jnp.float32
    )
    edge_sums = jnp.dot(
        shaped.reshape(row_count, blocks * capacity), onehot, precision=lax.Precision.HIGHEST
    )
    edge_sums = edge_sums.reshape(components, local_modes, node_count, 4, elements)
    counts = jnp.sum(onehot, axis=0).reshape(4, elements)
    return accumulate(field_data, edge_sums, counts)


def advance(
    adjoint_state,
    metric,
    base_now,
    edge_slots,
    flip_flags,
    deriv_table,
    span_basis,
    span_slope,
    forward,
    wave_local,
):
    components, local_modes, node_count, _, elements = adjoint_state.shape
    points = node_count * node_count * elements
    grad_x = directional(adjoint_state, metric, deriv_table, 0, 2)
    grad_y = directional(adjoint_state, metric, deriv_table, 1, 3)
    stacked = jnp.concatenate([adjoint_state, grad_x, grad_y], axis=0).reshape(
        9, local_modes, points
    )
    gathered = lax.all_to_all(stacked, "plane", split_axis=2, concat_axis=1, tiled=True)
    advective = advect(gathered, base_now, span_basis, span_slope, forward)
    returned = lax.all_to_all(advective, "plane", split_axis=1, concat_axis=2, tiled=True).reshape(
        adjoint_state.shape
    )
    laplacian = directional(grad_x, metric, deriv_table, 0, 2) + directional(
        grad_y, metric, deriv_table, 1, 3
    )
    updated = adjoint_state + step_size * (
        returned + viscosity * (laplacian - wave_local[None, :, None, None, None] * adjoint_state)
    )
    return assemble(updated, edge_slots, flip_flags)


NODES = 9
LANES = 128
SLAB_TILES = 3
STATE_TILES = 7
RING_TILES = 6
BASE_TILES = 11
SEND_TILES = 12
CHUNK_TILES = 6
BODY_TILES = 5
BACK_TILES = 31
GROUP = 8
PARTNERS = (0, 2, 1, 3)
BACK_PARTNERS = (0, 2, 3, 1)
FIELDS_ORDER = (0, 1, 2, 3)
STEP_VISC = step_size * viscosity


def cheb_numbers():
    order = NODES - 1
    coords = -np.cos(np.pi * np.arange(NODES) / order)
    weight = np.ones(NODES)
    weight[0] = weight[-1] = 2.0
    table = np.zeros((NODES, NODES))
    for a in range(NODES):
        for i in range(NODES):
            if a != i:
                table[a, i] = weight[a] / weight[i] * (-1.0) ** (a + i) / (coords[a] - coords[i])
    return table - np.diag(table.sum(axis=1))


DERIV = cheb_numbers()


def span_numbers():
    modes = np.arange(MODES)
    wave = (modes + 1) // 2
    is_cosine = (modes % 2 == 1) | (modes == 0)
    angles = 2.0 * np.pi * (np.arange(MODES)[:, None] * wave[None, :] % MODES) / MODES
    cosines, sines = np.cos(angles), np.sin(angles)
    basis = np.where(is_cosine, cosines, sines)
    slope = np.where(is_cosine, -wave * sines, wave * cosines)
    scaling = np.where((modes == 0) | (modes == MODES - 1), 1.0 / MODES, 2.0 / MODES)
    return basis, slope, basis.T * scaling[:, None]


def in_two(table):
    table = table.astype(np.float32)
    high = table.astype(jnp.bfloat16)
    low = (table - high.astype(np.float32)).astype(jnp.bfloat16)
    return high, low


def span_weights(planes):
    basis, slope, forward = span_numbers()
    local = MODES // planes
    to_span, to_span_last, to_modes = [], [], []
    for me in range(planes):
        came, goes = (
            np.concatenate([(me ^ step) * local + np.arange(local) for step in steps])
            for steps in (PARTNERS, BACK_PARTNERS)
        )
        high, low = in_two(np.concatenate([basis, slope])[:, came])
        early, last = slice(0, MODES - local), slice(MODES - local, MODES)
        for table, columns in ((to_span, early), (to_span_last, last)):
            table.append(np.concatenate([high[:, columns], high[:, columns], low[:, columns]], axis=1))
        high, low = in_two(forward[goes])
        to_modes.append(np.concatenate([high, high, low], axis=1))
    return np.stack(to_span), np.stack(to_span_last), np.stack(to_modes)


def eta_bands(first_lane, lanes, count):
    bands = np.zeros((24, lanes), np.float32)
    for lane in range(count):
        j = (first_lane + lane) % 288 // 32
        for d in range(-8, 9):
            if 0 <= j + d < NODES:
                bands[d + 8, lane] = DERIV[j, j + d]
    return bands


def tile_plan(segments, tiles):
    plan = [[] for _ in range(tiles)]
    for source, src, dst, length in segments:
        done = 0
        while done < length:
            s, d = src + done, dst + done
            size = min(length - done, LANES - s % LANES, LANES - d % LANES)
            plan[d // LANES].append((source, s // LANES, (d - s) % LANES, d % LANES, size))
            done += size
    return plan


def end_part(chunk, points):
    part = points - 2 * NODES * 32
    if chunk == 0:
        return 2, 0, points - part, part, 3
    if chunk == 3:
        return 6, NODES * 32 - part, 0, part, -7
    return None


def send_segments(chunk, points):
    ring, slab = STATE_TILES * LANES, NODES * 32
    turned = (points - 2 * slab) * chunk
    part = end_part(chunk, points)
    segments = []

    def add(source, src, dst, length):
        split = RING_TILES * LANES
        if dst < split < dst + length:
            add(source, src, dst, split - dst)
            add(source, src + split - dst, split, length - split + dst)
        else:
            segments.append((source, src, dst + (BASE_TILES - RING_TILES) * LANES * (dst >= split), length))

    if part is None:
        for r in range(3):
            start = (r * slab - turned) % ring
            first = min(slab, ring - start)
            add(("state", 2 * chunk + r), 0, start, first)
            if first < slab:
                add(("state", 2 * chunk + r), first, 0, slab - first)
        gap = (3 * slab - turned) % ring
    else:
        for i in range(NODES):
            low, high = max(i * slab, points * chunk), min((i + 1) * slab, points * (chunk + 1))
            if low < high:
                add(("state", i), low - i * slab, low - points * chunk, high - low)
        i, src, lane, length, ahead = part
        start = (lane + 32 * ahead) % ring
        add(("eta", i), src, start, length)
        gap = start + length
    body = points // LANES * LANES
    for i in range(NODES):
        low, high = max(i * slab, points * chunk), min((i + 1) * slab, points * (chunk + 1))
        cut = points * chunk + body
        if low < min(high, cut):
            segments.append(
                (("xi", i), low - i * slab, RING_TILES * LANES + low - points * chunk, min(high, cut) - low)
            )
        if max(low, cut) < high:
            low = max(low, cut)
            add(("xi", i), low - i * slab, gap + low - cut, high - low)
    return segments, gap


def chunk_eta_bands(chunk, points):
    bands = eta_bands((points - 2 * NODES * 32) * chunk, CHUNK_TILES * LANES, points)
    part = end_part(chunk, points)
    if part is not None:
        _, _, lane, length, ahead = part
        bands[:, lane : lane + length] = 0.0
        bands[ahead + 8, lane : lane + length] = 1.0
    return bands


def return_segments(points):
    slab = NODES * 32
    body = points // LANES * LANES
    plans = []
    for i in range(NODES):
        segments = []
        for chunk in range(4):
            for name, start, stop in (("body", 0, body), ("tail", body, points)):
                low = max(i * slab, chunk * points + start)
                high = min((i + 1) * slab, chunk * points + stop)
                if low < high:
                    segments.append(((name, chunk), low - chunk * points - start, low - i * slab, high - low))
        plans.append(tile_plan(segments, SLAB_TILES))
    return plans


def lane_ids(rows):
    return lax.broadcasted_iota(jnp.int32, (rows, LANES), 1)


def turn(value, shift):
    return value if shift % LANES == 0 else pltpu.roll(value, shift % LANES, 1)


def turner(load):
    made = {}

    def turned(source, tile, shift):
        key = source, tile, shift
        if key not in made:
            made[key] = turn(load(source, tile), shift)
        return made[key]

    return turned


def pieced(pieces, turned, lanes):
    total = None
    for source, tile, shift, low, size in pieces:
        value = turned(source, tile, shift)
        if total is None:
            total = value
        elif low + size == LANES:
            total = jnp.where(lanes >= low, value, total)
        else:
            total = jnp.where((lanes >= low) & (lanes < low + size), value, total)
    return total


def aligned(index, unit):
    return index if isinstance(index, int) else pl.multiple_of(index, unit)


def group_rows(g):
    return pl.ds(aligned(g * GROUP, GROUP), GROUP)


def tile_at(ref, lead, rows, tile):
    return ref[(*lead, rows, pl.ds(tile * LANES, LANES))]


def along_i(tiles):
    return [
        sum(tiles[i] * float(DERIV[a, i]) for i in range(1, NODES)) + tiles[0] * float(DERIV[a, 0])
        for a in range(NODES)
    ]


def turned_tiles(tiles, lanes):
    out = [tiles]
    for s in range(1, 4):
        spun = [pltpu.roll(t, LANES - 32 * s, 1) for t in tiles]
        out.append(
            [
                jnp.where(lanes < LANES - 32 * s, spun[t], spun[(t + 1) % len(tiles)])
                for t in range(len(tiles))
            ]
        )
    return out


def along_j(turned, ring, tile, band, used):
    total = None
    for d in used:
        term = turned[d % 4][(tile + d // 4) % ring] * band(d)
        total = term if total is None else total + term
    return total


def make_xi(groups, state, xi):
    for g in groups:
        rows = group_rows(g)
        for t in range(SLAB_TILES):
            for a, value in enumerate(along_i([tile_at(state, (i,), rows, t) for i in range(NODES)])):
                xi[a, rows, pl.ds(t * LANES, LANES)] = value


def used_offsets(tile):
    nodes = range(4 * tile, min(4 * tile + 4, NODES))
    return [d for d in range(-8, 9) if any(0 <= j + d < NODES for j in nodes)]


def make_buffer(plan, groups, state, xi, bands, put):
    lanes = lane_ids(GROUP)
    for g in groups:
        rows = group_rows(g)

        def load(source, tile, rows=rows):
            name, i = source
            if name != "eta":
                return tile_at(state if name == "state" else xi, (i,), rows, tile)
            turned = turned_tiles([tile_at(state, (i,), rows, t) for t in range(SLAB_TILES)], lanes)
            return along_j(
                turned, SLAB_TILES, tile, lambda d: tile_at(bands, (), pl.ds(d + 8, 1), tile), used_offsets(tile)
            )

        turned = turner(load)
        for t, pieces in enumerate(plan):
            value = pieced(pieces, turned, lanes) if pieces else jnp.zeros((GROUP, LANES), jnp.float32)
            put(rows, t, value)


def make_first(plans, state, xi, bands, out):
    target = lax.axis_index("plane") ^ PARTNERS[1]

    def put(rows, t, value):
        out[rows, pl.ds(t * LANES, LANES)] = value

    for chunk, plan in enumerate(plans):
        groups = range(state.shape[1] // GROUP)
        pl.when(target == chunk)(functools.partial(make_buffer, plan, groups, state, xi, bands, put))


def rest_kernel(plans, state, xi, bands, out0, out2, out3, extra3, staged):
    me = lax.axis_index("plane")
    for chunk, plan in enumerate(plans):

        def put(rows, t, value, chunk=chunk):
            staged[chunk, rows, pl.ds(t * LANES, LANES)] = value

        make_buffer(plan, range(state.shape[1] // GROUP), state, xi, bands, put)
    base, last = pl.ds(0, BASE_TILES * LANES), pl.ds(BASE_TILES * LANES, LANES)
    out0[...] = staged[me ^ PARTNERS[0]]
    out2[...] = staged[me ^ PARTNERS[2]]
    out3[...] = staged[me ^ PARTNERS[3], :, base]
    extra3[...] = staged[me ^ PARTNERS[3], :, last]


def first_kernel(plans, adjoint, far_bands, state, xi, out, taken, sems, bands):
    comps, local = taken.shape[0], taken.shape[3]

    def copy(c):
        return pltpu.make_async_copy(adjoint.at[c], taken.at[c], sems.at[c])

    for c in range(comps):
        copy(c).start()
    fetch = pltpu.make_async_copy(far_bands, bands, sems.at[comps])
    fetch.start()

    for c in range(comps):
        copy(c).wait()
        rows = pl.ds(c * local, local)
        for i in range(NODES):
            for t in range(SLAB_TILES):
                parts = [taken[c, i, j] for j in range(4 * t, min(4 * t + 4, NODES))]
                parts += [jnp.zeros_like(parts[0])] * (4 - len(parts))
                state[i, rows, pl.ds(t * LANES, LANES)] = jnp.concatenate(parts, axis=1)
        make_xi(range(c * local // GROUP, (c + 1) * local // GROUP), state, xi)
    fetch.wait()
    make_first(plans, state, xi, bands, out)


def metric_rows(metric):
    wide = jnp.concatenate([metric[...]] * (LANES // metric.shape[1]), axis=1)
    return jnp.concatenate([wide, wide], axis=0)


def flow_kernel(points, flow, metric, out0, out1, flat):
    me = lax.axis_index("plane")
    lanes, subs = lane_ids(8), lax.broadcasted_iota(jnp.int32, (8, LANES), 0)
    shift = lax.rem(LANES - lax.rem(me * points, LANES), LANES)
    turned = pltpu.roll(metric_rows(metric), shift, 1)
    ahead = pl.program_id(0) == 0
    first_first = jnp.where(ahead, turned[0:1], 1.0)
    first_second = jnp.where(ahead, turned[1:2], 0.0)
    second_first = jnp.where(ahead, turned[2:3], 0.0)
    second_second = jnp.where(ahead, turned[3:4], 1.0)
    per_sixteen = 16 * points // LANES
    last = CHUNK_TILES - 1

    for f in range(2):
        for s in range(STEPS):
            flat[f, s] = flow[f, s].reshape(flat.shape[2:])

    for s, out in enumerate((out0, out1)):
        for half in range(2):
            moved = (lanes + 64 * half + 8 * subs) & (LANES - 1)
            kept = lanes < LANES - 64 * half - 8 * subs

            def some_rows(h, _, s=s, half=half, out=out, moved=moved, kept=kept):
                rows = pl.ds(pl.multiple_of(16 * h + 8 * half, 8), 8)

                def field(f):
                    spun = []
                    for k in range(CHUNK_TILES):
                        start = per_sixteen * h + 40 * half + k
                        spun.append(pick(flat[f, s, pl.ds(start, 8, stride=5), :], moved))
                    return [jnp.where(kept, spun[k], spun[k + 1]) for k in range(last)] + [spun[last]]

                for t, (one, two) in enumerate(zip(field(0), field(1))):
                    out[0, rows, pl.ds(t * LANES, LANES)] = one * first_first + two * first_second
                    out[1, rows, pl.ds(t * LANES, LANES)] = one * second_first + two * second_second
                return 0

            lax.fori_loop(0, MODES // 16, some_rows, 0)


def tables_kernel(edges, flags, table, square):
    blocks, _, capacity = edges.shape
    lanes = lane_ids(capacity)
    slots = lax.broadcasted_iota(jnp.int32, (capacity, LANES), 0)
    here = slots == lax.rem(lanes, capacity)
    flag = jnp.zeros((1, LANES), jnp.int32)
    count = jnp.zeros((1, LANES), jnp.int32)
    table[...] = jnp.zeros(table.shape, jnp.int32)
    square[...] = jnp.zeros(square.shape, jnp.float32)
    for o in range(blocks):
        square[o : o + 1, 0:capacity] = edges[o].astype(jnp.float32)
        square[blocks + o : blocks + o + 1, 0:capacity] = flags[o].astype(jnp.float32)
    columns = square[...].T[0:capacity].astype(jnp.int32)
    for o in range(blocks):
        column = jnp.broadcast_to(columns[:, o : o + 1], (capacity, LANES))
        held = column == lanes

        def summed(mask, value):
            return jnp.sum(jnp.where(mask, value, 0), axis=0, keepdims=True)

        table[o : o + 1, :] = summed(here, jnp.maximum(column, 0))
        table[5 + o : 6 + o, :] = summed(held, slots)
        present = summed(held, jnp.ones_like(slots))
        table[10 + o : 11 + o, :] = present
        flag += summed(held, jnp.broadcast_to(columns[:, blocks + o : blocks + o + 1], (capacity, LANES)))
        count += present
        if o == blocks // 2:
            partner = slots + 1 - 2 * lax.rem(slots, 2)
            slot_of = jnp.broadcast_to(summed(held, partner), (capacity, LANES))
            partner_edge = summed(slots == slot_of, jnp.maximum(column, 0))
            table[16:17, :] = jnp.where(present > 0, partner_edge, 0)
    table[15:16, :] = flag
    table[17:18, :] = count


def diffuse_kernel(state, metric, bands, local_sum, first, second):
    me = lax.axis_index("plane")
    rows_total = state.shape[1]
    lanes = lane_ids(8)
    local = rows_total // 3
    wide = metric_rows(metric)
    xi_x, xi_y, eta_x, eta_y = (wide[r : r + 1] for r in range(4))
    g_ii = xi_x * xi_x + xi_y * xi_y
    g_ij = xi_x * eta_x + xi_y * eta_y
    g_jj = eta_x * eta_x + eta_y * eta_y
    def eta_of(tiles):
        turned = turned_tiles(tiles, lanes)
        return [
            along_j(turned, SLAB_TILES, t, lambda d, t=t: tile_at(bands, (), pl.ds(d + 8, 1), t), used_offsets(t))
            for t in range(SLAB_TILES)
        ]

    def some_rows(g, _):
        rows = pl.ds(pl.multiple_of(g * 8, 8), 8)
        first_mode = me * local + lax.rem(g * 8, local)
        wave = ((first_mode + lax.broadcasted_iota(jnp.int32, (8, LANES), 0) + 1) // 2).astype(jnp.float32)
        wave_sq = wave * wave
        for t in range(SLAB_TILES):
            for a, value in enumerate(along_i([tile_at(state, (i,), rows, t) for i in range(NODES)])):
                first[a, :, pl.ds(t * LANES, LANES)] = value
        for i in range(NODES):
            eta = eta_of([tile_at(state, (i,), rows, t) for t in range(SLAB_TILES)])
            mixed = []
            for t in range(SLAB_TILES):
                xi = first[i, :, pl.ds(t * LANES, LANES)]
                first[i, :, pl.ds(t * LANES, LANES)] = g_ii * xi + g_ij * eta[t]
                mixed.append(g_ij * xi + g_jj * eta[t])
            for t, value in enumerate(eta_of(mixed)):
                second[i, :, pl.ds(t * LANES, LANES)] = value
        for t in range(SLAB_TILES):
            tiles = [first[i, :, pl.ds(t * LANES, LANES)] for i in range(NODES)]
            for a, value in enumerate(along_i(tiles)):
                now = tile_at(state, (a,), rows, t)
                laplacian = value + second[a, :, pl.ds(t * LANES, LANES)]
                local_sum[a, rows, pl.ds(t * LANES, LANES)] = now + STEP_VISC * (laplacian - wave_sq * now)
        return 0

    lax.fori_loop(0, rows_total // 8, some_rows, 0)


def halves(value):
    high = value.astype(jnp.bfloat16)
    return high, (value - high.astype(jnp.float32)).astype(jnp.bfloat16)


def fields_kernel(gaps, split, source, *refs):
    extra, bands = (refs[0], refs[1]) if split else (None, refs[0])
    fields = refs[-1]
    me = lax.axis_index("plane")
    rows_total = source.shape[0]
    local = fields.shape[2]
    lanes = lane_ids(GROUP)
    gap = sum(jnp.where(me == b, g, 0) for b, g in enumerate(gaps))
    gap_late, gap_shift = gap >= RING_TILES * LANES, lax.rem(LANES - lax.rem(gap, LANES), LANES)

    for g in range(rows_total // GROUP):
        rows = group_rows(g)
        c = g * GROUP // local
        target = pl.ds(g * GROUP % local, GROUP)
        tiles = [tile_at(source, (), rows, t) for t in range(RING_TILES)]
        tiles.append(extra[rows, :] if split else tile_at(source, (), rows, BASE_TILES))
        turned = turned_tiles(tiles, lanes)
        for t in range(CHUNK_TILES):
            at = pl.ds(t * LANES, LANES)
            fields[0, c, target, at] = tiles[t]
            fields[2, c, target, at] = along_j(
                turned, STATE_TILES, t, lambda d, at=at: bands[me, pl.ds(d + 8, 1), at], range(-8, 9)
            )
        for t in range(BODY_TILES):
            fields[1, c, target, pl.ds(t * LANES, LANES)] = tile_at(source, (), rows, RING_TILES + t)
        tail = jnp.where(gap_late, tiles[RING_TILES], tiles[RING_TILES - 1])
        fields[1, c, target, pl.ds(BODY_TILES * LANES, LANES)] = pltpu.roll(tail, gap_shift, 1)


def span_dot(a, value):
    high, low = halves(value)
    stacked = jnp.concatenate([high, low, high], axis=0)
    return jnp.dot(a, stacked, preferred_element_type=jnp.float32)


LANE_PARTS = [pl.ds(first, 2 * LANES) for first in range(0, CHUNK_TILES * LANES, 2 * LANES)]


def products(sources, flow, both, part):
    def field(kind, c):
        return jnp.concatenate([fields[kind, c, :, part] for fields in sources], axis=0)

    comps, basis = sources[0].shape[1], both[:MODES]
    values, sums = [], []
    for c in range(comps):
        out = span_dot(both, field(0, c))
        values.append(out[:MODES])
        along_x = flow[0, :, part] * span_dot(basis, field(1, c))
        along_y = flow[1, :, part] * span_dot(basis, field(2, c))
        sums.append(along_x + along_y + flow[2, :, part] * out[MODES:])
    for c in range(comps):
        taken = values[0] * flow[3 + c, :, part]
        taken += values[1] * flow[6 + c, :, part]
        taken += values[2] * flow[9 + c, :, part]
        yield c, sums[c] - taken


def early_kernel(fields0, fields1, fields2, flow, to_span, early):
    both = to_span[lax.axis_index("plane")]
    for part in LANE_PARTS:
        for c, product in products((fields0, fields1, fields2), flow, both, part):
            early[c, :, part] = product


def advect_kernel(fields3, early, flow, to_span, to_modes, *refs):
    *outs, stacked = refs
    me = lax.axis_index("plane")
    both, back = to_span[me], to_modes[me]
    lanes = lane_ids(GROUP)
    local = MODES // len(outs)
    for part in LANE_PARTS:
        for c, product in products((fields3,), flow, both, part):
            high, low = halves(product + early[c, :, part])
            stacked[c, :, part] = jnp.concatenate([high, low, high], axis=0)
    tails = [None] * len(outs)
    for c in range(stacked.shape[0]):
        for n, part in enumerate(LANE_PARTS):
            result = jnp.dot(back, stacked[c, :, part], preferred_element_type=jnp.float32)
            for k, out in enumerate(outs):
                for half in range(local // GROUP):
                    g = c * (local // GROUP) + half
                    piece = result[k * local + half * GROUP : k * local + (half + 1) * GROUP]
                    first = (BODY_TILES * g + 2 * n) * LANES
                    if n < len(LANE_PARTS) - 1:
                        out[:, pl.ds(first, 2 * LANES)] = piece
                        continue
                    out[:, pl.ds(first, LANES)] = piece[:, :LANES]
                    tail = turn(piece[:, LANES:], 8 * g)
                    tails[k] = tail if g == 0 else jnp.where(lanes >= 8 * g, tail, tails[k])
    for out, tail in zip(outs, tails):
        out[:, pl.ds((BACK_TILES - 1) * LANES, LANES)] = tail


def trace_blocks(me):
    odd, late = lax.rem(me, 2), lax.rem(me, 4) // 2
    return 4 * late, 1 + 2 * odd, 4 - 4 * late, 3 - 2 * odd


def trace_partner(me, matching, size):
    step, start = ((2, 2), (1, 1), (2, 0), (1, 0))[matching]
    return (((me + start) ^ step) - start) % size


def update_kernel(plans, in0, in1, in2, in3, local_sum, table, updated, traces, out0, out1, out2, out3, chunks):
    me = lax.axis_index("plane")
    rows_total = local_sum.shape[1]
    last = NODES - 1
    lanes = lane_ids(8)
    for step, source in zip(BACK_PARTNERS, (in0, in1, in2, in3)):
        chunks[me ^ step] = source[...]

    trace_plans = [
        tile_plan([(k, 0, 0, 32), (last, 32 * k, 32, 32), (k, 256, 64, 32), (0, 32 * k, 96, 32)], 1)[0]
        for k in range(NODES)
    ]

    blocks = trace_blocks(lax.axis_index("dom"))

    def wide(row):
        return jnp.broadcast_to(table[pl.ds(row, 1), :], (8, LANES))

    turned_round = wide(15) == 1
    slot_edges = [wide(o) for o in blocks]
    groups = range(rows_total // GROUP)
    for g in groups:
        rows = group_rows(g)

        def load(source, tile, g=g):
            if source[0] == "tail":
                return turn(tile_at(chunks, (source[1],), slice(None), BACK_TILES - 1), -8 * g)
            return tile_at(chunks, (source[1],), slice(None), BODY_TILES * g + tile)

        turned = turner(load)
        for i in range(NODES):
            for t in range(SLAB_TILES):
                value = pieced(plans[i][t], turned, lanes)
                updated[i, rows, pl.ds(t * LANES, LANES)] = (
                    tile_at(local_sum, (i,), rows, t) + step_size * value
                )
    for g in groups:
        rows = group_rows(g)
        edges = turner(lambda i, tile, rows=rows: tile_at(updated, (i,), rows, tile))
        raw = [pieced(plan, edges, lanes) for plan in trace_plans]
        for k in range(NODES):
            traces[k, rows, :] = jnp.where(turned_round, raw[last - k], raw[k])
    for g in groups:
        rows = group_rows(g)
        for slot_edge, out in zip(slot_edges, (out0, out1, out2, out3)):
            for t in range(2):
                total = None
                for k in range(5 * t, min(5 * t + 5, NODES)):
                    value = pick(traces[k, rows, :], slot_edge)
                    total = value if total is None else jnp.where(lanes >= 24 * (k - 5 * t), value, total)
                out[rows, pl.ds(t * LANES, LANES)] = total


def own_kernel(table, traces, own):
    partner = jnp.broadcast_to(table[16:17, :], (GROUP, LANES))
    present = jnp.broadcast_to(table[12:13, :], (GROUP, LANES)) > 0
    for g in range(traces.shape[1] // GROUP):
        rows = group_rows(g)
        for k in range(NODES):
            own[k, rows, :] = jnp.where(present, pick(traces[k, rows, :], partner), 0.0)


def pick(value, index):
    return jnp.take_along_axis(value, index, axis=1, mode="promise_in_bounds")


def join_edges(table, updated, own, came, sums, put):
    rows_total = updated.shape[1]
    last = NODES - 1
    lanes = lane_ids(8)
    blocks = trace_blocks(lax.axis_index("dom"))

    def wide(row):
        return jnp.broadcast_to(table[pl.ds(row, 1), :], (8, LANES))

    share = wide(17).astype(jnp.float32)
    quarter = lanes // 32
    has = [wide(10 + o) > 0 for o in blocks]
    slots = [wide(5 + o) for o in blocks]

    def spread(values, at, t):
        value = None
        for k in range(4 * t, min(4 * t + 4, NODES)):
            moved = turn(values[k], 32 * (k - 4 * t - at))
            value = jnp.where(quarter == k - 4 * t, moved, 0.0 if value is None else value)
        return value

    def edge_parts(values, i, t):
        parts = []
        if t == 0:
            parts.append(jnp.where(quarter == 0, values[i], 0.0))
        if i == last:
            parts.append(spread(values, 1, t))
        if t == 2:
            parts.append(jnp.where(quarter == 0, turn(values[i], -64), 0.0))
        if i == 0:
            parts.append(spread(values, 3, t))
        return parts

    shares, scale = [share] * NODES, {}
    for i in (0, 1, last):
        for t in range(SLAB_TILES):
            parts = edge_parts(shares, i, t)
            if parts:
                scale[i, t] = 1.0 / (1.0 + sum(parts[1:], parts[0]))

    groups = range(rows_total // GROUP)
    for g in groups:
        rows = group_rows(g)
        for k in range(NODES):
            total = own[k, rows, :]
            for slot, there, source in zip(slots, has, came):
                value = pick(tile_at(source, (), rows, k // 5), slot + 24 * (k % 5))
                total = jnp.where(there, value, total)
            sums[k, rows, :] = total
    for g in groups:
        rows = group_rows(g)
        values = [sums[k, rows, :] for k in range(NODES)]
        for i in range(NODES):
            for t in range(SLAB_TILES):
                parts = edge_parts(values, i, t)
                if parts:
                    total = tile_at(updated, (i,), rows, t)
                    for part in parts:
                        total += part
                    put(g, i, t, total * scale[i if i in (0, last) else 1, t])


def next_kernel(plans, table, updated, own, r0, r1, r2, r3, bands, state, xi, out, sums):
    def put(g, i, t, value):
        state[i, group_rows(g), pl.ds(t * LANES, LANES)] = value

    for i in range(1, NODES - 1):
        state[i, :, pl.ds(LANES, LANES)] = updated[i, :, pl.ds(LANES, LANES)]
    join_edges(table, updated, own, (r0, r1, r2, r3), sums, put)
    make_xi(range(updated.shape[1] // GROUP), state, xi)
    make_first(plans, state, xi, bands, out)


def last_kernel(table, updated, own, r0, r1, r2, r3, out, state, sums, given, sems):
    comps, local, elements = given.shape[0], given.shape[3], given.shape[4]

    def put(g, i, t, value):
        state[i, group_rows(g), pl.ds(t * LANES, LANES)] = value

    join_edges(table, updated, own, (r0, r1, r2, r3), sums, put)
    copies = []
    for i in range(NODES):
        for c in range(comps):
            rows = pl.ds(c * local, local)
            for t in range(SLAB_TILES):
                joined = t != 1 or i in (0, NODES - 1)
                tile = tile_at(state if joined else updated, (i,), rows, t)
                for q in range(min(4, NODES - 4 * t)):
                    given[c, i, 4 * t + q] = turn(tile, -32 * q)[:, :elements]
        copies.append(pltpu.make_async_copy(given.at[:, i], out.at[:, i], sems.at[i]))
        copies[-1].start()
    for copy in copies:
        copy.wait()


def f32(*shape):
    return jax.ShapeDtypeStruct(shape, jnp.float32)


def kernel_call(body, outs, scratch, flops, moved, **more):
    return pl.pallas_call(
        body,
        out_shape=outs,
        scratch_shapes=scratch,
        compiler_params=pltpu.CompilerParams(vmem_limit_bytes=16 * 1024 * 1024),
        cost_estimate=pl.CostEstimate(flops=flops, bytes_accessed=moved, transcendentals=0),
        **more,
    )


def swapped(buffers, steps):
    return [buffers[0]] + [swap(buffer, step) for buffer, step in zip(buffers[1:], steps[1:])]


def swap(buffer, step, wanted=range(4)):
    return lax.ppermute(buffer, "plane", sorted((i ^ step, i) for i in wanted))


def packed_shards(adjoint, metric, base_flow, edge_list, flips):
    comps, local, nodes, _, elements = adjoint.shape
    planes = MODES // local
    points = nodes * nodes * elements // planes
    rows_total = comps * local
    partitions = lax.axis_size("dom")
    state_shape = (nodes, rows_total, SLAB_TILES * LANES)

    layouts = [send_segments(chunk, points) for chunk in range(planes)]
    plans = [tile_plan(segments, SEND_TILES) for segments, _ in layouts]
    gaps = [gap for _, gap in layouts]
    back_plans = return_segments(points)
    to_span, to_span_last, to_modes = span_weights(planes)
    slab_bands = eta_bands(0, SLAB_TILES * LANES, nodes * elements)
    middle = [chunk for chunk, plan in enumerate(plans) if plan[-1]]
    chunk_bands = np.stack([chunk_eta_bands(b, points) for b in range(planes)])

    in_hbm, vmem = (pl.BlockSpec(memory_space=space) for space in (pltpu.HBM, pltpu.VMEM))
    buffer, base, extra = (f32(rows_total, tiles * LANES) for tiles in (SEND_TILES, BASE_TILES, 1))
    row_copies = [
        pltpu.VMEM((comps, nodes, nodes, local, elements), jnp.float32),
        pltpu.SemaphoreType.DMA((nodes,)),
    ]
    edge_scratch = pltpu.VMEM((nodes, rows_total, LANES), jnp.float32)

    def forward(state, xi, first):
        own, second, third, last_tile = kernel_call(
            functools.partial(rest_kernel, plans),
            [buffer, buffer, base, extra],
            [pltpu.VMEM((planes, *buffer.shape), jnp.float32)],
            10**6,
            2 * 10**6,
        )(state, xi, slab_bands)
        came = swapped([own, first, second, third], PARTNERS)
        return [(part,) for part in came[:-1]] + [(came[-1], swap(last_tile, PARTNERS[-1], middle))]

    in_rows = pltpu.with_memory_space_constraint(adjoint.transpose(0, 2, 3, 1, 4), pltpu.HBM)
    state, *prepared = kernel_call(
        functools.partial(first_kernel, plans),
        [f32(*state_shape), f32(*state_shape), buffer],
        row_copies + [pltpu.VMEM(slab_bands.shape, jnp.float32)],
        4 * 10**6,
        4 * 10**6,
        in_specs=[in_hbm, in_hbm],
    )(in_rows, pltpu.with_memory_space_constraint(jnp.asarray(slab_bands), pltpu.HBM))
    incoming = forward(state, *prepared)
    whole, two_fields = (12, MODES, CHUNK_TILES * LANES), (2, MODES, CHUNK_TILES * LANES)
    lay = base_flow.transpose(1, 0, 2)
    flows = kernel_call(
        functools.partial(flow_kernel, points),
        [f32(*whole)] * STEPS,
        [pltpu.VMEM((2, STEPS, lay.shape[2] // LANES, LANES), jnp.float32)],
        4 * 10**6,
        9 * 10**6,
        grid=(6,),
        in_specs=[
            pl.BlockSpec((2, *lay.shape[1:]), lambda pair: (pair, 0, 0)),
            pl.BlockSpec(metric.shape, lambda pair: (0, 0)),
        ],
        out_specs=[pl.BlockSpec(two_fields, lambda pair: (pair, 0, 0))] * STEPS,
    )(lay, metric)
    table = kernel_call(
        tables_kernel,
        jax.ShapeDtypeStruct((24, LANES), jnp.int32),
        [pltpu.VMEM((LANES, LANES), jnp.float32)],
        10**5,
        10**5,
    )(edge_list.transpose(1, 0, 2), flips.transpose(1, 0, 2))

    for step_index in range(STEPS):
        fields = [None] * planes
        before = []
        for k in FIELDS_ORDER:
            parts = incoming[k]
            fields[k] = kernel_call(
                functools.partial(fields_kernel, gaps, len(parts) > 1),
                f32(3, comps, local, CHUNK_TILES * LANES),
                [],
                2 * 10**6,
                10**6,
                in_specs=[vmem] * (len(parts) + 1) + [pl.BlockSpec(memory_space=pl.ANY)] * len(before),
            )(*parts, chunk_bands, *before)
            before = [fields[k]] if k > 0 else []
        early = kernel_call(
            early_kernel, f32(comps, MODES, CHUNK_TILES * LANES), [], 50 * 10**6, 5 * 10**6
        )(*fields[:-1], flows[step_index], to_span)
        returning = kernel_call(
            advect_kernel,
            [f32(GROUP, BACK_TILES * LANES)] * planes,
            [pltpu.VMEM((comps, 3 * MODES, CHUNK_TILES * LANES), jnp.bfloat16)],
            30 * 10**6,
            5 * 10**6,
        )(fields[-1], early, flows[step_index], to_span_last, to_modes)
        local_sum = kernel_call(
            diffuse_kernel,
            f32(*state_shape),
            [pltpu.VMEM((nodes, GROUP, SLAB_TILES * LANES), jnp.float32)] * 2,
            12 * 10**6,
            2 * 10**6,
        )(state, metric, slab_bands)
        updated, seen, *leaving = kernel_call(
            functools.partial(update_kernel, back_plans),
            [f32(*state_shape), f32(nodes, rows_total, LANES)] + [f32(rows_total, 2 * LANES)] * 4,
            [pltpu.VMEM((planes, GROUP, BACK_TILES * LANES), jnp.float32)],
            2 * 10**6,
            3 * 10**6,
        )(*swapped(returning, BACK_PARTNERS), local_sum, table)
        traces = [
            lax.ppermute(
                buffer, "dom", [(i, trace_partner(i, matching, partitions)) for i in range(partitions)]
            )
            for matching, buffer in enumerate(leaving)
        ]
        own = kernel_call(own_kernel, f32(nodes, rows_total, LANES), [], 10**5, 10**6)(table, seen)
        if step_index + 1 < STEPS:
            state, *prepared = kernel_call(
                functools.partial(next_kernel, plans),
                [f32(*state_shape), f32(*state_shape), buffer],
                [edge_scratch],
                6 * 10**6,
                4 * 10**6,
            )(table, updated, own, *traces, slab_bands)
            incoming = forward(state, *prepared)
        else:
            result = kernel_call(
                last_kernel,
                f32(comps, nodes, nodes, local, elements),
                [pltpu.VMEM(state_shape, jnp.float32), edge_scratch, *row_copies],
                2 * 10**6,
                3 * 10**6,
                out_specs=in_hbm,
            )(table, updated, own, *traces)
    return result.transpose(0, 3, 1, 2, 4)


def plain_shards(adjoint, metric, base_flow, edge_list, flips):
    local_modes = adjoint.shape[1]
    deriv_table = cheb_table(adjoint.shape[2])
    span_basis, span_slope, forward, wave_sq = span_tables(MODES)
    wave_local = lax.dynamic_slice_in_dim(
        wave_sq, lax.axis_index("plane") * local_modes, local_modes, 0
    )
    adjoint_state = adjoint
    for step_index in range(STEPS):
        base_now = base_flow[step_index].reshape(12, MODES, -1)
        adjoint_state = advance(
            adjoint_state,
            metric,
            base_now,
            edge_list[0],
            flips[0],
            deriv_table,
            span_basis,
            span_slope,
            forward,
            wave_local,
        )
    return adjoint_state


def shards(adjoint, metric, base_flow, edge_list, flips):
    if adjoint.shape[1:] == (MODES // 4, NODES, NODES, 32) and (
        edge_list.shape[1:] == (5, 24) and lax.axis_size("dom") % 4 == 0
    ):
        return packed_shards(adjoint, metric, base_flow, edge_list, flips)
    return plain_shards(adjoint, metric, base_flow, edge_list, flips)


def solution(mesh):
    placed = (
        P(None, "plane", None, None, "dom"),
        P(None, "dom"),
        P(None, None, ("dom", "plane")),
        P("dom", None, None),
        P("dom", None, None),
    )
    return jax.shard_map(
        shards,
        mesh=mesh,
        in_specs=placed,
        out_specs=P(None, "plane", None, None, "dom"),
        check_vma=False,
    )
```

```python
import functools

import jax
import jax.numpy as jnp
import numpy as np
from jax import lax
from jax.experimental import pallas as pl
from jax.experimental.pallas import tpu as pltpu
from jax.sharding import PartitionSpec as P

MODES = 64
STEPS = 2


step_size = 0.01
viscosity = 0.02


def passed_along(shard, axis, by):
    size = lax.axis_size(axis)
    return lax.ppermute(shard, axis, [(i, (i + by) % size) for i in range(size)])


def cheb_table(node_count):
    order = node_count - 1
    node_ids = jnp.arange(node_count, dtype=jnp.int32)
    node_coords = -jnp.cos(jnp.pi * node_ids.astype(jnp.float32) / order)
    weight = jnp.where((node_ids == 0) | (node_ids == order), 2.0, 1.0).astype(jnp.float32)
    parity = jnp.where((node_ids[:, None] + node_ids[None, :]) % 2 == 0, 1.0, -1.0).astype(
        jnp.float32
    )
    on_diag = node_ids[:, None] == node_ids[None, :]
    differ = jnp.where(on_diag, 1.0, node_coords[:, None] - node_coords[None, :])
    off_diag = jnp.where(on_diag, 0.0, weight[:, None] / weight[None, :] * parity / differ)
    return off_diag - jnp.diag(jnp.sum(off_diag, axis=1))


def span_tables(modes):
    mode_ids = jnp.arange(modes, dtype=jnp.int32)
    wavenumber = (mode_ids + 1) // 2
    is_cosine = (mode_ids % 2 == 1) | (mode_ids == 0)
    span_ids = jnp.arange(modes, dtype=jnp.int32)
    phase_num = span_ids[:, None] * wavenumber[None, :] % modes
    angles = 2.0 * jnp.pi * phase_num.astype(jnp.float32) / modes
    cosines = jnp.cos(angles)
    sines = jnp.sin(angles)
    wave_f = wavenumber.astype(jnp.float32)
    span_basis = jnp.where(is_cosine[None, :], cosines, sines)
    span_slope = jnp.where(is_cosine[None, :], -wave_f[None, :] * sines, wave_f[None, :] * cosines)
    scaling = jnp.where((mode_ids == 0) | (mode_ids == modes - 1), 1.0 / modes, 2.0 / modes).astype(
        jnp.float32
    )
    forward = span_basis.T * scaling[:, None]
    return (span_basis, span_slope, forward, wave_f * wave_f)


def directional(field_data, metric, deriv_table, xi_row, eta_row):
    along_xi = jnp.einsum(
        "ai,cmije->cmaje", deriv_table, field_data, precision=lax.Precision.HIGHEST
    )
    along_eta = jnp.einsum(
        "bj,cmije->cmibe", deriv_table, field_data, precision=lax.Precision.HIGHEST
    )
    return metric[xi_row] * along_xi + metric[eta_row] * along_eta


def advect(coeffs, base_now, span_basis, span_slope, forward):
    values = jnp.einsum("nm,fmq->fnq", span_basis, coeffs, precision=lax.Precision.HIGHEST)
    along_z = jnp.einsum("nm,cmq->cnq", span_slope, coeffs[0:3], precision=lax.Precision.HIGHEST)
    products = []
    for comp in range(3):
        term = (
            base_now[0] * values[3 + comp]
            + base_now[1] * values[6 + comp]
            + base_now[2] * along_z[comp]
        )
        term = term - (
            values[0] * base_now[3 + comp]
            + values[1] * base_now[6 + comp]
            + values[2] * base_now[9 + comp]
        )
        products.append(term)
    return jnp.einsum("mn,cnq->cmq", forward, jnp.stack(products), precision=lax.Precision.HIGHEST)


def accumulate(field_data, edge_sums, counts):
    node_count = field_data.shape[2]
    last = node_count - 1
    total = field_data
    total = total.at[:, :, :, 0, :].add(edge_sums[:, :, :, 0, :])
    total = total.at[:, :, last, :, :].add(edge_sums[:, :, :, 1, :])
    total = total.at[:, :, :, last, :].add(edge_sums[:, :, :, 2, :])
    total = total.at[:, :, 0, :, :].add(edge_sums[:, :, :, 3, :])
    weight = jnp.ones((node_count, node_count, field_data.shape[4]), jnp.float32)
    weight = weight.at[:, 0, :].add(counts[0][None, :])
    weight = weight.at[last, :, :].add(counts[1][None, :])
    weight = weight.at[:, last, :].add(counts[2][None, :])
    weight = weight.at[0, :, :].add(counts[3][None, :])
    return total / weight


def assemble(field_data, edge_slots, flip_flags):
    components, local_modes, node_count, _, elements = field_data.shape
    last = node_count - 1
    row_count = components * local_modes * node_count
    traces = jnp.stack(
        [
            field_data[:, :, :, 0, :],
            field_data[:, :, last, :, :],
            field_data[:, :, :, last, :],
            field_data[:, :, 0, :, :],
        ],
        axis=3,
    )
    edge_table = traces.reshape(row_count, 4 * elements)
    blocks, capacity = edge_slots.shape
    half_span = (blocks - 1) // 2
    slot_edges = edge_slots.reshape(-1)
    occupied = (slot_edges >= 0).astype(jnp.float32)
    outgoing = jnp.take(edge_table, jnp.maximum(slot_edges, 0), axis=1) * occupied[None, :]

    def block_of(block_id):
        return outgoing[:, block_id * capacity : (block_id + 1) * capacity]

    own_pairs = (
        block_of(half_span)
        .reshape(row_count, capacity // 2, 2)[:, :, ::-1]
        .reshape(row_count, capacity)
    )
    received = {half_span: own_pairs}
    for block_id in range(blocks):
        if block_id != half_span:
            received[block_id] = passed_along(
                block_of(blocks - 1 - block_id), "dom", half_span - block_id
            )
    partners = jnp.concatenate([received[block_id] for block_id in range(blocks)], axis=1)
    shaped = partners.reshape(components * local_modes, node_count, blocks * capacity)
    shaped = (
        jnp.where(flip_flags.reshape(-1)[None, None, :] == 1, shaped[:, ::-1, :], shaped)
        * occupied[None, None, :]
    )
    onehot = (slot_edges[:, None] == jnp.arange(4 * elements, dtype=jnp.int32)[None, :]).astype(
        jnp.float32
    )
    edge_sums = jnp.dot(
        shaped.reshape(row_count, blocks * capacity), onehot, precision=lax.Precision.HIGHEST
    )
    edge_sums = edge_sums.reshape(components, local_modes, node_count, 4, elements)
    counts = jnp.sum(onehot, axis=0).reshape(4, elements)
    return accumulate(field_data, edge_sums, counts)


def advance(
    adjoint_state,
    metric,
    base_now,
    edge_slots,
    flip_flags,
    deriv_table,
    span_basis,
    span_slope,
    forward,
    wave_local,
):
    components, local_modes, node_count, _, elements = adjoint_state.shape
    points = node_count * node_count * elements
    grad_x = directional(adjoint_state, metric, deriv_table, 0, 2)
    grad_y = directional(adjoint_state, metric, deriv_table, 1, 3)
    stacked = jnp.concatenate([adjoint_state, grad_x, grad_y], axis=0).reshape(
        9, local_modes, points
    )
    gathered = lax.all_to_all(stacked, "plane", split_axis=2, concat_axis=1, tiled=True)
    advective = advect(gathered, base_now, span_basis, span_slope, forward)
    returned = lax.all_to_all(advective, "plane", split_axis=1, concat_axis=2, tiled=True).reshape(
        adjoint_state.shape
    )
    laplacian = directional(grad_x, metric, deriv_table, 0, 2) + directional(
        grad_y, metric, deriv_table, 1, 3
    )
    updated = adjoint_state + step_size * (
        returned + viscosity * (laplacian - wave_local[None, :, None, None, None] * adjoint_state)
    )
    return assemble(updated, edge_slots, flip_flags)


NODES = 9
LANES = 128
SLAB_TILES = 3
STATE_TILES = 7
RING_TILES = 6
BASE_TILES = 11
SEND_TILES = 12
CHUNK_TILES = 6
BODY_TILES = 5
BACK_TILES = 31
GROUP = 8
PARTNERS = (0, 2, 1, 3)
BACK_PARTNERS = (0, 2, 3, 1)
FIELDS_ORDER = (0, 1, 2, 3)
STEP_VISC = step_size * viscosity


def cheb_numbers():
    order = NODES - 1
    coords = -np.cos(np.pi * np.arange(NODES) / order)
    weight = np.ones(NODES)
    weight[0] = weight[-1] = 2.0
    table = np.zeros((NODES, NODES))
    for a in range(NODES):
        for i in range(NODES):
            if a != i:
                table[a, i] = weight[a] / weight[i] * (-1.0) ** (a + i) / (coords[a] - coords[i])
    return table - np.diag(table.sum(axis=1))


DERIV = cheb_numbers()


def span_numbers():
    modes = np.arange(MODES)
    wave = (modes + 1) // 2
    is_cosine = (modes % 2 == 1) | (modes == 0)
    angles = 2.0 * np.pi * (np.arange(MODES)[:, None] * wave[None, :] % MODES) / MODES
    cosines, sines = np.cos(angles), np.sin(angles)
    basis = np.where(is_cosine, cosines, sines)
    slope = np.where(is_cosine, -wave * sines, wave * cosines)
    scaling = np.where((modes == 0) | (modes == MODES - 1), 1.0 / MODES, 2.0 / MODES)
    return basis, slope, basis.T * scaling[:, None]


def in_two(table):
    table = table.astype(np.float32)
    high = table.astype(jnp.bfloat16)
    low = (table - high.astype(np.float32)).astype(jnp.bfloat16)
    return high, low


def span_weights(planes):
    basis, slope, forward = span_numbers()
    local = MODES // planes
    to_span, to_span_last, to_modes = [], [], []
    for me in range(planes):
        came, goes = (
            np.concatenate([(me ^ step) * local + np.arange(local) for step in steps])
            for steps in (PARTNERS, BACK_PARTNERS)
        )
        high, low = in_two(np.concatenate([basis, slope])[:, came])
        early, last = slice(0, MODES - local), slice(MODES - local, MODES)
        for table, columns in ((to_span, early), (to_span_last, last)):
            table.append(np.concatenate([high[:, columns], high[:, columns], low[:, columns]], axis=1))
        high, low = in_two(forward[goes])
        to_modes.append(np.concatenate([high, high, low], axis=1))
    return np.stack(to_span), np.stack(to_span_last), np.stack(to_modes)


def eta_bands(first_lane, lanes, count):
    bands = np.zeros((24, lanes), np.float32)
    for lane in range(count):
        j = (first_lane + lane) % 288 // 32
        for d in range(-8, 9):
            if 0 <= j + d < NODES:
                bands[d + 8, lane] = DERIV[j, j + d]
    return bands


def tile_plan(segments, tiles):
    plan = [[] for _ in range(tiles)]
    for source, src, dst, length in segments:
        done = 0
        while done < length:
            s, d = src + done, dst + done
            size = min(length - done, LANES - s % LANES, LANES - d % LANES)
            plan[d // LANES].append((source, s // LANES, (d - s) % LANES, d % LANES, size))
            done += size
    return plan


def end_part(chunk, points):
    part = points - 2 * NODES * 32
    if chunk == 0:
        return 2, 0, points - part, part, 3
    if chunk == 3:
        return 6, NODES * 32 - part, 0, part, -7
    return None


def send_segments(chunk, points):
    ring, slab = STATE_TILES * LANES, NODES * 32
    turned = (points - 2 * slab) * chunk
    part = end_part(chunk, points)
    segments = []

    def add(source, src, dst, length):
        split = RING_TILES * LANES
        if dst < split < dst + length:
            add(source, src, dst, split - dst)
            add(source, src + split - dst, split, length - split + dst)
        else:
            segments.append((source, src, dst + (BASE_TILES - RING_TILES) * LANES * (dst >= split), length))

    if part is None:
        for r in range(3):
            start = (r * slab - turned) % ring
            first = min(slab, ring - start)
            add(("state", 2 * chunk + r), 0, start, first)
            if first < slab:
                add(("state", 2 * chunk + r), first, 0, slab - first)
        gap = (3 * slab - turned) % ring
    else:
        for i in range(NODES):
            low, high = max(i * slab, points * chunk), min((i + 1) * slab, points * (chunk + 1))
            if low < high:
                add(("state", i), low - i * slab, low - points * chunk, high - low)
        i, src, lane, length, ahead = part
        start = (lane + 32 * ahead) % ring
        add(("eta", i), src, start, length)
        gap = start + length
    body = points // LANES * LANES
    for i in range(NODES):
        low, high = max(i * slab, points * chunk), min((i + 1) * slab, points * (chunk + 1))
        cut = points * chunk + body
        if low < min(high, cut):
            segments.append(
                (("xi", i), low - i * slab, RING_TILES * LANES + low - points * chunk, min(high, cut) - low)
            )
        if max(low, cut) < high:
            low = max(low, cut)
            add(("xi", i), low - i * slab, gap + low - cut, high - low)
    return segments, gap


def chunk_eta_bands(chunk, points):
    bands = eta_bands((points - 2 * NODES * 32) * chunk, CHUNK_TILES * LANES, points)
    part = end_part(chunk, points)
    if part is not None:
        _, _, lane, length, ahead = part
        bands[:, lane : lane + length] = 0.0
        bands[ahead + 8, lane : lane + length] = 1.0
    return bands


def return_segments(points):
    slab = NODES * 32
    body = points // LANES * LANES
    plans = []
    for i in range(NODES):
        segments = []
        for chunk in range(4):
            for name, start, stop in (("body", 0, body), ("tail", body, points)):
                low = max(i * slab, chunk * points + start)
                high = min((i + 1) * slab, chunk * points + stop)
                if low < high:
                    segments.append(((name, chunk), low - chunk * points - start, low - i * slab, high - low))
        plans.append(tile_plan(segments, SLAB_TILES))
    return plans


def lane_ids(rows):
    return lax.broadcasted_iota(jnp.int32, (rows, LANES), 1)


def turn(value, shift):
    return value if shift % LANES == 0 else pltpu.roll(value, shift % LANES, 1)


def turner(load):
    made = {}

    def turned(source, tile, shift):
        key = source, tile, shift
        if key not in made:
            made[key] = turn(load(source, tile), shift)
        return made[key]

    return turned


def pieced(pieces, turned, lanes):
    total = None
    for source, tile, shift, low, size in pieces:
        value = turned(source, tile, shift)
        if total is None:
            total = value
        elif low + size == LANES:
            total = jnp.where(lanes >= low, value, total)
        else:
            total = jnp.where((lanes >= low) & (lanes < low + size), value, total)
    return total


def aligned(index, unit):
    return index if isinstance(index, int) else pl.multiple_of(index, unit)


def group_rows(g):
    return pl.ds(aligned(g * GROUP, GROUP), GROUP)


def tile_at(ref, lead, rows, tile):
    return ref[(*lead, rows, pl.ds(tile * LANES, LANES))]


def along_i(tiles):
    return [
        sum(tiles[i] * float(DERIV[a, i]) for i in range(1, NODES)) + tiles[0] * float(DERIV[a, 0])
        for a in range(NODES)
    ]


def turned_tiles(tiles, lanes):
    out = [tiles]
    for s in range(1, 4):
        spun = [pltpu.roll(t, LANES - 32 * s, 1) for t in tiles]
        out.append(
            [
                jnp.where(lanes < LANES - 32 * s, spun[t], spun[(t + 1) % len(tiles)])
                for t in range(len(tiles))
            ]
        )
    return out


def along_j(turned, ring, tile, band, used):
    total = None
    for d in used:
        term = turned[d % 4][(tile + d // 4) % ring] * band(d)
        total = term if total is None else total + term
    return total


def make_xi(groups, state, xi):
    for g in groups:
        rows = group_rows(g)
        for t in range(SLAB_TILES):
            for a, value in enumerate(along_i([tile_at(state, (i,), rows, t) for i in range(NODES)])):
                xi[a, rows, pl.ds(t * LANES, LANES)] = value


def used_offsets(tile):
    nodes = range(4 * tile, min(4 * tile + 4, NODES))
    return [d for d in range(-8, 9) if any(0 <= j + d < NODES for j in nodes)]


def make_buffer(plan, groups, state, xi, bands, put):
    lanes = lane_ids(GROUP)
    for g in groups:
        rows = group_rows(g)

        def load(source, tile, rows=rows):
            name, i = source
            if name != "eta":
                return tile_at(state if name == "state" else xi, (i,), rows, tile)
            turned = turned_tiles([tile_at(state, (i,), rows, t) for t in range(SLAB_TILES)], lanes)
            return along_j(
                turned, SLAB_TILES, tile, lambda d: tile_at(bands, (), pl.ds(d + 8, 1), tile), used_offsets(tile)
            )

        turned = turner(load)
        for t, pieces in enumerate(plan):
            value = pieced(pieces, turned, lanes) if pieces else jnp.zeros((GROUP, LANES), jnp.float32)
            put(rows, t, value)


def make_first(plans, state, xi, bands, out):
    target = lax.axis_index("plane") ^ PARTNERS[1]

    def put(rows, t, value):
        out[rows, pl.ds(t * LANES, LANES)] = value

    for chunk, plan in enumerate(plans):
        groups = range(state.shape[1] // GROUP)
        pl.when(target == chunk)(functools.partial(make_buffer, plan, groups, state, xi, bands, put))


def rest_kernel(plans, state, xi, bands, out0, out2, out3, extra3, staged):
    me = lax.axis_index("plane")
    for chunk, plan in enumerate(plans):

        def put(rows, t, value, chunk=chunk):
            staged[chunk, rows, pl.ds(t * LANES, LANES)] = value

        make_buffer(plan, range(state.shape[1] // GROUP), state, xi, bands, put)
    base, last = pl.ds(0, BASE_TILES * LANES), pl.ds(BASE_TILES * LANES, LANES)
    out0[...] = staged[me ^ PARTNERS[0]]
    out2[...] = staged[me ^ PARTNERS[2]]
    out3[...] = staged[me ^ PARTNERS[3], :, base]
    extra3[...] = staged[me ^ PARTNERS[3], :, last]


def first_kernel(plans, adjoint, far_bands, state, xi, out, taken, sems, bands):
    comps, local = taken.shape[0], taken.shape[3]

    def copy(c):
        return pltpu.make_async_copy(adjoint.at[c], taken.at[c], sems.at[c])

    for c in range(comps):
        copy(c).start()
    fetch = pltpu.make_async_copy(far_bands, bands, sems.at[comps])
    fetch.start()

    for c in range(comps):
        copy(c).wait()
        rows = pl.ds(c * local, local)
        for i in range(NODES):
            for t in range(SLAB_TILES):
                parts = [taken[c, i, j] for j in range(4 * t, min(4 * t + 4, NODES))]
                parts += [jnp.zeros_like(parts[0])] * (4 - len(parts))
                state[i, rows, pl.ds(t * LANES, LANES)] = jnp.concatenate(parts, axis=1)
        make_xi(range(c * local // GROUP, (c + 1) * local // GROUP), state, xi)
    fetch.wait()
    make_first(plans, state, xi, bands, out)


def metric_rows(metric):
    wide = jnp.concatenate([metric[...]] * (LANES // metric.shape[1]), axis=1)
    return jnp.concatenate([wide, wide], axis=0)


def flow_kernel(points, flow, metric, out0, out1, flat):
    me = lax.axis_index("plane")
    lanes, subs = lane_ids(8), lax.broadcasted_iota(jnp.int32, (8, LANES), 0)
    shift = lax.rem(LANES - lax.rem(me * points, LANES), LANES)
    turned = pltpu.roll(metric_rows(metric), shift, 1)
    ahead = pl.program_id(0) == 0
    first_first = jnp.where(ahead, turned[0:1], 1.0)
    first_second = jnp.where(ahead, turned[1:2], 0.0)
    second_first = jnp.where(ahead, turned[2:3], 0.0)
    second_second = jnp.where(ahead, turned[3:4], 1.0)
    per_sixteen = 16 * points // LANES
    last = CHUNK_TILES - 1

    for f in range(2):
        for s in range(STEPS):
            flat[f, s] = flow[f, s].reshape(flat.shape[2:])

    for s, out in enumerate((out0, out1)):
        for half in range(2):
            moved = (lanes + 64 * half + 8 * subs) & (LANES - 1)
            kept = lanes < LANES - 64 * half - 8 * subs

            def some_rows(h, _, s=s, half=half, out=out, moved=moved, kept=kept):
                rows = pl.ds(pl.multiple_of(16 * h + 8 * half, 8), 8)

                def field(f):
                    spun = []
                    for k in range(CHUNK_TILES):
                        start = per_sixteen * h + 40 * half + k
                        spun.append(pick(flat[f, s, pl.ds(start, 8, stride=5), :], moved))
                    return [jnp.where(kept, spun[k], spun[k + 1]) for k in range(last)] + [spun[last]]

                for t, (one, two) in enumerate(zip(field(0), field(1))):
                    out[0, rows, pl.ds(t * LANES, LANES)] = one * first_first + two * first_second
                    out[1, rows, pl.ds(t * LANES, LANES)] = one * second_first + two * second_second
                return 0

            lax.fori_loop(0, MODES // 16, some_rows, 0)


def tables_kernel(edges, flags, table, square):
    blocks, _, capacity = edges.shape
    lanes = lane_ids(capacity)
    slots = lax.broadcasted_iota(jnp.int32, (capacity, LANES), 0)
    here = slots == lax.rem(lanes, capacity)
    flag = jnp.zeros((1, LANES), jnp.int32)
    count = jnp.zeros((1, LANES), jnp.int32)
    table[...] = jnp.zeros(table.shape, jnp.int32)
    square[...] = jnp.zeros(square.shape, jnp.float32)
    for o in range(blocks):
        square[o : o + 1, 0:capacity] = edges[o].astype(jnp.float32)
        square[blocks + o : blocks + o + 1, 0:capacity] = flags[o].astype(jnp.float32)
    columns = square[...].T[0:capacity].astype(jnp.int32)
    for o in range(blocks):
        column = jnp.broadcast_to(columns[:, o : o + 1], (capacity, LANES))
        held = column == lanes

        def summed(mask, value):
            return jnp.sum(jnp.where(mask, value, 0), axis=0, keepdims=True)

        table[o : o + 1, :] = summed(here, jnp.maximum(column, 0))
        table[5 + o : 6 + o, :] = summed(held, slots)
        present = summed(held, jnp.ones_like(slots))
        table[10 + o : 11 + o, :] = present
        flag += summed(held, jnp.broadcast_to(columns[:, blocks + o : blocks + o + 1], (capacity, LANES)))
        count += present
        if o == blocks // 2:
            partner = slots + 1 - 2 * lax.rem(slots, 2)
            slot_of = jnp.broadcast_to(summed(held, partner), (capacity, LANES))
            partner_edge = summed(slots == slot_of, jnp.maximum(column, 0))
            table[16:17, :] = jnp.where(present > 0, partner_edge, 0)
    table[15:16, :] = flag
    table[17:18, :] = count


def diffuse_kernel(state, metric, bands, local_sum, first, second):
    me = lax.axis_index("plane")
    rows_total = state.shape[1]
    lanes = lane_ids(8)
    local = rows_total // 3
    wide = metric_rows(metric)
    xi_x, xi_y, eta_x, eta_y = (wide[r : r + 1] for r in range(4))
    g_ii = xi_x * xi_x + xi_y * xi_y
    g_ij = xi_x * eta_x + xi_y * eta_y
    g_jj = eta_x * eta_x + eta_y * eta_y
    def eta_of(tiles):
        turned = turned_tiles(tiles, lanes)
        return [
            along_j(turned, SLAB_TILES, t, lambda d, t=t: tile_at(bands, (), pl.ds(d + 8, 1), t), used_offsets(t))
            for t in range(SLAB_TILES)
        ]

    def some_rows(g, _):
        rows = pl.ds(pl.multiple_of(g * 8, 8), 8)
        first_mode = me * local + lax.rem(g * 8, local)
        wave = ((first_mode + lax.broadcasted_iota(jnp.int32, (8, LANES), 0) + 1) // 2).astype(jnp.float32)
        wave_sq = wave * wave
        for t in range(SLAB_TILES):
            for a, value in enumerate(along_i([tile_at(state, (i,), rows, t) for i in range(NODES)])):
                first[a, :, pl.ds(t * LANES, LANES)] = value
        for i in range(NODES):
            eta = eta_of([tile_at(state, (i,), rows, t) for t in range(SLAB_TILES)])
            mixed = []
            for t in range(SLAB_TILES):
                xi = first[i, :, pl.ds(t * LANES, LANES)]
                first[i, :, pl.ds(t * LANES, LANES)] = g_ii * xi + g_ij * eta[t]
                mixed.append(g_ij * xi + g_jj * eta[t])
            for t, value in enumerate(eta_of(mixed)):
                second[i, :, pl.ds(t * LANES, LANES)] = value
        for t in range(SLAB_TILES):
            tiles = [first[i, :, pl.ds(t * LANES, LANES)] for i in range(NODES)]
            for a, value in enumerate(along_i(tiles)):
                now = tile_at(state, (a,), rows, t)
                laplacian = value + second[a, :, pl.ds(t * LANES, LANES)]
                local_sum[a, rows, pl.ds(t * LANES, LANES)] = now + STEP_VISC * (laplacian - wave_sq * now)
        return 0

    lax.fori_loop(0, rows_total // 8, some_rows, 0)


def halves(value):
    high = value.astype(jnp.bfloat16)
    return high, (value - high.astype(jnp.float32)).astype(jnp.bfloat16)


def fields_kernel(gaps, split, source, *refs):
    extra, bands = (refs[0], refs[1]) if split else (None, refs[0])
    fields = refs[-1]
    me = lax.axis_index("plane")
    rows_total = source.shape[0]
    local = fields.shape[2]
    lanes = lane_ids(GROUP)
    gap = sum(jnp.where(me == b, g, 0) for b, g in enumerate(gaps))
    gap_late, gap_shift = gap >= RING_TILES * LANES, lax.rem(LANES - lax.rem(gap, LANES), LANES)

    for g in range(rows_total // GROUP):
        rows = group_rows(g)
        c = g * GROUP // local
        target = pl.ds(g * GROUP % local, GROUP)
        tiles = [tile_at(source, (), rows, t) for t in range(RING_TILES)]
        tiles.append(extra[rows, :] if split else tile_at(source, (), rows, BASE_TILES))
        turned = turned_tiles(tiles, lanes)
        for t in range(CHUNK_TILES):
            at = pl.ds(t * LANES, LANES)
            fields[0, c, target, at] = tiles[t]
            fields[2, c, target, at] = along_j(
                turned, STATE_TILES, t, lambda d, at=at: bands[me, pl.ds(d + 8, 1), at], range(-8, 9)
            )
        for t in range(BODY_TILES):
            fields[1, c, target, pl.ds(t * LANES, LANES)] = tile_at(source, (), rows, RING_TILES + t)
        tail = jnp.where(gap_late, tiles[RING_TILES], tiles[RING_TILES - 1])
        fields[1, c, target, pl.ds(BODY_TILES * LANES, LANES)] = pltpu.roll(tail, gap_shift, 1)


def span_dot(a, value):
    high, low = halves(value)
    stacked = jnp.concatenate([high, low, high], axis=0)
    return jnp.dot(a, stacked, preferred_element_type=jnp.float32)


LANE_PARTS = [pl.ds(first, 2 * LANES) for first in range(0, CHUNK_TILES * LANES, 2 * LANES)]


def products(sources, flow, both, part):
    def field(kind, c):
        return jnp.concatenate([fields[kind, c, :, part] for fields in sources], axis=0)

    comps, basis = sources[0].shape[1], both[:MODES]
    values, sums = [], []
    for c in range(comps):
        out = span_dot(both, field(0, c))
        values.append(out[:MODES])
        along_x = flow[0, :, part] * span_dot(basis, field(1, c))
        along_y = flow[1, :, part] * span_dot(basis, field(2, c))
        sums.append(along_x + along_y + flow[2, :, part] * out[MODES:])
    for c in range(comps):
        taken = values[0] * flow[3 + c, :, part]
        taken += values[1] * flow[6 + c, :, part]
        taken += values[2] * flow[9 + c, :, part]
        yield c, sums[c] - taken


def early_kernel(fields0, fields1, fields2, flow, to_span, early):
    both = to_span[lax.axis_index("plane")]
    for part in LANE_PARTS:
        for c, product in products((fields0, fields1, fields2), flow, both, part):
            early[c, :, part] = product


def advect_kernel(fields3, early, flow, to_span, to_modes, *refs):
    *outs, stacked = refs
    me = lax.axis_index("plane")
    both, back = to_span[me], to_modes[me]
    lanes = lane_ids(GROUP)
    local = MODES // len(outs)
    for part in LANE_PARTS:
        for c, product in products((fields3,), flow, both, part):
            high, low = halves(product + early[c, :, part])
            stacked[c, :, part] = jnp.concatenate([high, low, high], axis=0)
    tails = [None] * len(outs)
    for c in range(stacked.shape[0]):
        for n, part in enumerate(LANE_PARTS):
            result = jnp.dot(back, stacked[c, :, part], preferred_element_type=jnp.float32)
            for k, out in enumerate(outs):
                for half in range(local // GROUP):
                    g = c * (local // GROUP) + half
                    piece = result[k * local + half * GROUP : k * local + (half + 1) * GROUP]
                    first = (BODY_TILES * g + 2 * n) * LANES
                    if n < len(LANE_PARTS) - 1:
                        out[:, pl.ds(first, 2 * LANES)] = piece
                        continue
                    out[:, pl.ds(first, LANES)] = piece[:, :LANES]
                    tail = turn(piece[:, LANES:], 8 * g)
                    tails[k] = tail if g == 0 else jnp.where(lanes >= 8 * g, tail, tails[k])
    for out, tail in zip(outs, tails):
        out[:, pl.ds((BACK_TILES - 1) * LANES, LANES)] = tail


def trace_blocks(me):
    odd, late = lax.rem(me, 2), lax.rem(me, 4) // 2
    return 1 + 2 * odd, 4 * late, 4 - 4 * late, 3 - 2 * odd


def trace_partner(me, matching, size):
    step, start = ((1, 1), (2, 2), (2, 0), (1, 0))[matching]
    return (((me + start) ^ step) - start) % size


def update_kernel(plans, in0, in1, in2, in3, local_sum, table, updated, traces, out0, out1, out2, out3, chunks):
    me = lax.axis_index("plane")
    rows_total = local_sum.shape[1]
    last = NODES - 1
    lanes = lane_ids(8)
    for step, source in zip(BACK_PARTNERS, (in0, in1, in2, in3)):
        chunks[me ^ step] = source[...]

    trace_plans = [
        tile_plan([(k, 0, 0, 32), (last, 32 * k, 32, 32), (k, 256, 64, 32), (0, 32 * k, 96, 32)], 1)[0]
        for k in range(NODES)
    ]

    blocks = trace_blocks(lax.axis_index("dom"))

    def wide(row):
        return jnp.broadcast_to(table[pl.ds(row, 1), :], (8, LANES))

    turned_round = wide(15) == 1
    slot_edges = [wide(o) for o in blocks]
    groups = range(rows_total // GROUP)
    for g in groups:
        rows = group_rows(g)

        def load(source, tile, g=g):
            if source[0] == "tail":
                return turn(tile_at(chunks, (source[1],), slice(None), BACK_TILES - 1), -8 * g)
            return tile_at(chunks, (source[1],), slice(None), BODY_TILES * g + tile)

        turned = turner(load)
        for i in range(NODES):
            for t in range(SLAB_TILES):
                value = pieced(plans[i][t], turned, lanes)
                updated[i, rows, pl.ds(t * LANES, LANES)] = (
                    tile_at(local_sum, (i,), rows, t) + step_size * value
                )
    for g in groups:
        rows = group_rows(g)
        edges = turner(lambda i, tile, rows=rows: tile_at(updated, (i,), rows, tile))
        raw = [pieced(plan, edges, lanes) for plan in trace_plans]
        for k in range(NODES):
            traces[k, rows, :] = jnp.where(turned_round, raw[last - k], raw[k])
    for g in groups:
        rows = group_rows(g)
        for slot_edge, out in zip(slot_edges, (out0, out1, out2, out3)):
            for t in range(2):
                total = None
                for k in range(5 * t, min(5 * t + 5, NODES)):
                    value = pick(traces[k, rows, :], slot_edge)
                    total = value if total is None else jnp.where(lanes >= 24 * (k - 5 * t), value, total)
                out[rows, pl.ds(t * LANES, LANES)] = total


def own_kernel(table, traces, own):
    partner = jnp.broadcast_to(table[16:17, :], (GROUP, LANES))
    present = jnp.broadcast_to(table[12:13, :], (GROUP, LANES)) > 0
    for g in range(traces.shape[1] // GROUP):
        rows = group_rows(g)
        for k in range(NODES):
            own[k, rows, :] = jnp.where(present, pick(traces[k, rows, :], partner), 0.0)


def pick(value, index):
    return jnp.take_along_axis(value, index, axis=1, mode="promise_in_bounds")


def join_edges(table, updated, own, came, sums, put):
    rows_total = updated.shape[1]
    last = NODES - 1
    lanes = lane_ids(8)
    blocks = trace_blocks(lax.axis_index("dom"))

    def wide(row):
        return jnp.broadcast_to(table[pl.ds(row, 1), :], (8, LANES))

    share = wide(17).astype(jnp.float32)
    quarter = lanes // 32
    has = [wide(10 + o) > 0 for o in blocks]
    slots = [wide(5 + o) for o in blocks]

    def spread(values, at, t):
        value = None
        for k in range(4 * t, min(4 * t + 4, NODES)):
            moved = turn(values[k], 32 * (k - 4 * t - at))
            value = jnp.where(quarter == k - 4 * t, moved, 0.0 if value is None else value)
        return value

    def edge_parts(values, i, t):
        parts = []
        if t == 0:
            parts.append(jnp.where(quarter == 0, values[i], 0.0))
        if i == last:
            parts.append(spread(values, 1, t))
        if t == 2:
            parts.append(jnp.where(quarter == 0, turn(values[i], -64), 0.0))
        if i == 0:
            parts.append(spread(values, 3, t))
        return parts

    shares, scale = [share] * NODES, {}
    for i in (0, 1, last):
        for t in range(SLAB_TILES):
            parts = edge_parts(shares, i, t)
            if parts:
                scale[i, t] = 1.0 / (1.0 + sum(parts[1:], parts[0]))

    groups = range(rows_total // GROUP)
    for g in groups:
        rows = group_rows(g)
        for k in range(NODES):
            total = own[k, rows, :]
            for slot, there, source in zip(slots, has, came):
                value = pick(tile_at(source, (), rows, k // 5), slot + 24 * (k % 5))
                total = jnp.where(there, value, total)
            sums[k, rows, :] = total
    for g in groups:
        rows = group_rows(g)
        values = [sums[k, rows, :] for k in range(NODES)]
        for i in range(NODES):
            for t in range(SLAB_TILES):
                parts = edge_parts(values, i, t)
                if parts:
                    total = tile_at(updated, (i,), rows, t)
                    for part in parts:
                        total += part
                    put(g, i, t, total * scale[i if i in (0, last) else 1, t])


def next_kernel(plans, table, updated, own, r0, r1, r2, r3, bands, state, xi, out, sums):
    def put(g, i, t, value):
        state[i, group_rows(g), pl.ds(t * LANES, LANES)] = value

    for i in range(1, NODES - 1):
        state[i, :, pl.ds(LANES, LANES)] = updated[i, :, pl.ds(LANES, LANES)]
    join_edges(table, updated, own, (r0, r1, r2, r3), sums, put)
    make_xi(range(updated.shape[1] // GROUP), state, xi)
    make_first(plans, state, xi, bands, out)


def last_kernel(table, updated, own, r0, r1, r2, r3, out, state, sums, given, sems):
    comps, local, elements = given.shape[0], given.shape[3], given.shape[4]

    def put(g, i, t, value):
        state[i, group_rows(g), pl.ds(t * LANES, LANES)] = value

    join_edges(table, updated, own, (r0, r1, r2, r3), sums, put)
    copies = []
    for i in range(NODES):
        for c in range(comps):
            rows = pl.ds(c * local, local)
            for t in range(SLAB_TILES):
                joined = t != 1 or i in (0, NODES - 1)
                tile = tile_at(state if joined else updated, (i,), rows, t)
                for q in range(min(4, NODES - 4 * t)):
                    given[c, i, 4 * t + q] = turn(tile, -32 * q)[:, :elements]
        copies.append(pltpu.make_async_copy(given.at[:, i], out.at[:, i], sems.at[i]))
        copies[-1].start()
    for copy in copies:
        copy.wait()


def f32(*shape):
    return jax.ShapeDtypeStruct(shape, jnp.float32)


def kernel_call(body, outs, scratch, flops, moved, **more):
    return pl.pallas_call(
        body,
        out_shape=outs,
        scratch_shapes=scratch,
        compiler_params=pltpu.CompilerParams(vmem_limit_bytes=16 * 1024 * 1024),
        cost_estimate=pl.CostEstimate(flops=flops, bytes_accessed=moved, transcendentals=0),
        **more,
    )


def swapped(buffers, steps):
    return [buffers[0]] + [swap(buffer, step) for buffer, step in zip(buffers[1:], steps[1:])]


def swap(buffer, step, wanted=range(4)):
    return lax.ppermute(buffer, "plane", sorted((i ^ step, i) for i in wanted))


def packed_shards(adjoint, metric, base_flow, edge_list, flips):
    comps, local, nodes, _, elements = adjoint.shape
    planes = MODES // local
    points = nodes * nodes * elements // planes
    rows_total = comps * local
    partitions = lax.axis_size("dom")
    state_shape = (nodes, rows_total, SLAB_TILES * LANES)

    layouts = [send_segments(chunk, points) for chunk in range(planes)]
    plans = [tile_plan(segments, SEND_TILES) for segments, _ in layouts]
    gaps = [gap for _, gap in layouts]
    back_plans = return_segments(points)
    to_span, to_span_last, to_modes = span_weights(planes)
    slab_bands = eta_bands(0, SLAB_TILES * LANES, nodes * elements)
    middle = [chunk for chunk, plan in enumerate(plans) if plan[-1]]
    chunk_bands = np.stack([chunk_eta_bands(b, points) for b in range(planes)])

    in_hbm, vmem = (pl.BlockSpec(memory_space=space) for space in (pltpu.HBM, pltpu.VMEM))
    buffer, base, extra = (f32(rows_total, tiles * LANES) for tiles in (SEND_TILES, BASE_TILES, 1))
    row_copies = [
        pltpu.VMEM((comps, nodes, nodes, local, elements), jnp.float32),
        pltpu.SemaphoreType.DMA((nodes,)),
    ]
    edge_scratch = pltpu.VMEM((nodes, rows_total, LANES), jnp.float32)

    def forward(state, xi, first):
        own, second, third, last_tile = kernel_call(
            functools.partial(rest_kernel, plans),
            [buffer, buffer, base, extra],
            [pltpu.VMEM((planes, *buffer.shape), jnp.float32)],
            10**6,
            2 * 10**6,
        )(state, xi, slab_bands)
        came = swapped([own, first, second, third], PARTNERS)
        return [(part,) for part in came[:-1]] + [(came[-1], swap(last_tile, PARTNERS[-1], middle))]

    in_rows = pltpu.with_memory_space_constraint(adjoint.transpose(0, 2, 3, 1, 4), pltpu.HBM)
    state, *prepared = kernel_call(
        functools.partial(first_kernel, plans),
        [f32(*state_shape), f32(*state_shape), buffer],
        row_copies + [pltpu.VMEM(slab_bands.shape, jnp.float32)],
        4 * 10**6,
        4 * 10**6,
        in_specs=[in_hbm, in_hbm],
    )(in_rows, pltpu.with_memory_space_constraint(jnp.asarray(slab_bands), pltpu.HBM))
    incoming = forward(state, *prepared)
    whole, two_fields = (12, MODES, CHUNK_TILES * LANES), (2, MODES, CHUNK_TILES * LANES)
    lay = base_flow.transpose(1, 0, 2)
    flows = kernel_call(
        functools.partial(flow_kernel, points),
        [f32(*whole)] * STEPS,
        [pltpu.VMEM((2, STEPS, lay.shape[2] // LANES, LANES), jnp.float32)],
        4 * 10**6,
        9 * 10**6,
        grid=(6,),
        in_specs=[
            pl.BlockSpec((2, *lay.shape[1:]), lambda pair: (pair, 0, 0)),
            pl.BlockSpec(metric.shape, lambda pair: (0, 0)),
        ],
        out_specs=[pl.BlockSpec(two_fields, lambda pair: (pair, 0, 0))] * STEPS,
    )(lay, metric)
    table = kernel_call(
        tables_kernel,
        jax.ShapeDtypeStruct((24, LANES), jnp.int32),
        [pltpu.VMEM((LANES, LANES), jnp.float32)],
        10**5,
        10**5,
    )(edge_list.transpose(1, 0, 2), flips.transpose(1, 0, 2))

    for step_index in range(STEPS):
        fields = [None] * planes
        before = []
        for k in FIELDS_ORDER:
            parts = incoming[k]
            fields[k] = kernel_call(
                functools.partial(fields_kernel, gaps, len(parts) > 1),
                f32(3, comps, local, CHUNK_TILES * LANES),
                [],
                2 * 10**6,
                10**6,
                in_specs=[vmem] * (len(parts) + 1) + [pl.BlockSpec(memory_space=pl.ANY)] * len(before),
            )(*parts, chunk_bands, *before)
            before = [fields[k]] if k > 0 else []
        early = kernel_call(
            early_kernel, f32(comps, MODES, CHUNK_TILES * LANES), [], 50 * 10**6, 5 * 10**6
        )(*fields[:-1], flows[step_index], to_span)
        returning = kernel_call(
            advect_kernel,
            [f32(GROUP, BACK_TILES * LANES)] * planes,
            [pltpu.VMEM((comps, 3 * MODES, CHUNK_TILES * LANES), jnp.bfloat16)],
            30 * 10**6,
            5 * 10**6,
        )(fields[-1], early, flows[step_index], to_span_last, to_modes)
        local_sum = kernel_call(
            diffuse_kernel,
            f32(*state_shape),
            [pltpu.VMEM((nodes, GROUP, SLAB_TILES * LANES), jnp.float32)] * 2,
            12 * 10**6,
            2 * 10**6,
        )(state, metric, slab_bands)
        updated, seen, *leaving = kernel_call(
            functools.partial(update_kernel, back_plans),
            [f32(*state_shape), f32(nodes, rows_total, LANES)] + [f32(rows_total, 2 * LANES)] * 4,
            [pltpu.VMEM((planes, GROUP, BACK_TILES * LANES), jnp.float32)],
            2 * 10**6,
            3 * 10**6,
        )(*swapped(returning, BACK_PARTNERS), local_sum, table)
        traces = [
            lax.ppermute(
                buffer, "dom", [(i, trace_partner(i, matching, partitions)) for i in range(partitions)]
            )
            for matching, buffer in enumerate(leaving)
        ]
        own = kernel_call(own_kernel, f32(nodes, rows_total, LANES), [], 10**5, 10**6)(table, seen)
        if step_index + 1 < STEPS:
            state, *prepared = kernel_call(
                functools.partial(next_kernel, plans),
                [f32(*state_shape), f32(*state_shape), buffer],
                [edge_scratch],
                6 * 10**6,
                4 * 10**6,
            )(table, updated, own, *traces, slab_bands)
            incoming = forward(state, *prepared)
        else:
            result = kernel_call(
                last_kernel,
                f32(comps, nodes, nodes, local, elements),
                [pltpu.VMEM(state_shape, jnp.float32), edge_scratch, *row_copies],
                2 * 10**6,
                3 * 10**6,
                out_specs=in_hbm,
            )(table, updated, own, *traces)
    return result.transpose(0, 3, 1, 2, 4)


def plain_shards(adjoint, metric, base_flow, edge_list, flips):
    local_modes = adjoint.shape[1]
    deriv_table = cheb_table(adjoint.shape[2])
    span_basis, span_slope, forward, wave_sq = span_tables(MODES)
    wave_local = lax.dynamic_slice_in_dim(
        wave_sq, lax.axis_index("plane") * local_modes, local_modes, 0
    )
    adjoint_state = adjoint
    for step_index in range(STEPS):
        base_now = base_flow[step_index].reshape(12, MODES, -1)
        adjoint_state = advance(
            adjoint_state,
            metric,
            base_now,
            edge_list[0],
            flips[0],
            deriv_table,
            span_basis,
            span_slope,
            forward,
            wave_local,
        )
    return adjoint_state


def shards(adjoint, metric, base_flow, edge_list, flips):
    if adjoint.shape[1:] == (MODES // 4, NODES, NODES, 32) and (
        edge_list.shape[1:] == (5, 24) and lax.axis_size("dom") % 4 == 0
    ):
        return packed_shards(adjoint, metric, base_flow, edge_list, flips)
    return plain_shards(adjoint, metric, base_flow, edge_list, flips)


def solution(mesh):
    placed = (
        P(None, "plane", None, None, "dom"),
        P(None, "dom"),
        P(None, None, ("dom", "plane")),
        P("dom", None, None),
        P("dom", None, None),
    )
    return jax.shard_map(
        shards,
        mesh=mesh,
        in_specs=placed,
        out_specs=P(None, "plane", None, None, "dom"),
        check_vma=False,
    )
```
